32 devices in a mesh: groups: 2 (over x), lon: 16 (over z, y, core).
Axes of the slice: x: 2, y: 2, z: 4, core: 2. Of those that a mesh axis runs over, the one named last changes fastest.
Arguments:
- fields: bfloat16 [32, 32, 1500], P(('groups', 'lon')), parts along dimension 0, may hold values from -6 to 6
- level_ids: int32 [6], P('groups'), parts along dimension 0, may hold values from 0 to 2, each once
- embed_weight: bfloat16 [500, 512], replicated, may hold values from -0.25 to 0.25
- level_embed: bfloat16 [3, 512], replicated, may hold values from -6 to 6
- enc_gain: float32 [512], replicated, may hold values from 0.1 to 1.9
- latent_query: bfloat16 [2, 512], replicated, may hold values from -0.049804688 to 0.049804688
- kv_weight: bfloat16 [512, 1024], replicated, may hold values from -0.25 to 0.25
- pool_out: bfloat16 [512, 512], replicated, may hold values from -0.25 to 0.25
- attn_gain: float32 [512], replicated, may hold values from 0.1 to 1.9
- qkv_weight: bfloat16 [512, 1536], replicated, may hold values from -0.25 to 0.25
- attn_proj: bfloat16 [512, 512], replicated, may hold values from -0.25 to 0.25
- mlp_gain: float32 [512], replicated, may hold values from 0.1 to 1.9
- mlp_up: bfloat16 [512, 2048], replicated, may hold values from -0.25 to 0.25
- mlp_down: bfloat16 [2048, 512], replicated, may hold values from -0.125 to 0.125
- level_mix: float32 [3, 2], replicated, may hold values from 0.25 to 4
- dec_gain: float32 [512], replicated, may hold values from 0.1 to 1.9
- dec_weight: bfloat16 [512, 500], replicated, may hold values from -0.25 to 0.25
Outputs:
- forecast: bfloat16 [32, 32, 1500], P(('groups', 'lon')), parts along dimension 0
The draws below stay inside these ranges and needn't reach their ends.
There are 2 independent parts, one for each index of `groups`. The reference program is written for one: setup_inputs(seed, part) draws one part's arguments, and reference() takes and returns one part's arrays. A program takes and returns all parts, laid end to end along the dimension named above; an argument that names none is the same for every part. Nothing has to cross between parts.
Inputs may be any that keep to these rules, and one draw needn't show every extreme that they name: level_ids holds each of 0 to 2 once.
All inputs are finite; a program needn't handle non-finite values.
Results may differ from the reference program's by a relative error of at most 0.014.
Values may be sent and summed in bfloat16 or wider, within the bound.
No kernel may reach another device: no remote copies, remote signals or barrier semaphores. Data moves between devices by JAX's collectives and lax.ppermute only.
A program may use at most 128 MiB of HBM per device.

```python
import math
import jax
import jax.numpy as jnp
from jax import lax

D = 512
HEADS = 8
MLP = 2048
PIN = 500
LEV = 3
LATL = 2
W_LAT = 4
W_LON = 8
STEPS = 2
LON_DEV = 8
ROW_PARTS = 4
LAT_P = 4
LON_P = 128
N_LON = 16


def draw_fields(key, part):
    row_count = LAT_P * ROW_PARTS
    col_count = LON_P // ROW_PARTS
    scale_key = jax.random.fold_in(key, 11)
    value_key = jax.random.fold_in(key, 23)
    log_scales = jax.random.uniform(scale_key, (row_count, col_count, LEV, 1), jnp.float32, -1.5, 1.5)
    scales = jnp.exp(log_scales)
    base = jax.random.normal(value_key, (row_count, col_count, LEV, PIN), jnp.float32)
    values = jnp.clip(scales * base, -6.0, 6.0)
    return values.reshape(row_count, col_count, LEV * PIN).astype(jnp.bfloat16)


def normal_values(key, extent, scale, limit, kind=jnp.bfloat16):
    return jnp.clip(scale * jax.random.normal(key, extent, jnp.float32), -limit, limit).astype(kind)


def setup_inputs(seed: int = 0, part: int = 0) -> dict:
    arg_keys = jax.random.split(jax.random.key(seed), 18)
    own_keys = jax.random.split(jax.random.fold_in(arg_keys[17], part), 18)
    return {
        "fields": draw_fields(jax.random.fold_in(jax.random.fold_in(arg_keys[17], part), 71), part),
        "level_ids": jax.random.permutation(own_keys[1], LEV).astype(jnp.int32),
        "embed_weight": normal_values(arg_keys[2], (PIN, D), PIN ** -0.5, 0.25),
        "level_embed": normal_values(arg_keys[3], (LEV, D), 1.0, 6.0),
        "enc_gain": jnp.clip(1.0 + 0.18 * jax.random.normal(arg_keys[4], (D,), jnp.float32), 0.1, 1.9),
        "latent_query": jnp.clip(jax.random.uniform(arg_keys[5], (LATL, D), jnp.float32, -0.049804688, 0.049804688), -0.049804688, 0.049804688).astype(jnp.bfloat16),
        "kv_weight": normal_values(arg_keys[6], (D, 2 * D), D ** -0.5, 0.25),
        "pool_out": normal_values(arg_keys[7], (D, D), D ** -0.5, 0.25),
        "attn_gain": jnp.clip(1.0 + 0.18 * jax.random.normal(arg_keys[8], (D,), jnp.float32), 0.1, 1.9),
        "qkv_weight": normal_values(arg_keys[9], (D, 3 * D), D ** -0.5, 0.25),
        "attn_proj": normal_values(arg_keys[10], (D, D), D ** -0.5, 0.25),
        "mlp_gain": jnp.clip(1.0 + 0.18 * jax.random.normal(arg_keys[11], (D,), jnp.float32), 0.1, 1.9),
        "mlp_up": normal_values(arg_keys[12], (D, MLP), D ** -0.5, 0.25),
        "mlp_down": normal_values(arg_keys[13], (MLP, D), MLP ** -0.5, 0.125),
        "level_mix": jnp.clip(jnp.exp(jax.random.uniform(arg_keys[14], (LEV, LATL), jnp.float32, math.log(0.25), math.log(4.0))), 0.25, 4.0),
        "dec_gain": jnp.clip(1.0 + 0.18 * jax.random.normal(arg_keys[15], (D,), jnp.float32), 0.1, 1.9),
        "dec_weight": normal_values(arg_keys[16], (D, PIN), D ** -0.5, 0.25),
    }


norm_eps = 1e-05
head_eps = 1e-06

def product(einsum_form, left_side, right_side):
    return jnp.einsum(einsum_form, left_side.astype(jnp.float32), right_side.astype(jnp.float32))

def layer_norm(values, scale_row):
    average = lax.optimization_barrier(jnp.mean(values, axis=-1, keepdims=True))
    centred = values - average
    spread = lax.optimization_barrier(jnp.mean(centred * centred, axis=-1, keepdims=True))
    return centred * lax.rsqrt(spread + norm_eps) * scale_row

def unit_heads(values):
    shaped = values.reshape(values.shape[:-1] + (HEADS, D // HEADS))
    mean_square = lax.optimization_barrier(jnp.mean(shaped * shaped, axis=-1, keepdims=True))
    return (shaped * lax.rsqrt(mean_square + head_eps)).reshape(values.shape)

def level_tables(level_ids, level_embed, level_mix):
    picker = (level_ids[:, None] == jnp.arange(LEV, dtype=jnp.int32)[None, :]).astype(jnp.float32)
    embeds = jnp.dot(picker, level_embed.astype(jnp.float32), precision=lax.Precision.HIGHEST)
    mixing = jnp.dot(picker, level_mix, precision=lax.Precision.HIGHEST)
    return (embeds, mixing)

def encode(flat_fields, embeds, queries, embed_weight, enc_gain, kv_weight, pool_out, latent_query):
    head_dim = D // HEADS
    patch_count = flat_fields.shape[0]
    patches = flat_fields.reshape(patch_count * LEV, PIN)
    tokens = jnp.dot(patches, embed_weight, preferred_element_type=jnp.float32).reshape(patch_count, LEV, D)
    tokens = layer_norm(tokens + embeds[None], enc_gain).astype(jnp.bfloat16)
    keyval = jnp.dot(tokens.reshape(patch_count * LEV, D), kv_weight, preferred_element_type=jnp.float32)
    key_heads = unit_heads(keyval[:, :D]).astype(jnp.bfloat16).reshape(patch_count, LEV, HEADS, head_dim)
    value_heads = keyval[:, D:].astype(jnp.bfloat16).reshape(patch_count, LEV, HEADS, head_dim)
    scores = product('jhc,rlhc->rjhl', queries.reshape(LATL, HEADS, head_dim), key_heads) * head_dim ** (-0.5)
    weights = jnp.exp(scores)
    weights = (weights / lax.optimization_barrier(jnp.sum(weights, axis=-1, keepdims=True))).astype(jnp.bfloat16)
    pooled = product('rjhl,rlhc->rjhc', weights, value_heads).astype(jnp.bfloat16).reshape(patch_count * LATL, D)
    latents = jnp.dot(pooled, pool_out, preferred_element_type=jnp.float32).reshape(patch_count, LATL, D)
    return (latents + latent_query.astype(jnp.float32)[None]).astype(jnp.bfloat16)

def increments(backbone_out, embeds, mixing, dec_gain, dec_weight):
    patch_count = backbone_out.shape[0]
    blended = mixing[None, :, 0, None] * backbone_out[:, None, 0, :].astype(jnp.float32)
    for latent_index in range(1, LATL):
        blended = blended + mixing[None, :, latent_index, None] * backbone_out[:, None, latent_index, :].astype(jnp.float32)
    blended = blended + embeds[None]
    normed = layer_norm(blended, dec_gain).astype(jnp.bfloat16)
    result = jnp.dot(normed.reshape(patch_count * LEV, D), dec_weight, preferred_element_type=jnp.float32)
    return result.astype(jnp.bfloat16).reshape(patch_count, LEV * PIN)

def window_block(shifted, attn_gain, qkv_weight, attn_proj):
    head_dim = D // HEADS
    lat_count, lon_count = (shifted.shape[0], shifted.shape[1])
    lat_win, lon_win = (lat_count // W_LAT, lon_count // W_LON)
    inside = W_LAT * W_LON * LATL
    flat_tokens = shifted.reshape(-1, D)
    normed = layer_norm(flat_tokens.astype(jnp.float32), attn_gain).astype(jnp.bfloat16)
    projected = jnp.dot(normed, qkv_weight, preferred_element_type=jnp.float32)
    query_heads = unit_heads(projected[:, :D]).astype(jnp.bfloat16)
    key_heads = unit_heads(projected[:, D:2 * D]).astype(jnp.bfloat16)
    value_heads = projected[:, 2 * D:].astype(jnp.bfloat16)

    def to_windows(head_data):
        shaped = head_data.reshape(lat_win, W_LAT, lon_win, W_LON, LATL, HEADS, head_dim)
        return shaped.transpose(0, 2, 5, 1, 3, 4, 6).reshape(lat_win, lon_win, HEADS, inside, head_dim)
    scores = product('abhqc,abhkc->abhqk', to_windows(query_heads), to_windows(key_heads)) * head_dim ** (-0.5)
    row_index = jnp.arange(lat_count, dtype=jnp.int32).reshape(lat_win, W_LAT)
    region = (row_index >= lat_count - W_LAT // 2).astype(jnp.int32)
    region_tok = jnp.broadcast_to(region[:, :, None, None], (lat_win, W_LAT, W_LON, LATL)).reshape(lat_win, inside)
    allowed = (region_tok[:, :, None] == region_tok[:, None, :]).astype(jnp.float32)
    weights = jnp.exp(scores) * allowed[:, None, None, :, :]
    weights = (weights / lax.optimization_barrier(jnp.sum(weights, axis=-1, keepdims=True))).astype(jnp.bfloat16)
    win_mix = product('abhqk,abhkc->abhqc', weights, to_windows(value_heads)).astype(jnp.bfloat16)
    win_mix = win_mix.reshape(lat_win, lon_win, HEADS, W_LAT, W_LON, LATL, head_dim)
    win_mix = win_mix.transpose(0, 3, 1, 4, 5, 2, 6).reshape(-1, D)
    attended = flat_tokens.astype(jnp.float32) + jnp.dot(win_mix, attn_proj, preferred_element_type=jnp.float32)
    return attended.astype(jnp.bfloat16).reshape(shifted.shape)

def mlp_block(restored, mlp_gain, mlp_up, mlp_down):
    flat_tokens = restored.reshape(-1, D)
    normed = layer_norm(flat_tokens.astype(jnp.float32), mlp_gain).astype(jnp.bfloat16)
    hidden = jax.nn.gelu(jnp.dot(normed, mlp_up, preferred_element_type=jnp.float32)).astype(jnp.bfloat16)
    result = flat_tokens.astype(jnp.float32) + jnp.dot(hidden, mlp_down, preferred_element_type=jnp.float32)
    return result.astype(jnp.bfloat16).reshape(restored.shape)

def unfold_grid(folded):
    piece_cols = LON_DEV // ROW_PARTS
    shaped = folded.reshape(ROW_PARTS, LAT_P, N_LON, piece_cols, folded.shape[-1])
    return shaped.transpose(1, 2, 0, 3, 4).reshape(LAT_P, LON_P, folded.shape[-1])

def fold_grid(grid):
    piece_cols = LON_DEV // ROW_PARTS
    shaped = grid.reshape(LAT_P, N_LON, ROW_PARTS, piece_cols, grid.shape[-1])
    return shaped.transpose(2, 0, 1, 3, 4).reshape(LAT_P * ROW_PARTS, LON_P // ROW_PARTS, grid.shape[-1])

def reference(fields, level_ids, embed_weight, level_embed, enc_gain, latent_query, kv_weight, pool_out, attn_gain, qkv_weight, attn_proj, mlp_gain, mlp_up, mlp_down, level_mix, dec_gain, dec_weight):
    embeds, mixing = level_tables(level_ids, level_embed, level_mix)
    queries = unit_heads(latent_query.astype(jnp.float32)).astype(jnp.bfloat16)

    def encode_row(lat_row):
        return encode(lat_row, embeds, queries, embed_weight, enc_gain, kv_weight, pool_out, latent_query)

    def column_step(column_block):
        attended = window_block(column_block, attn_gain, qkv_weight, attn_proj)
        return mlp_block(attended, mlp_gain, mlp_up, mlp_down)

    def decode_row(lat_row):
        return increments(lat_row, embeds, mixing, dec_gain, dec_weight)
    current = unfold_grid(fields)
    for turn_index in range(STEPS):
        latents = lax.map(encode_row, current)
        shifted = jnp.roll(latents, (-(W_LAT // 2), -(W_LON // 2)), axis=(0, 1))
        columns = shifted.reshape(LAT_P, LON_P // W_LON, W_LON, LATL, D).transpose(1, 0, 2, 3, 4)
        backbone_out = lax.map(column_step, columns).transpose(1, 0, 2, 3, 4).reshape(LAT_P, LON_P, LATL, D)
        backbone_out = jnp.roll(backbone_out, (W_LAT // 2, W_LON // 2), axis=(0, 1))
        added = lax.map(decode_row, backbone_out)
        current = (current.astype(jnp.float32) + added.astype(jnp.float32)).astype(jnp.bfloat16)
    return fold_grid(current)
```

```python
import functools

import jax
import jax.numpy as jnp
from jax import lax
from jax.experimental import pallas as pl
from jax.experimental.pallas import tpu as pltpu
from jax.sharding import PartitionSpec as P

D = 512
HEADS = 8
HEAD_DIM = D // HEADS
PIN = 500
LEV = 3
LATL = 2
W_LAT = 4
W_LON = 8
STEPS = 2
ROW_PARTS = 4
MLP = 2048
PATCHES = W_LAT * W_LON
TOKENS = PATCHES * LATL
HALF = D // 2
PAIR = 2 * HEAD_DIM

norm_eps = 1e-05
head_eps = 1e-06

F32 = jnp.float32
BF16 = jnp.bfloat16


def mm(a, b):
    return jnp.dot(a, b, preferred_element_type=F32)


def mm_t(a, b):
    return lax.dot_general(a, b, (((1,), (1,)), ((), ())), preferred_element_type=F32)


def layer_norm(values, gain):
    average = jnp.mean(values, axis=-1, keepdims=True)
    centred = values - average
    spread = jnp.mean(centred * centred, axis=-1, keepdims=True)
    return centred * lax.rsqrt(spread + norm_eps) * gain


def iota(shape, dim):
    return lax.broadcasted_iota(jnp.int32, shape, dim)


def picked(index, rows):
    result = rows[LEV - 1]
    for i in reversed(range(LEV - 1)):
        result = jnp.where(index == i, rows[i], result)
    return result


def forecast_kernel(
    windows,
    ids_ref,
    mix_ref,
    x_ref,
    level_embed_ref,
    enc_gain_ref,
    latent_query_ref,
    attn_gain_ref,
    mlp_gain_ref,
    dec_gain_ref,
    embed_ref,
    kv_ref,
    pool_ref,
    qkv_ref,
    proj_ref,
    up_ref,
    down_ref,
    dec_ref,
    out_ref,
    state,
    wide,
):
    table = level_embed_ref[...].astype(F32)
    rows = [table[i : i + 1] for i in range(LEV)]
    embeds = [picked(ids_ref[l], rows) for l in range(LEV)]
    mixing = [[mix_ref[ids_ref[l], j] for j in range(LATL)] for l in range(LEV)]
    latent = latent_query_ref[...].astype(F32)

    row16 = iota((LATL * HEADS, D), 0)
    lane_head = iota((LATL * HEADS, D), 1) // HEAD_DIM
    on_head = (row16 % HEADS) == lane_head
    square = (latent * latent)
    query_rows = []
    for j in range(LATL):
        masked = jnp.where(on_head[:HEADS], square[j : j + 1], 0.0)
        scale = lax.rsqrt(jnp.sum(masked, axis=-1, keepdims=True) / HEAD_DIM + head_eps)
        query_rows.append(jnp.where(on_head[:HEADS], latent[j : j + 1] * scale, 0.0))
    query_table = jnp.concatenate(query_rows, axis=0).astype(BF16)
    mean_table = jnp.where(on_head, 1.0 / HEAD_DIM, 0.0).astype(BF16)
    spread_row = iota((LATL * HEADS, LATL * D), 0)
    spread_lane = iota((LATL * HEADS, LATL * D), 1)
    spreader = jnp.where(spread_row == spread_lane // HEAD_DIM, 1.0, 0.0).astype(BF16)
    block_ones = jnp.where(
        iota((HALF, HALF), 0) // HEAD_DIM == iota((HALF, HALF), 1) // HEAD_DIM, 1.0 / HEAD_DIM, 0.0
    ).astype(BF16)
    low = iota((1, PAIR), 1) < HEAD_DIM
    half_ones = jnp.where(
        (iota((PAIR, PAIR), 0) < HEAD_DIM) == (iota((PAIR, PAIR), 1) < HEAD_DIM), 1.0, 0.0
    ).astype(BF16)
    row_bit = (iota((TOKENS, PAIR), 0) // 4) % 2
    lane_bit = (iota((TOKENS, PAIR), 1) // 4) % 2
    cut = jnp.where(pl.program_id(0) == windows - 1, 1, 0)
    allowed = jnp.where((row_bit - lane_bit) * cut == 0, 1.0, 0.0)

    arrived = x_ref[0].astype(F32).reshape(PATCHES, LEV * PIN)
    for l in range(LEV):
        state[l * PATCHES : (l + 1) * PATCHES, :] = arrived[:, l * PIN : (l + 1) * PIN]

    def step(_, carry):
        patches = state[...].astype(BF16)
        tokens = mm(patches, embed_ref[...])
        tokens = jnp.concatenate(
            [tokens[l * PATCHES : (l + 1) * PATCHES] + embeds[l] for l in range(LEV)], axis=0
        )
        tokens = layer_norm(tokens, enc_gain_ref[...]).astype(BF16)
        keyval = mm(tokens, kv_ref[...])
        keys = keyval[:, :D]
        values = keyval[:, D:].astype(BF16).astype(F32)
        mean_square = mm_t((keys * keys).astype(BF16), mean_table)
        scores = mm_t(keys.astype(BF16), query_table)
        scores = scores * lax.rsqrt(mean_square + head_eps) * HEAD_DIM ** (-0.5)
        weights = jnp.exp(scores)
        parts = [weights[l * PATCHES : (l + 1) * PATCHES] for l in range(LEV)]
        inverse = 1.0 / (parts[0] + parts[1] + parts[2])
        weights = jnp.concatenate([part * inverse for part in parts], axis=0).astype(BF16)
        wide_weights = mm(weights, spreader)
        pooled = []
        for j in range(LATL):
            total = None
            for l in range(LEV):
                term = (
                    wide_weights[l * PATCHES : (l + 1) * PATCHES, j * D : (j + 1) * D]
                    * values[l * PATCHES : (l + 1) * PATCHES]
                )
                total = term if total is None else total + term
            pooled.append(total)
        pooled = jnp.concatenate(pooled, axis=0).astype(BF16)
        latents = mm(pooled, pool_ref[...])
        latents = jnp.concatenate(
            [latents[j * PATCHES : (j + 1) * PATCHES] + latent[j : j + 1] for j in range(LATL)],
            axis=0,
        )
        normed = layer_norm(latents, attn_gain_ref[...]).astype(BF16)
        projected = mm(normed, qkv_ref[...])
        halves = jnp.concatenate(
            [projected[:, i * HALF : (i + 1) * HALF] for i in range(4)], axis=0
        )
        mean_square = mm((halves * halves).astype(BF16), block_ones)
        halves = halves * lax.rsqrt(mean_square + head_eps)
        win_values = projected[:, 2 * D :]
        mixed = []
        for pair in range(HEADS // 2):
            half, at = pair // 2, (pair % 2) * PAIR
            query = halves[half * TOKENS : (half + 1) * TOKENS, at : at + PAIR].astype(BF16)
            key = halves[(2 + half) * TOKENS : (3 + half) * TOKENS, at : at + PAIR]
            value = win_values[:, pair * PAIR : (pair + 1) * PAIR]
            key = jnp.concatenate(
                [jnp.where(low, key, 0.0), jnp.where(low, 0.0, key)], axis=0
            ).astype(BF16)
            value = jnp.concatenate(
                [jnp.where(low, value, 0.0), jnp.where(low, 0.0, value)], axis=0
            ).astype(BF16)
            weights = jnp.exp(mm_t(query, key) * HEAD_DIM ** (-0.5)) * allowed
            weights = weights.astype(BF16)
            both = mm(weights, jnp.concatenate([value, half_ones], axis=1))
            mixed.append((both[:, :PAIR] / both[:, PAIR:]).astype(BF16))
        attended = latents + mm(jnp.concatenate(mixed, axis=1), proj_ref[...])
        normed = layer_norm(attended, mlp_gain_ref[...]).astype(BF16)
        hidden = jax.nn.gelu(mm(normed, up_ref[...])).astype(BF16)
        backbone = attended + mm(hidden, down_ref[...])
        blended = jnp.concatenate(
            [
                mixing[l][0] * backbone[:PATCHES] + mixing[l][1] * backbone[PATCHES:] + embeds[l]
                for l in range(LEV)
            ],
            axis=0,
        )
        normed = layer_norm(blended, dec_gain_ref[...]).astype(BF16)
        state[...] = (state[...] + mm(normed, dec_ref[...])).astype(BF16).astype(F32)
        return carry

    lax.fori_loop(0, STEPS, step, 0)
    for l in range(LEV):
        wide[:, l * PIN : (l + 1) * PIN] = state[l * PATCHES : (l + 1) * PATCHES, :]
    out_ref[0] = wide[...].reshape(PATCHES // 2, 2, LEV * PIN).astype(BF16)


def turn_kernel(step, direction, x_ref, out_ref):
    count = x_ref.shape[0] if len(x_ref.shape) == 3 else out_ref.shape[0]
    turned = lax.axis_index("lon") < step
    blocks = x_ref[...].astype(F32).reshape(count, 2, LEV * PIN)

    @pl.when(turned)
    def _():
        if direction > 0:
            moved = jnp.concatenate([blocks[1:], blocks[:1]], axis=0)
        else:
            moved = jnp.concatenate([blocks[-1:], blocks[:-1]], axis=0)
        out_ref[...] = moved.reshape(out_ref.shape).astype(BF16)

    @pl.when(jnp.logical_not(turned))
    def _():
        out_ref[...] = blocks.reshape(out_ref.shape).astype(BF16)


def turn(array, shape, step, direction):
    return pl.pallas_call(
        functools.partial(turn_kernel, step, direction),
        out_shape=jax.ShapeDtypeStruct(shape, BF16),
    )(array)


def forecast(windows, arranged, ids, mix, *tensors):
    vmem = pl.BlockSpec(memory_space=pltpu.VMEM)
    smem = pl.BlockSpec(memory_space=pltpu.SMEM)
    block = pl.BlockSpec((1,) + arranged.shape[1:], lambda i: (i, 0, 0, 0))
    return pl.pallas_call(
        functools.partial(forecast_kernel, windows),
        grid=(windows,),
        in_specs=[smem, smem, block] + [vmem] * len(tensors),
        out_specs=block,
        out_shape=jax.ShapeDtypeStruct(arranged.shape, BF16),
        scratch_shapes=[
            pltpu.VMEM((LEV * PATCHES, PIN), F32),
            pltpu.VMEM((PATCHES, LEV * PIN), F32),
        ],
        compiler_params=pltpu.CompilerParams(vmem_limit_bytes=40 * 1024 * 1024),
    )(ids, mix, arranged, *tensors)


def shards(
    fields,
    level_ids,
    embed_weight,
    level_embed,
    enc_gain,
    latent_query,
    kv_weight,
    pool_out,
    attn_gain,
    qkv_weight,
    attn_proj,
    mlp_gain,
    mlp_up,
    mlp_down,
    level_mix,
    dec_gain,
    dec_weight,
):
    devices = lax.axis_size("lon")
    width = fields.shape[2]
    local_count = fields.shape[1]
    piece_cols = local_count // devices
    lat_count = devices // ROW_PARTS
    bands = lat_count // W_LAT
    cut = (W_LON // 2 // piece_cols) * lat_count
    outgoing = turn(fields.reshape(local_count, width), (devices, piece_cols, width), cut, 1)
    got = lax.all_to_all(outgoing, "lon", split_axis=0, concat_axis=0, tiled=True)
    if bands > 1:
        got = got.reshape(ROW_PARTS, lat_count, piece_cols, width)
        got = jnp.roll(got, -(W_LAT // 2), axis=1)
        got = got.reshape(ROW_PARTS, bands, W_LAT, piece_cols, width).transpose(1, 0, 2, 3, 4)
    arranged = got.reshape(bands, ROW_PARTS * W_LAT, piece_cols, width)
    done = forecast(
        bands,
        arranged,
        level_ids,
        level_mix,
        level_embed,
        enc_gain.reshape(1, D),
        latent_query,
        attn_gain.reshape(1, D),
        mlp_gain.reshape(1, D),
        dec_gain.reshape(1, D),
        embed_weight,
        kv_weight,
        pool_out,
        qkv_weight,
        attn_proj,
        mlp_up,
        mlp_down,
        dec_weight,
    )
    if bands > 1:
        done = done.reshape(bands, ROW_PARTS, W_LAT, piece_cols, width).transpose(1, 0, 2, 3, 4)
        done = done.reshape(ROW_PARTS, lat_count, piece_cols, width)
        done = jnp.roll(done, W_LAT // 2, axis=1)
    done = done.reshape(devices, piece_cols, width)
    home = lax.all_to_all(done, "lon", split_axis=0, concat_axis=0, tiled=True)
    return turn(home, (local_count, width), cut, -1).reshape(fields.shape)


def solution(mesh):
    placed = (P(("groups", "lon"), None, None), P("groups")) + (P(),) * 15
    return jax.shard_map(
        shards,
        mesh=mesh,
        in_specs=placed,
        out_specs=P(("groups", "lon"), None, None),
        check_vma=False,
    )
```

```python
import functools

import jax
import jax.numpy as jnp
from jax import lax
from jax.experimental import pallas as pl
from jax.experimental.pallas import tpu as pltpu
from jax.sharding import PartitionSpec as P

D = 512
HEADS = 8
HEAD_DIM = D // HEADS
PIN = 500
LEV = 3
LATL = 2
W_LAT = 4
W_LON = 8
STEPS = 2
ROW_PARTS = 4
MLP = 2048
PATCHES = W_LAT * W_LON
TOKENS = PATCHES * LATL
HALF = D // 2
PAIR = 2 * HEAD_DIM
PARAMETERS = 16

norm_eps = 1e-05
head_eps = 1e-06

F32 = jnp.float32
BF16 = jnp.bfloat16


def mm(a, b):
    return jnp.dot(a, b, preferred_element_type=F32)


def mm_t(a, b):
    return lax.dot_general(a, b, (((1,), (1,)), ((), ())), preferred_element_type=F32)


def layer_norm(values, gain):
    average = jnp.mean(values, axis=-1, keepdims=True)
    centred = values - average
    spread = jnp.mean(centred * centred, axis=-1, keepdims=True)
    return centred * lax.rsqrt(spread + norm_eps) * gain


def iota(shape, dim):
    return lax.broadcasted_iota(jnp.int32, shape, dim)


def picked(index, rows):
    result = rows[LEV - 1]
    for i in reversed(range(LEV - 1)):
        result = jnp.where(index == i, rows[i], result)
    return result


def forecast_kernel(windows, *refs):
    parameters, (x_ref, out_ref) = refs[:PARAMETERS], refs[PARAMETERS : PARAMETERS + 2]
    held = refs[PARAMETERS + 2 : 2 * PARAMETERS + 2]
    state, wide, arrivals = refs[2 * PARAMETERS + 2 :]
    (
        ids_ref,
        mix_ref,
        level_embed_ref,
        latent_query_ref,
        enc_gain_ref,
        embed_ref,
        kv_ref,
        pool_ref,
        attn_gain_ref,
        qkv_ref,
        proj_ref,
        mlp_gain_ref,
        up_ref,
        down_ref,
        dec_gain_ref,
        dec_ref,
    ) = held
    copies = {
        id(there): pltpu.make_async_copy(here, there, arrivals.at[i])
        for i, (here, there) in enumerate(zip(parameters, held))
    }

    def in_first_window(action):
        if windows == 1:
            action()
        else:
            pl.when(pl.program_id(0) == 0)(action)

    def start_all():
        for there in held:
            copies[id(there)].start()

    def wait_for(*wanted):
        def action():
            for there in wanted:
                copies[id(there)].wait()

        in_first_window(action)

    in_first_window(start_all)
    wait_for(ids_ref, mix_ref, level_embed_ref, latent_query_ref)

    table = level_embed_ref[...].astype(F32)
    rows = [table[i : i + 1] for i in range(LEV)]
    embeds = [picked(ids_ref[l], rows) for l in range(LEV)]
    mixing = [[mix_ref[j, ids_ref[l]] for j in range(LATL)] for l in range(LEV)]
    latent = latent_query_ref[...].astype(F32)

    row16 = iota((LATL * HEADS, D), 0)
    lane_head = iota((LATL * HEADS, D), 1) // HEAD_DIM
    on_head = (row16 % HEADS) == lane_head
    square = (latent * latent)
    query_rows = []
    for j in range(LATL):
        masked = jnp.where(on_head[:HEADS], square[j : j + 1], 0.0)
        scale = lax.rsqrt(jnp.sum(masked, axis=-1, keepdims=True) / HEAD_DIM + head_eps)
        query_rows.append(jnp.where(on_head[:HEADS], latent[j : j + 1] * scale, 0.0))
    query_table = jnp.concatenate(query_rows, axis=0).astype(BF16)
    mean_table = jnp.where(on_head, 1.0 / HEAD_DIM, 0.0).astype(BF16)
    spread_row = iota((LATL * HEADS, LATL * D), 0)
    spread_lane = iota((LATL * HEADS, LATL * D), 1)
    spreader = jnp.where(spread_row == spread_lane // HEAD_DIM, 1.0, 0.0).astype(BF16)
    block_ones = jnp.where(
        iota((HALF, HALF), 0) // HEAD_DIM == iota((HALF, HALF), 1) // HEAD_DIM, 1.0 / HEAD_DIM, 0.0
    ).astype(BF16)
    low = iota((1, PAIR), 1) < HEAD_DIM
    half_ones = jnp.where(
        (iota((PAIR, PAIR), 0) < HEAD_DIM) == (iota((PAIR, PAIR), 1) < HEAD_DIM), 1.0, 0.0
    ).astype(BF16)
    row_bit = (iota((TOKENS, PAIR), 0) // 4) % 2
    lane_bit = (iota((TOKENS, PAIR), 1) // 4) % 2
    cut = jnp.where(pl.program_id(0) == windows - 1, 1, 0)
    allowed = jnp.where((row_bit - lane_bit) * cut == 0, 1.0, 0.0)

    arrived = x_ref[0].astype(F32).reshape(PATCHES, LEV * PIN)
    for l in range(LEV):
        state[l * PATCHES : (l + 1) * PATCHES, :] = arrived[:, l * PIN : (l + 1) * PIN]

    def step(first):
        wait = wait_for if first else lambda *wanted: None
        wait(enc_gain_ref, embed_ref)
        patches = state[...].astype(BF16)
        tokens = mm(patches, embed_ref[...])
        tokens = jnp.concatenate(
            [tokens[l * PATCHES : (l + 1) * PATCHES] + embeds[l] for l in range(LEV)], axis=0
        )
        tokens = layer_norm(tokens, enc_gain_ref[...]).astype(BF16)
        wait(kv_ref)
        keyval = mm(tokens, kv_ref[...])
        keys = keyval[:, :D]
        values = keyval[:, D:].astype(BF16).astype(F32)
        mean_square = mm_t((keys * keys).astype(BF16), mean_table)
        scores = mm_t(keys.astype(BF16), query_table)
        scores = scores * lax.rsqrt(mean_square + head_eps) * HEAD_DIM ** (-0.5)
        weights = jnp.exp(scores)
        parts = [weights[l * PATCHES : (l + 1) * PATCHES] for l in range(LEV)]
        inverse = 1.0 / (parts[0] + parts[1] + parts[2])
        weights = jnp.concatenate([part * inverse for part in parts], axis=0).astype(BF16)
        wide_weights = mm(weights, spreader)
        pooled = []
        for j in range(LATL):
            total = None
            for l in range(LEV):
                term = (
                    wide_weights[l * PATCHES : (l + 1) * PATCHES, j * D : (j + 1) * D]
                    * values[l * PATCHES : (l + 1) * PATCHES]
                )
                total = term if total is None else total + term
            pooled.append(total)
        pooled = jnp.concatenate(pooled, axis=0).astype(BF16)
        wait(pool_ref)
        latents = mm(pooled, pool_ref[...])
        latents = jnp.concatenate(
            [latents[j * PATCHES : (j + 1) * PATCHES] + latent[j : j + 1] for j in range(LATL)],
            axis=0,
        )
        wait(attn_gain_ref, qkv_ref)
        normed = layer_norm(latents, attn_gain_ref[...]).astype(BF16)
        projected = mm(normed, qkv_ref[...])
        halves = jnp.concatenate(
            [projected[:, i * HALF : (i + 1) * HALF] for i in range(4)], axis=0
        )
        mean_square = mm((halves * halves).astype(BF16), block_ones)
        halves = halves * lax.rsqrt(mean_square + head_eps)
        win_values = projected[:, 2 * D :]
        mixed = []
        for pair in range(HEADS // 2):
            half, at = pair // 2, (pair % 2) * PAIR
            query = halves[half * TOKENS : (half + 1) * TOKENS, at : at + PAIR].astype(BF16)
            key = halves[(2 + half) * TOKENS : (3 + half) * TOKENS, at : at + PAIR]
            value = win_values[:, pair * PAIR : (pair + 1) * PAIR]
            key = jnp.concatenate(
                [jnp.where(low, key, 0.0), jnp.where(low, 0.0, key)], axis=0
            ).astype(BF16)
            value = jnp.concatenate(
                [jnp.where(low, value, 0.0), jnp.where(low, 0.0, value)], axis=0
            ).astype(BF16)
            weights = jnp.exp(mm_t(query, key) * HEAD_DIM ** (-0.5)) * allowed
            weights = weights.astype(BF16)
            both = mm(weights, jnp.concatenate([value, half_ones], axis=1))
            mixed.append((both[:, :PAIR] / both[:, PAIR:]).astype(BF16))
        wait(proj_ref)
        attended = latents + mm(jnp.concatenate(mixed, axis=1), proj_ref[...])
        wait(mlp_gain_ref, up_ref)
        normed = layer_norm(attended, mlp_gain_ref[...]).astype(BF16)
        hidden = jax.nn.gelu(mm(normed, up_ref[...])).astype(BF16)
        wait(down_ref)
        backbone = attended + mm(hidden, down_ref[...])
        wait(dec_gain_ref, dec_ref)
        blended = jnp.concatenate(
            [
                mixing[l][0] * backbone[:PATCHES] + mixing[l][1] * backbone[PATCHES:] + embeds[l]
                for l in range(LEV)
            ],
            axis=0,
        )
        normed = layer_norm(blended, dec_gain_ref[...]).astype(BF16)
        state[...] = (state[...] + mm_t(normed, dec_ref[...])).astype(BF16).astype(F32)

    for turn_index in range(STEPS):
        step(turn_index == 0)
    for l in range(LEV):
        wide[:, l * PIN : (l + 1) * PIN] = state[l * PATCHES : (l + 1) * PATCHES, :]
    out_ref[0] = wide[...].reshape(PATCHES // 2, 2, LEV * PIN).astype(BF16)


def turn_kernel(step, direction, x_ref, out_ref):
    count = x_ref.shape[0] if len(x_ref.shape) == 3 else out_ref.shape[0]
    turned = lax.axis_index("lon") < step
    blocks = x_ref[...].astype(F32).reshape(count, 2, LEV * PIN)

    @pl.when(turned)
    def _():
        if direction > 0:
            moved = jnp.concatenate([blocks[1:], blocks[:1]], axis=0)
        else:
            moved = jnp.concatenate([blocks[-1:], blocks[:-1]], axis=0)
        out_ref[...] = moved.reshape(out_ref.shape).astype(BF16)

    @pl.when(jnp.logical_not(turned))
    def _():
        out_ref[...] = blocks.reshape(out_ref.shape).astype(BF16)


def turn(array, shape, step, direction):
    return pl.pallas_call(
        functools.partial(turn_kernel, step, direction),
        out_shape=jax.ShapeDtypeStruct(shape, BF16),
    )(array)


def forecast(windows, arranged, *parameters):
    block = pl.BlockSpec((1,) + arranged.shape[1:], lambda i: (i, 0, 0, 0))
    held = [
        pltpu.SMEM(a.shape, a.dtype) if i < 2 else pltpu.VMEM(a.shape, a.dtype)
        for i, a in enumerate(parameters)
    ]
    return pl.pallas_call(
        functools.partial(forecast_kernel, windows),
        grid=(windows,),
        in_specs=[pl.BlockSpec(memory_space=pl.ANY)] * PARAMETERS + [block],
        out_specs=block,
        out_shape=jax.ShapeDtypeStruct(arranged.shape, BF16),
        scratch_shapes=held
        + [
            pltpu.VMEM((LEV * PATCHES, PIN), F32),
            pltpu.VMEM((PATCHES, LEV * PIN), F32),
            pltpu.SemaphoreType.DMA((PARAMETERS,)),
        ],
        compiler_params=pltpu.CompilerParams(vmem_limit_bytes=56 * 1024 * 1024),
    )(*parameters, arranged)


def shards(
    fields,
    level_ids,
    embed_weight,
    level_embed,
    enc_gain,
    latent_query,
    kv_weight,
    pool_out,
    attn_gain,
    qkv_weight,
    attn_proj,
    mlp_gain,
    mlp_up,
    mlp_down,
    level_mix,
    dec_gain,
    dec_weight,
):
    devices = lax.axis_size("lon")
    width = fields.shape[2]
    local_count = fields.shape[1]
    piece_cols = local_count // devices
    lat_count = devices // ROW_PARTS
    bands = lat_count // W_LAT
    cut = (W_LON // 2 // piece_cols) * lat_count
    outgoing = turn(fields.reshape(local_count, width), (devices, piece_cols, width), cut, 1)
    got = lax.all_to_all(outgoing, "lon", split_axis=0, concat_axis=0, tiled=True)
    if bands > 1:
        got = got.reshape(ROW_PARTS, lat_count, piece_cols, width)
        got = jnp.roll(got, -(W_LAT // 2), axis=1)
        got = got.reshape(ROW_PARTS, bands, W_LAT, piece_cols, width).transpose(1, 0, 2, 3, 4)
    arranged = got.reshape(bands, ROW_PARTS * W_LAT, piece_cols, width)
    done = forecast(
        bands,
        arranged,
        level_ids,
        level_mix.T,
        level_embed,
        latent_query,
        enc_gain.reshape(1, D),
        embed_weight,
        kv_weight,
        pool_out,
        attn_gain.reshape(1, D),
        qkv_weight,
        attn_proj,
        mlp_gain.reshape(1, D),
        mlp_up,
        mlp_down,
        dec_gain.reshape(1, D),
        dec_weight.T,
    )
    if bands > 1:
        done = done.reshape(bands, ROW_PARTS, W_LAT, piece_cols, width).transpose(1, 0, 2, 3, 4)
        done = done.reshape(ROW_PARTS, lat_count, piece_cols, width)
        done = jnp.roll(done, W_LAT // 2, axis=1)
    done = done.reshape(devices, piece_cols, width)
    home = lax.all_to_all(done, "lon", split_axis=0, concat_axis=0, tiled=True)
    return turn(home, (local_count, width), cut, -1).reshape(fields.shape)


def solution(mesh):
    placed = (P(("groups", "lon"), None, None), P("groups")) + (P(),) * 15
    return jax.shard_map(
        shards,
        mesh=mesh,
        in_specs=placed,
        out_specs=P(("groups", "lon"), None, None),
        check_vma=False,
    )
```

```python
import functools

import jax
import jax.numpy as jnp
from jax import lax
from jax.experimental import pallas as pl
from jax.experimental.pallas import tpu as pltpu
from jax.sharding import PartitionSpec as P

D = 512
HEADS = 8
HEAD_DIM = D // HEADS
PIN = 500
LEV = 3
LATL = 2
W_LAT = 4
W_LON = 8
STEPS = 2
ROW_PARTS = 4
MLP = 2048
PATCHES = W_LAT * W_LON
TOKENS = PATCHES * LATL
HALF = D // 2
PAIR = 2 * HEAD_DIM
PARAMETERS = 16

norm_eps = 1e-05
head_eps = 1e-06

F32 = jnp.float32
BF16 = jnp.bfloat16


def mm(a, b):
    return jnp.dot(a, b, preferred_element_type=F32)


def mm_t(a, b):
    return lax.dot_general(a, b, (((1,), (1,)), ((), ())), preferred_element_type=F32)


def layer_norm(values, gain):
    average = jnp.mean(values, axis=-1, keepdims=True)
    centred = values - average
    spread = jnp.mean(centred * centred, axis=-1, keepdims=True)
    return centred * lax.rsqrt(spread + norm_eps) * gain


def iota(shape, dim):
    return lax.broadcasted_iota(jnp.int32, shape, dim)


def picked(index, rows):
    result = rows[LEV - 1]
    for i in reversed(range(LEV - 1)):
        result = jnp.where(index == i, rows[i], result)
    return result


def forecast_kernel(windows, blocks, *refs):
    (
        ids_ref,
        mix_ref,
        level_embed_ref,
        latent_query_ref,
        enc_gain_ref,
        attn_gain_ref,
        mlp_gain_ref,
        dec_gain_ref,
        embed_ref,
        kv_ref,
        pool_ref,
        qkv_ref,
        proj_ref,
        up_ref,
        down_ref,
        dec_ref,
    ) = refs[:PARAMETERS]
    refs = refs[PARAMETERS:]
    x_refs, out_refs, (state, wide) = refs[:blocks], refs[blocks : 2 * blocks], refs[2 * blocks :]

    table = level_embed_ref[...].astype(F32)
    rows = [table[i : i + 1] for i in range(LEV)]
    embeds = [picked(ids_ref[l], rows) for l in range(LEV)]
    mixing = [[mix_ref[j, ids_ref[l]] for j in range(LATL)] for l in range(LEV)]
    latent = latent_query_ref[...].astype(F32)

    row16 = iota((LATL * HEADS, D), 0)
    lane_head = iota((LATL * HEADS, D), 1) // HEAD_DIM
    on_head = (row16 % HEADS) == lane_head
    square = (latent * latent)
    query_rows = []
    for j in range(LATL):
        masked = jnp.where(on_head[:HEADS], square[j : j + 1], 0.0)
        scale = lax.rsqrt(jnp.sum(masked, axis=-1, keepdims=True) / HEAD_DIM + head_eps)
        query_rows.append(jnp.where(on_head[:HEADS], latent[j : j + 1] * scale, 0.0))
    query_table = jnp.concatenate(query_rows, axis=0).astype(BF16)
    mean_table = jnp.where(on_head, 1.0 / HEAD_DIM, 0.0).astype(BF16)
    spread_row = iota((LATL * HEADS, LATL * D), 0)
    spread_lane = iota((LATL * HEADS, LATL * D), 1)
    spreader = jnp.where(spread_row == spread_lane // HEAD_DIM, 1.0, 0.0).astype(BF16)
    block_ones = jnp.where(
        iota((HALF, HALF), 0) // HEAD_DIM == iota((HALF, HALF), 1) // HEAD_DIM, 1.0 / HEAD_DIM, 0.0
    ).astype(BF16)
    low = iota((1, PAIR), 1) < HEAD_DIM
    half_ones = jnp.where(
        (iota((PAIR, PAIR), 0) < HEAD_DIM) == (iota((PAIR, PAIR), 1) < HEAD_DIM), 1.0, 0.0
    ).astype(BF16)
    row_bit = (iota((TOKENS, PAIR), 0) // 4) % 2
    lane_bit = (iota((TOKENS, PAIR), 1) // 4) % 2
    cut = jnp.where(pl.program_id(0) == windows - 1, 1, 0)
    allowed = jnp.where((row_bit - lane_bit) * cut == 0, 1.0, 0.0)

    if blocks == 1:
        arrived = x_refs[0][0].astype(F32).reshape(PATCHES, LEV * PIN)
    else:
        arrived = jnp.concatenate([x_ref[...].astype(F32) for x_ref in x_refs], axis=0)
    for l in range(LEV):
        state[l * PATCHES : (l + 1) * PATCHES, :] = arrived[:, l * PIN : (l + 1) * PIN]

    def step():
        patches = state[...].astype(BF16)
        tokens = mm(patches, embed_ref[...])
        tokens = jnp.concatenate(
            [tokens[l * PATCHES : (l + 1) * PATCHES] + embeds[l] for l in range(LEV)], axis=0
        )
        tokens = layer_norm(tokens, enc_gain_ref[...]).astype(BF16)
        keyval = mm(tokens, kv_ref[...])
        keys = keyval[:, :D]
        values = keyval[:, D:].astype(BF16).astype(F32)
        mean_square = mm_t((keys * keys).astype(BF16), mean_table)
        scores = mm_t(keys.astype(BF16), query_table)
        scores = scores * lax.rsqrt(mean_square + head_eps) * HEAD_DIM ** (-0.5)
        weights = jnp.exp(scores)
        parts = [weights[l * PATCHES : (l + 1) * PATCHES] for l in range(LEV)]
        inverse = 1.0 / (parts[0] + parts[1] + parts[2])
        weights = jnp.concatenate([part * inverse for part in parts], axis=0).astype(BF16)
        wide_weights = mm(weights, spreader)
        pooled = []
        for j in range(LATL):
            total = None
            for l in range(LEV):
                term = (
                    wide_weights[l * PATCHES : (l + 1) * PATCHES, j * D : (j + 1) * D]
                    * values[l * PATCHES : (l + 1) * PATCHES]
                )
                total = term if total is None else total + term
            pooled.append(total)
        pooled = jnp.concatenate(pooled, axis=0).astype(BF16)
        latents = mm(pooled, pool_ref[...])
        latents = jnp.concatenate(
            [latents[j * PATCHES : (j + 1) * PATCHES] + latent[j : j + 1] for j in range(LATL)],
            axis=0,
        )
        normed = layer_norm(latents, attn_gain_ref[...]).astype(BF16)
        projected = mm(normed, qkv_ref[...])
        halves = jnp.concatenate(
            [projected[:, i * HALF : (i + 1) * HALF] for i in range(4)], axis=0
        )
        mean_square = mm((halves * halves).astype(BF16), block_ones)
        halves = halves * lax.rsqrt(mean_square + head_eps)
        win_values = projected[:, 2 * D :]
        mixed = []
        for pair in range(HEADS // 2):
            half, at = pair // 2, (pair % 2) * PAIR
            query = halves[half * TOKENS : (half + 1) * TOKENS, at : at + PAIR].astype(BF16)
            key = halves[(2 + half) * TOKENS : (3 + half) * TOKENS, at : at + PAIR]
            value = win_values[:, pair * PAIR : (pair + 1) * PAIR]
            key = jnp.concatenate(
                [jnp.where(low, key, 0.0), jnp.where(low, 0.0, key)], axis=0
            ).astype(BF16)
            value = jnp.concatenate(
                [jnp.where(low, value, 0.0), jnp.where(low, 0.0, value)], axis=0
            ).astype(BF16)
            weights = jnp.exp(mm_t(query, key) * HEAD_DIM ** (-0.5)) * allowed
            weights = weights.astype(BF16)
            both = mm(weights, jnp.concatenate([value, half_ones], axis=1))
            mixed.append((both[:, :PAIR] / both[:, PAIR:]).astype(BF16))
        attended = latents + mm(jnp.concatenate(mixed, axis=1), proj_ref[...])
        normed = layer_norm(attended, mlp_gain_ref[...]).astype(BF16)
        hidden = jax.nn.gelu(mm(normed, up_ref[...])).astype(BF16)
        backbone = attended + mm(hidden, down_ref[...])
        blended = jnp.concatenate(
            [
                mixing[l][0] * backbone[:PATCHES] + mixing[l][1] * backbone[PATCHES:] + embeds[l]
                for l in range(LEV)
            ],
            axis=0,
        )
        normed = layer_norm(blended, dec_gain_ref[...]).astype(BF16)
        state[...] = (state[...] + mm_t(normed, dec_ref[...])).astype(BF16).astype(F32)

    for _ in range(STEPS):
        step()
    for l in range(LEV):
        wide[:, l * PIN : (l + 1) * PIN] = state[l * PATCHES : (l + 1) * PATCHES, :]
    if blocks == 1:
        out_refs[0][0] = wide[...].reshape(out_refs[0].shape[1:]).astype(BF16)
    else:
        size = PATCHES // blocks
        for k in range(blocks):
            out_refs[k][...] = wide[k * size : (k + 1) * size].astype(BF16)


def turn_kernel(step, direction, x_ref, out_ref):
    count = x_ref.shape[0] if len(x_ref.shape) == 3 else out_ref.shape[0]
    turned = lax.axis_index("lon") < step
    blocks = x_ref[...].astype(F32).reshape(count, 2, LEV * PIN)

    @pl.when(turned)
    def _():
        if direction > 0:
            moved = jnp.concatenate([blocks[1:], blocks[:1]], axis=0)
        else:
            moved = jnp.concatenate([blocks[-1:], blocks[:-1]], axis=0)
        out_ref[...] = moved.reshape(out_ref.shape).astype(BF16)

    @pl.when(jnp.logical_not(turned))
    def _():
        out_ref[...] = blocks.reshape(out_ref.shape).astype(BF16)


def turn(array, shape, step, direction):
    return pl.pallas_call(
        functools.partial(turn_kernel, step, direction),
        out_shape=jax.ShapeDtypeStruct(shape, BF16),
    )(array)


def scatter_kernel(devices, lag, x_ref, *refs):
    out_refs, apart = refs[:devices], refs[devices]
    me = lax.axis_index("lon")
    shift = jnp.where(me < lag, 1, 0)
    apart[...] = x_ref[...].astype(F32).reshape(apart.shape)
    for k in range(devices):
        place = lax.rem((me ^ k) + shift, devices)
        out_refs[k][...] = apart[place].astype(BF16)


def gather_kernel(devices, lag, *refs):
    x_refs, (out_ref, apart) = refs[:devices], refs[devices:]
    me = lax.axis_index("lon")
    shift = jnp.where(me < lag, 1, 0)
    for k in range(devices):
        place = lax.rem((me ^ k) + shift, devices)
        apart[place] = x_refs[k][...].astype(F32)
    out_ref[...] = apart[...].reshape(out_ref.shape).astype(BF16)


def load_kernel(*refs):
    count = (len(refs) - 2) // 2
    here, there, arrivals = refs[:count], refs[count + 1 : -1], refs[-1]
    copies = [
        pltpu.make_async_copy(here[i], there[i], arrivals.at[i]) for i in range(count)
    ]
    for copy in copies:
        copy.start()
    for copy in copies:
        copy.wait()


def load(after, parameters):
    far = pl.BlockSpec(memory_space=pl.ANY)
    return pl.pallas_call(
        load_kernel,
        in_specs=[far] * (len(parameters) + 1),
        out_specs=[pl.BlockSpec(memory_space=pltpu.VMEM)] * len(parameters),
        out_shape=[pltpu.VMEM(a.shape, a.dtype) for a in parameters],
        scratch_shapes=[pltpu.SemaphoreType.DMA((len(parameters),))],
        compiler_params=pltpu.CompilerParams(vmem_limit_bytes=55 * 1024 * 1024),
        cost_estimate=pl.CostEstimate(
            flops=0,
            bytes_accessed=sum(a.size * a.dtype.itemsize for a in parameters),
            transcendentals=0,
        ),
    )(*parameters, after)


def exchange(blocks):
    devices = len(blocks)
    return list(blocks[:1]) + [
        lax.ppermute(blocks[k], "lon", [(i, i ^ k) for i in range(devices)])
        for k in range(1, devices)
    ]


def forecast(windows, arranged, *parameters):
    blocks = len(arranged)
    shape = arranged[0].shape
    vmem = pl.BlockSpec(memory_space=pltpu.VMEM)
    smem = pl.BlockSpec(memory_space=pltpu.SMEM)
    block = pl.BlockSpec((1,) + shape[1:], lambda i: (i, 0, 0, 0)) if blocks == 1 else vmem
    return pl.pallas_call(
        functools.partial(forecast_kernel, windows, blocks),
        grid=(windows,),
        in_specs=[smem] * 2 + [vmem] * (PARAMETERS - 2) + [block] * blocks,
        out_specs=[block] * blocks,
        out_shape=[jax.ShapeDtypeStruct(shape, BF16)] * blocks,
        scratch_shapes=[
            pltpu.VMEM((LEV * PATCHES, PIN), F32),
            pltpu.VMEM((PATCHES, LEV * PIN), F32),
        ],
        compiler_params=pltpu.CompilerParams(vmem_limit_bytes=24 * 1024 * 1024),
    )(*parameters, *arranged)


def shards(
    fields,
    level_ids,
    embed_weight,
    level_embed,
    enc_gain,
    latent_query,
    kv_weight,
    pool_out,
    attn_gain,
    qkv_weight,
    attn_proj,
    mlp_gain,
    mlp_up,
    mlp_down,
    level_mix,
    dec_gain,
    dec_weight,
):
    devices = lax.axis_size("lon")
    width = fields.shape[2]
    local_count = fields.shape[1]
    piece_cols = local_count // devices
    lat_count = devices // ROW_PARTS
    bands = lat_count // W_LAT
    cut = (W_LON // 2 // piece_cols) * lat_count
    scalars = (level_ids, level_mix.T)
    tensors = (
        level_embed,
        latent_query,
        enc_gain.reshape(1, D),
        attn_gain.reshape(1, D),
        mlp_gain.reshape(1, D),
        dec_gain.reshape(1, D),
        embed_weight,
        kv_weight,
        pool_out,
        qkv_weight,
        attn_proj,
        mlp_up,
        mlp_down,
        dec_weight.T,
    )
    if devices == ROW_PARTS * W_LAT:
        piece = jax.ShapeDtypeStruct((piece_cols, width), BF16)
        apart = pltpu.VMEM((devices, piece_cols, width), F32)
        outgoing = pl.pallas_call(
            functools.partial(scatter_kernel, devices, cut),
            out_shape=[piece] * devices,
            scratch_shapes=[apart],
        )(fields.reshape(local_count, width))
        held = load(outgoing[0], tensors)
        done = forecast(1, exchange(outgoing), *scalars, *held)
        home = pl.pallas_call(
            functools.partial(gather_kernel, devices, cut),
            out_shape=jax.ShapeDtypeStruct((local_count, width), BF16),
            scratch_shapes=[apart],
        )(*exchange(done))
        return home.reshape(fields.shape)
    outgoing = turn(fields.reshape(local_count, width), (devices, piece_cols, width), cut, 1)
    held = load(outgoing, tensors)
    got = lax.all_to_all(outgoing, "lon", split_axis=0, concat_axis=0, tiled=True)
    got = got.reshape(ROW_PARTS, lat_count, piece_cols, width)
    got = jnp.roll(got, -(W_LAT // 2), axis=1)
    got = got.reshape(ROW_PARTS, bands, W_LAT, piece_cols, width).transpose(1, 0, 2, 3, 4)
    arranged = got.reshape(bands, ROW_PARTS * W_LAT, piece_cols, width)
    (done,) = forecast(bands, [arranged], *scalars, *held)
    done = done.reshape(bands, ROW_PARTS, W_LAT, piece_cols, width).transpose(1, 0, 2, 3, 4)
    done = done.reshape(ROW_PARTS, lat_count, piece_cols, width)
    done = jnp.roll(done, W_LAT // 2, axis=1).reshape(devices, piece_cols, width)
    home = lax.all_to_all(done, "lon", split_axis=0, concat_axis=0, tiled=True)
    return turn(home, (local_count, width), cut, -1).reshape(fields.shape)


def solution(mesh):
    placed = (P(("groups", "lon"), None, None), P("groups")) + (P(),) * 15
    return jax.shard_map(
        shards,
        mesh=mesh,
        in_specs=placed,
        out_specs=P(("groups", "lon"), None, None),
        check_vma=False,
    )
```

```python
import functools

import jax
import jax.numpy as jnp
from jax import lax
from jax.experimental import pallas as pl
from jax.experimental.pallas import tpu as pltpu
from jax.sharding import PartitionSpec as P

D = 512
HEADS = 8
HEAD_DIM = D // HEADS
PIN = 500
LEV = 3
LATL = 2
W_LAT = 4
W_LON = 8
STEPS = 2
ROW_PARTS = 4
MLP = 2048
PATCHES = W_LAT * W_LON
TOKENS = PATCHES * LATL
HALF = D // 2
PAIR = 2 * HEAD_DIM
LANES = 128
EMBED_ROW, MIX_ROW, LATENT_ROW, GAIN_ROW, TABLE_ROWS = 0, 3, 9, 11, 16

norm_eps = 1e-05
head_eps = 1e-06

F32 = jnp.float32
BF16 = jnp.bfloat16


def mm(a, b):
    return jnp.dot(a, b, preferred_element_type=F32)


def mm_t(a, b):
    return lax.dot_general(a, b, (((1,), (1,)), ((), ())), preferred_element_type=F32)


def layer_norm(values, gain):
    average = jnp.mean(values, axis=-1, keepdims=True)
    centred = values - average
    spread = jnp.mean(centred * centred, axis=-1, keepdims=True)
    return centred * lax.rsqrt(spread + norm_eps) * gain


def iota(shape, dim):
    return lax.broadcasted_iota(jnp.int32, shape, dim)


def load_kernel(*refs):
    (
        ids_from,
        mix_from,
        level_embed_from,
        latent_query_from,
        enc_gain_from,
        attn_gain_from,
        mlp_gain_from,
        dec_gain_from,
        dec_from,
        embed_from,
        kv_from,
        pool_from,
        qkv_from,
        proj_from,
        up_from,
        down_from,
        _,
        table_ref,
        query_ref,
        mean_ref,
        spread_ref,
        ones_ref,
        half_ref,
        allowed_ref,
        dec_ref,
        embed_ref,
        kv_ref,
        pool_ref,
        qkv_ref,
        proj_ref,
        up_ref,
        down_ref,
        ids_ref,
        mix_ref,
        level_embed_ref,
        latent_query_ref,
        gain_refs,
        dec_rows_ref,
        arrivals,
    ) = refs
    pairs = [
        (ids_from, ids_ref),
        (mix_from, mix_ref),
        (level_embed_from, level_embed_ref),
        (latent_query_from, latent_query_ref),
        (enc_gain_from, gain_refs.at[0]),
        (attn_gain_from, gain_refs.at[1]),
        (mlp_gain_from, gain_refs.at[2]),
        (dec_gain_from, gain_refs.at[3]),
        (dec_from, dec_rows_ref),
        (embed_from, embed_ref),
        (kv_from, kv_ref),
        (pool_from, pool_ref),
        (qkv_from, qkv_ref),
        (proj_from, proj_ref),
        (up_from, up_ref),
        (down_from, down_ref),
    ]
    copies = [
        pltpu.make_async_copy(here, there, arrivals.at[i]) for i, (here, there) in enumerate(pairs)
    ]
    for copy in copies:
        copy.start()

    feature_head = iota((D, LANES), 0) // HEAD_DIM
    lane = iota((D, LANES), 1)
    on_head = (feature_head == lane % HEADS) & (lane < LATL * HEADS)
    mean_ref[...] = jnp.where(on_head, 1.0 / HEAD_DIM, 0.0).astype(BF16)
    spread_ref[...] = jnp.where(
        iota((LANES, LATL * D), 0) == iota((LANES, LATL * D), 1) // HEAD_DIM, 1.0, 0.0
    ).astype(BF16)
    ones_ref[...] = jnp.where(
        iota((HALF, HALF), 0) // HEAD_DIM == iota((HALF, HALF), 1) // HEAD_DIM, 1.0 / HEAD_DIM, 0.0
    ).astype(BF16)
    half_ref[...] = jnp.where(
        (iota((PAIR, PAIR), 0) < HEAD_DIM) == (iota((PAIR, PAIR), 1) < HEAD_DIM), 1.0, 0.0
    ).astype(BF16)
    row_bit = (iota((TOKENS, PAIR), 0) // 4) % 2
    lane_bit = (iota((TOKENS, PAIR), 1) // 4) % 2
    allowed_ref[...] = jnp.where(row_bit == lane_bit, 1.0, 0.0)

    for copy in copies[:8]:
        copy.wait()
    level_embed = level_embed_ref[...].astype(F32)
    for l in range(LEV):
        level = ids_ref[l]
        row = level_embed[LEV - 1 : LEV]
        for i in reversed(range(LEV - 1)):
            row = jnp.where(level == i, level_embed[i : i + 1], row)
        table_ref[EMBED_ROW + l : EMBED_ROW + l + 1, :] = row
        for j in range(LATL):
            at = MIX_ROW + l * LATL + j
            table_ref[at : at + 1, :] = jnp.full((1, D), mix_ref[j, level])
    latent = latent_query_ref[...].astype(F32)
    table_ref[LATENT_ROW : LATENT_ROW + LATL, :] = latent
    for i in range(4):
        table_ref[GAIN_ROW + i : GAIN_ROW + i + 1, :] = gain_refs[i]
    row_id = iota((LANES, D), 0)
    own_head = (row_id % HEADS) == iota((LANES, D), 1) // HEAD_DIM
    spots = jnp.zeros((LANES, D), F32)
    for j in range(LATL):
        mine = own_head & (row_id // HEADS == j)
        spots = jnp.where(mine, jnp.broadcast_to(latent[j : j + 1], (LANES, D)), spots)
    mean_square = jnp.sum(spots * spots, axis=-1, keepdims=True) / HEAD_DIM
    query_ref[...] = (spots * lax.rsqrt(mean_square + head_eps)).T.astype(BF16)

    copies[8].wait()
    dec_ref[...] = dec_rows_ref[...].astype(F32).T.astype(BF16)
    for copy in copies[9:]:
        copy.wait()


def load(after, scalars, rows, matrices):
    far = pl.BlockSpec(memory_space=pl.ANY)
    dec = matrices[0]
    made = [
        pltpu.VMEM((TABLE_ROWS, D), F32),
        pltpu.VMEM((D, LANES), BF16),
        pltpu.VMEM((D, LANES), BF16),
        pltpu.VMEM((LANES, LATL * D), BF16),
        pltpu.VMEM((HALF, HALF), BF16),
        pltpu.VMEM((PAIR, PAIR), BF16),
        pltpu.VMEM((TOKENS, PAIR), F32),
        pltpu.VMEM(dec.shape[::-1], BF16),
    ] + [pltpu.VMEM(a.shape, a.dtype) for a in matrices[1:]]
    inputs = (*scalars, *rows, *matrices)
    return pl.pallas_call(
        load_kernel,
        in_specs=[far] * (len(inputs) + 1),
        out_specs=[pl.BlockSpec(memory_space=pltpu.VMEM)] * len(made),
        out_shape=made,
        scratch_shapes=[pltpu.SMEM(a.shape, a.dtype) for a in scalars]
        + [
            pltpu.VMEM((LEV, D), BF16),
            pltpu.VMEM((LATL, D), BF16),
            pltpu.VMEM((4, 1, D), F32),
            pltpu.VMEM(dec.shape, BF16),
            pltpu.SemaphoreType.DMA((len(inputs),)),
        ],
        compiler_params=pltpu.CompilerParams(vmem_limit_bytes=107 * 512 * 1024),
        cost_estimate=pl.CostEstimate(
            flops=0,
            bytes_accessed=2 * sum(a.size * a.dtype.itemsize for a in inputs),
            transcendentals=0,
        ),
    )(*inputs, after)


def forecast_kernel(
    windows,
    table_ref,
    query_ref,
    mean_ref,
    spread_ref,
    ones_ref,
    half_ref,
    allowed_ref,
    dec_ref,
    embed_ref,
    kv_ref,
    pool_ref,
    qkv_ref,
    proj_ref,
    up_ref,
    down_ref,
    x_ref,
    out_ref,
    state,
    wide,
):
    def entry(at):
        return table_ref[at : at + 1, :]

    def embed(l):
        return entry(EMBED_ROW + l)

    def mixing(l, j):
        return entry(MIX_ROW + l * LATL + j)

    low = iota((1, PAIR), 1) < HEAD_DIM
    allowed = allowed_ref[...]
    if windows > 1:
        cut = jnp.where(pl.program_id(0) == windows - 1, 1.0, 0.0)
        allowed = 1.0 - cut * (1.0 - allowed)

    arrived = x_ref[0].astype(F32).reshape(PATCHES, LEV * PIN)
    for l in range(LEV):
        state[l * PATCHES : (l + 1) * PATCHES, :] = arrived[:, l * PIN : (l + 1) * PIN]

    def by_level(values):
        return [values[l * PATCHES : (l + 1) * PATCHES] for l in range(LEV)]

    for _ in range(STEPS):
        tokens = by_level(mm(state[...].astype(BF16), embed_ref[...]))
        tokens = jnp.concatenate([tokens[l] + embed(l) for l in range(LEV)], axis=0)
        tokens = layer_norm(tokens, entry(GAIN_ROW)).astype(BF16)
        keyval = mm(tokens, kv_ref[...])
        keys = keyval[:, :D]
        values = by_level(keyval[:, D:])
        mean_square = mm((keys * keys).astype(BF16), mean_ref[...])
        scores = mm(keys.astype(BF16), query_ref[...])
        scores = scores * lax.rsqrt(mean_square + head_eps) * HEAD_DIM ** (-0.5)
        parts = by_level(jnp.exp(scores))
        inverse = 1.0 / (parts[0] + parts[1] + parts[2])
        weights = jnp.concatenate([part * inverse for part in parts], axis=0).astype(BF16)
        wide_weights = by_level(mm(weights, spread_ref[...]))
        pooled = []
        for j in range(LATL):
            terms = [wide_weights[l][:, j * D : (j + 1) * D] * values[l] for l in range(LEV)]
            pooled.append(terms[0] + terms[1] + terms[2])
        latents = mm(jnp.concatenate(pooled, axis=0).astype(BF16), pool_ref[...])
        latents = jnp.concatenate(
            [
                latents[j * PATCHES : (j + 1) * PATCHES] + entry(LATENT_ROW + j)
                for j in range(LATL)
            ],
            axis=0,
        )
        normed = layer_norm(latents, entry(GAIN_ROW + 1)).astype(BF16)
        projected = mm(normed, qkv_ref[...])
        halves = jnp.concatenate(
            [projected[:, i * HALF : (i + 1) * HALF] for i in range(4)], axis=0
        )
        mean_square = mm((halves * halves).astype(BF16), ones_ref[...])
        halves = halves * lax.rsqrt(mean_square + head_eps)
        win_values = projected[:, 2 * D :]
        mixed = []
        for pair in range(HEADS // 2):
            half, at = pair // 2, (pair % 2) * PAIR
            query = halves[half * TOKENS : (half + 1) * TOKENS, at : at + PAIR].astype(BF16)
            key = halves[(2 + half) * TOKENS : (3 + half) * TOKENS, at : at + PAIR]
            value = win_values[:, pair * PAIR : (pair + 1) * PAIR]
            key = jnp.concatenate(
                [jnp.where(low, key, 0.0), jnp.where(low, 0.0, key)], axis=0
            ).astype(BF16)
            value = jnp.concatenate(
                [jnp.where(low, value, 0.0), jnp.where(low, 0.0, value)], axis=0
            ).astype(BF16)
            weights = jnp.exp(mm_t(query, key) * HEAD_DIM ** (-0.5)) * allowed
            both = mm(weights.astype(BF16), jnp.concatenate([value, half_ref[...]], axis=1))
            mixed.append((both[:, :PAIR] / both[:, PAIR:]).astype(BF16))
        attended = latents + mm(jnp.concatenate(mixed, axis=1), proj_ref[...])
        normed = layer_norm(attended, entry(GAIN_ROW + 2)).astype(BF16)
        hidden = jax.nn.gelu(mm(normed, up_ref[...])).astype(BF16)
        backbone = attended + mm(hidden, down_ref[...])
        first, second = backbone[:PATCHES], backbone[PATCHES:]
        blended = jnp.concatenate(
            [mixing(l, 0) * first + mixing(l, 1) * second + embed(l) for l in range(LEV)], axis=0
        )
        normed = layer_norm(blended, entry(GAIN_ROW + 3)).astype(BF16)
        state[...] = (state[...] + mm(normed, dec_ref[...])).astype(BF16).astype(F32)

    for l in range(LEV):
        wide[:, l * PIN : (l + 1) * PIN] = state[l * PATCHES : (l + 1) * PATCHES, :]
    out_ref[0] = wide[...].reshape(out_ref.shape[1:]).astype(BF16)


def forecast(windows, arranged, held):
    vmem = pl.BlockSpec(memory_space=pltpu.VMEM)
    if windows == 1:
        block, grid = vmem, ()
    else:
        block = pl.BlockSpec((1,) + arranged.shape[1:], lambda i: (i, 0, 0, 0))
        grid = (windows,)
    return pl.pallas_call(
        functools.partial(forecast_kernel, windows),
        grid=grid,
        in_specs=[vmem] * len(held) + [block],
        out_specs=block,
        out_shape=jax.ShapeDtypeStruct(arranged.shape, BF16),
        scratch_shapes=[
            pltpu.VMEM((LEV * PATCHES, PIN), F32),
            pltpu.VMEM((PATCHES, LEV * PIN), F32),
        ],
        compiler_params=pltpu.CompilerParams(vmem_limit_bytes=24 * 1024 * 1024),
    )(*held, arranged)


def turn_kernel(step, direction, x_ref, out_ref, *token_ref):
    count = x_ref.shape[0] if len(x_ref.shape) == 3 else out_ref.shape[0]
    for ref in token_ref:
        ref[...] = jnp.zeros_like(ref)
    turned = lax.axis_index("lon") < step
    blocks = x_ref[...].astype(F32).reshape(count, 2, LEV * PIN)

    @pl.when(turned)
    def _():
        if direction > 0:
            moved = jnp.concatenate([blocks[1:], blocks[:1]], axis=0)
        else:
            moved = jnp.concatenate([blocks[-1:], blocks[:-1]], axis=0)
        out_ref[...] = moved.reshape(out_ref.shape).astype(BF16)

    @pl.when(jnp.logical_not(turned))
    def _():
        out_ref[...] = blocks.reshape(out_ref.shape).astype(BF16)


def turn(array, shape, step, direction, token=False):
    shapes = [jax.ShapeDtypeStruct(shape, BF16)]
    if token:
        shapes.append(jax.ShapeDtypeStruct((8, LANES), F32))
    return pl.pallas_call(
        functools.partial(turn_kernel, step, direction), out_shape=shapes
    )(array)


def shards(
    fields,
    level_ids,
    embed_weight,
    level_embed,
    enc_gain,
    latent_query,
    kv_weight,
    pool_out,
    attn_gain,
    qkv_weight,
    attn_proj,
    mlp_gain,
    mlp_up,
    mlp_down,
    level_mix,
    dec_gain,
    dec_weight,
):
    devices = lax.axis_size("lon")
    width = fields.shape[2]
    local_count = fields.shape[1]
    piece_cols = local_count // devices
    lat_count = devices // ROW_PARTS
    bands = lat_count // W_LAT
    cut = (W_LON // 2 // piece_cols) * lat_count
    scalars = (level_ids, level_mix.T)
    rows = (
        level_embed,
        latent_query,
        enc_gain.reshape(1, D),
        attn_gain.reshape(1, D),
        mlp_gain.reshape(1, D),
        dec_gain.reshape(1, D),
    )
    matrices = (
        dec_weight.T,
        embed_weight,
        kv_weight,
        pool_out,
        qkv_weight,
        attn_proj,
        mlp_up,
        mlp_down,
    )
    outgoing, token = turn(
        fields.reshape(local_count, width), (devices, piece_cols, width), cut, 1, token=True
    )
    held = load(token, scalars, rows, matrices)
    got = lax.all_to_all(outgoing, "lon", split_axis=0, concat_axis=0, tiled=True)
    if bands > 1:
        got = got.reshape(ROW_PARTS, lat_count, piece_cols, width)
        got = jnp.roll(got, -(W_LAT // 2), axis=1)
        got = got.reshape(ROW_PARTS, bands, W_LAT, piece_cols, width).transpose(1, 0, 2, 3, 4)
    done = forecast(bands, got.reshape(bands, ROW_PARTS * W_LAT, piece_cols, width), held)
    if bands > 1:
        done = done.reshape(bands, ROW_PARTS, W_LAT, piece_cols, width).transpose(1, 0, 2, 3, 4)
        done = done.reshape(ROW_PARTS, lat_count, piece_cols, width)
        done = jnp.roll(done, W_LAT // 2, axis=1)
    done = done.reshape(devices, piece_cols, width)
    home = lax.all_to_all(done, "lon", split_axis=0, concat_axis=0, tiled=True)
    (forecast_here,) = turn(home, (local_count, width), cut, -1)
    return forecast_here.reshape(fields.shape)


def solution(mesh):
    placed = (P(("groups", "lon"), None, None), P("groups")) + (P(),) * 15
    return jax.shard_map(
        shards,
        mesh=mesh,
        in_specs=placed,
        out_specs=P(("groups", "lon"), None, None),
        check_vma=False,
    )
```

```python
import functools

import jax
import jax.numpy as jnp
from jax import lax
from jax.experimental import pallas as pl
from jax.experimental.pallas import tpu as pltpu
from jax.sharding import PartitionSpec as P

D = 512
HEADS = 8
HEAD_DIM = D // HEADS
PIN = 500
LEV = 3
LATL = 2
W_LAT = 4
W_LON = 8
STEPS = 2
ROW_PARTS = 4
MLP = 2048
PATCHES = W_LAT * W_LON
TOKENS = PATCHES * LATL
HALF = D // 2
PAIR = 2 * HEAD_DIM
INPUTS = 15
LANES = 128
VMEM_LIMIT = 56 * 1024 * 1024
EMBED_ROW, MIX_ROW, LATENT_ROW, GAIN_ROW, TABLE_ROWS = 0, 3, 9, 11, 16

norm_eps = 1e-05
head_eps = 1e-06

F32 = jnp.float32
BF16 = jnp.bfloat16


def mm(a, b):
    return jnp.dot(a, b, preferred_element_type=F32)


def mm_t(a, b):
    return lax.dot_general(a, b, (((1,), (1,)), ((), ())), preferred_element_type=F32)


def layer_norm(values, gain):
    average = jnp.mean(values, axis=-1, keepdims=True)
    centred = values - average
    spread = jnp.mean(centred * centred, axis=-1, keepdims=True)
    return centred * lax.rsqrt(spread + norm_eps) * gain


def iota(shape, dim):
    return lax.broadcasted_iota(jnp.int32, shape, dim)


def load_kernel(*refs):
    (
        ids_from,
        mix_from,
        level_embed_from,
        latent_query_from,
        enc_gain_from,
        attn_gain_from,
        mlp_gain_from,
        dec_gain_from,
        dec_from,
        _,
        table_ref,
        query_ref,
        mean_ref,
        spread_ref,
        ones_ref,
        half_ref,
        allowed_ref,
        dec_ref,
        ids_ref,
        mix_ref,
        level_embed_ref,
        latent_query_ref,
        gain_refs,
        dec_rows_ref,
        arrivals,
    ) = refs
    pairs = [
        (ids_from, ids_ref),
        (mix_from, mix_ref),
        (level_embed_from, level_embed_ref),
        (latent_query_from, latent_query_ref),
        (enc_gain_from, gain_refs.at[0]),
        (attn_gain_from, gain_refs.at[1]),
        (mlp_gain_from, gain_refs.at[2]),
        (dec_gain_from, gain_refs.at[3]),
        (dec_from, dec_rows_ref),
    ]
    copies = [
        pltpu.make_async_copy(here, there, arrivals.at[i]) for i, (here, there) in enumerate(pairs)
    ]
    for copy in copies:
        copy.start()

    feature_head = iota((D, LANES), 0) // HEAD_DIM
    lane = iota((D, LANES), 1)
    on_head = (feature_head == lane % HEADS) & (lane < LATL * HEADS)
    mean_ref[...] = jnp.where(on_head, 1.0 / HEAD_DIM, 0.0).astype(BF16)
    spread_ref[...] = jnp.where(
        iota((LATL * HEADS, LATL * D), 0) == iota((LATL * HEADS, LATL * D), 1) // HEAD_DIM, 1.0, 0.0
    ).astype(BF16)
    ones_ref[...] = jnp.where(
        iota((HALF, HALF), 0) // HEAD_DIM == iota((HALF, HALF), 1) // HEAD_DIM, 1.0 / HEAD_DIM, 0.0
    ).astype(BF16)
    half_ref[...] = jnp.where(
        (iota((PAIR, PAIR), 0) < HEAD_DIM) == (iota((PAIR, PAIR), 1) < HEAD_DIM), 1.0, 0.0
    ).astype(BF16)
    row_bit = (iota((TOKENS, PAIR), 0) // 4) % 2
    lane_bit = (iota((TOKENS, PAIR), 1) // 4) % 2
    allowed_ref[...] = jnp.where(row_bit == lane_bit, 1.0, 0.0)

    for copy in copies[:8]:
        copy.wait()
    level_embed = level_embed_ref[...].astype(F32)
    for l in range(LEV):
        level = ids_ref[l]
        row = level_embed[LEV - 1 : LEV]
        for i in reversed(range(LEV - 1)):
            row = jnp.where(level == i, level_embed[i : i + 1], row)
        table_ref[EMBED_ROW + l : EMBED_ROW + l + 1, :] = row
        for j in range(LATL):
            at = MIX_ROW + l * LATL + j
            table_ref[at : at + 1, :] = jnp.full((1, D), mix_ref[j, level])
    latent = latent_query_ref[...].astype(F32)
    table_ref[LATENT_ROW : LATENT_ROW + LATL, :] = latent
    for i in range(4):
        table_ref[GAIN_ROW + i : GAIN_ROW + i + 1, :] = gain_refs[i]
    row_id = iota((LANES, D), 0)
    own_head = (row_id % HEADS) == iota((LANES, D), 1) // HEAD_DIM
    spots = jnp.zeros((LANES, D), F32)
    for j in range(LATL):
        mine = own_head & (row_id // HEADS == j)
        spots = jnp.where(mine, jnp.broadcast_to(latent[j : j + 1], (LANES, D)), spots)
    mean_square = jnp.sum(spots * spots, axis=-1, keepdims=True) / HEAD_DIM
    query_ref[...] = (spots * lax.rsqrt(mean_square + head_eps)).T.astype(BF16)

    copies[8].wait()
    dec_ref[...] = dec_rows_ref[...].astype(F32).T.astype(BF16)


def load(after, scalars, rows, dec):
    far = pl.BlockSpec(memory_space=pl.ANY)
    made = [
        jax.ShapeDtypeStruct((TABLE_ROWS, D), F32),
        jax.ShapeDtypeStruct((D, LANES), BF16),
        jax.ShapeDtypeStruct((D, LANES), BF16),
        jax.ShapeDtypeStruct((LATL * HEADS, LATL * D), BF16),
        jax.ShapeDtypeStruct((HALF, HALF), BF16),
        jax.ShapeDtypeStruct((PAIR, PAIR), BF16),
        jax.ShapeDtypeStruct((TOKENS, PAIR), F32),
        jax.ShapeDtypeStruct(dec.shape[::-1], BF16),
    ]
    inputs = (*scalars, *rows, dec)
    return pl.pallas_call(
        load_kernel,
        in_specs=[far] * (len(inputs) + 1),
        out_shape=made,
        scratch_shapes=[pltpu.SMEM(a.shape, a.dtype) for a in scalars]
        + [
            pltpu.VMEM((LEV, D), BF16),
            pltpu.VMEM((LATL, D), BF16),
            pltpu.VMEM((4, 1, D), F32),
            pltpu.VMEM(dec.shape, BF16),
            pltpu.SemaphoreType.DMA((len(inputs),)),
        ],
        compiler_params=pltpu.CompilerParams(vmem_limit_bytes=VMEM_LIMIT),
        cost_estimate=pl.CostEstimate(flops=0, bytes_accessed=4_000_000, transcendentals=0),
    )(*inputs, after)


def forecast_kernel(windows, *refs):
    far, (x_ref, out_ref), refs = refs[:INPUTS], refs[INPUTS : INPUTS + 2], refs[INPUTS + 2 :]
    near, (block_ref, state, wide, arrivals) = refs[:INPUTS], refs[INPUTS:]
    (
        table_ref,
        embed_ref,
        kv_ref,
        mean_ref,
        query_ref,
        spread_ref,
        pool_ref,
        qkv_ref,
        ones_ref,
        allowed_ref,
        half_ref,
        proj_ref,
        up_ref,
        down_ref,
        dec_ref,
    ) = near
    copies = [
        pltpu.make_async_copy(far[i], near[i], arrivals.at[i]) for i in range(INPUTS)
    ]
    fetch = pltpu.make_async_copy(x_ref.at[pl.program_id(0)], block_ref, arrivals.at[INPUTS])

    def in_first_window(action):
        if windows == 1:
            action()
        else:
            pl.when(pl.program_id(0) == 0)(action)

    def start(*wanted):
        def action():
            for i in wanted:
                copies[i].start()

        in_first_window(action)

    def wait(turn_index, *wanted):
        def action():
            for i in wanted:
                copies[i].wait()

        if turn_index == 0:
            in_first_window(action)

    fetch.start()
    start(0, 1, 2, 3, 4, 5)

    def entry(at):
        return table_ref[at : at + 1, :]

    def embed(l):
        return entry(EMBED_ROW + l)

    def mixing(l, j):
        return entry(MIX_ROW + l * LATL + j)

    low = iota((1, PAIR), 1) < HEAD_DIM

    fetch.wait()
    start(6, 7, 8, 9, 10)
    arrived = block_ref[...].astype(F32).reshape(PATCHES, LEV * PIN)
    for l in range(LEV):
        state[l * PATCHES : (l + 1) * PATCHES, :] = arrived[:, l * PIN : (l + 1) * PIN]

    def by_level(values):
        return [values[l * PATCHES : (l + 1) * PATCHES] for l in range(LEV)]

    for turn_index in range(STEPS):
        wait(turn_index, 0, 1)
        if turn_index == 0:
            start(11, 12, 13, 14)
        tokens = by_level(mm(state[...].astype(BF16), embed_ref[...]))
        tokens = jnp.concatenate([tokens[l] + embed(l) for l in range(LEV)], axis=0)
        tokens = layer_norm(tokens, entry(GAIN_ROW)).astype(BF16)
        wait(turn_index, 2)
        keyval = mm(tokens, kv_ref[...])
        keys = keyval[:, :D]
        values = by_level(keyval[:, D:])
        wait(turn_index, 3, 4, 5)
        mean_square = mm((keys * keys).astype(BF16), mean_ref[...])
        scores = mm(keys.astype(BF16), query_ref[...])
        scores = scores * lax.rsqrt(mean_square + head_eps) * HEAD_DIM ** (-0.5)
        scores = scores[:, : LATL * HEADS]
        parts = by_level(jnp.exp(scores))
        inverse = 1.0 / (parts[0] + parts[1] + parts[2])
        weights = jnp.concatenate([part * inverse for part in parts], axis=0).astype(BF16)
        wide_weights = by_level(mm(weights, spread_ref[...]))
        pooled = []
        for j in range(LATL):
            terms = [wide_weights[l][:, j * D : (j + 1) * D] * values[l] for l in range(LEV)]
            pooled.append(terms[0] + terms[1] + terms[2])
        wait(turn_index, 6)
        latents = mm(jnp.concatenate(pooled, axis=0).astype(BF16), pool_ref[...])
        latents = jnp.concatenate(
            [
                latents[j * PATCHES : (j + 1) * PATCHES] + entry(LATENT_ROW + j)
                for j in range(LATL)
            ],
            axis=0,
        )
        normed = layer_norm(latents, entry(GAIN_ROW + 1)).astype(BF16)
        wait(turn_index, 7)
        projected = mm(normed, qkv_ref[...])
        wait(turn_index, 8, 9, 10)
        allowed = allowed_ref[...]
        if windows > 1:
            cut = jnp.where(pl.program_id(0) == windows - 1, 1.0, 0.0)
            allowed = 1.0 - cut * (1.0 - allowed)
        halves = jnp.concatenate(
            [projected[:, i * HALF : (i + 1) * HALF] for i in range(4)], axis=0
        )
        mean_square = mm((halves * halves).astype(BF16), ones_ref[...])
        halves = halves * lax.rsqrt(mean_square + head_eps)
        win_values = projected[:, 2 * D :]
        mixed = []
        for pair in range(HEADS // 2):
            half, at = pair // 2, (pair % 2) * PAIR
            query = halves[half * TOKENS : (half + 1) * TOKENS, at : at + PAIR].astype(BF16)
            key = halves[(2 + half) * TOKENS : (3 + half) * TOKENS, at : at + PAIR]
            value = win_values[:, pair * PAIR : (pair + 1) * PAIR]
            key = jnp.concatenate(
                [jnp.where(low, key, 0.0), jnp.where(low, 0.0, key)], axis=0
            ).astype(BF16)
            value = jnp.concatenate(
                [jnp.where(low, value, 0.0), jnp.where(low, 0.0, value)], axis=0
            ).astype(BF16)
            weights = jnp.exp(mm_t(query, key) * HEAD_DIM ** (-0.5)) * allowed
            both = mm(weights.astype(BF16), jnp.concatenate([value, half_ref[...]], axis=1))
            mixed.append((both[:, :PAIR] / both[:, PAIR:]).astype(BF16))
        wait(turn_index, 11)
        attended = latents + mm(jnp.concatenate(mixed, axis=1), proj_ref[...])
        normed = layer_norm(attended, entry(GAIN_ROW + 2)).astype(BF16)
        wait(turn_index, 12)
        hidden = jax.nn.gelu(mm(normed, up_ref[...])).astype(BF16)
        wait(turn_index, 13)
        backbone = attended + mm(hidden, down_ref[...])
        wait(turn_index, 14)
        first, second = backbone[:PATCHES], backbone[PATCHES:]
        blended = jnp.concatenate(
            [mixing(l, 0) * first + mixing(l, 1) * second + embed(l) for l in range(LEV)], axis=0
        )
        normed = layer_norm(blended, entry(GAIN_ROW + 3)).astype(BF16)
        state[...] = (state[...] + mm(normed, dec_ref[...])).astype(BF16).astype(F32)

    for l in range(LEV):
        wide[:, l * PIN : (l + 1) * PIN] = state[l * PATCHES : (l + 1) * PATCHES, :]
    out_ref[0] = wide[...].reshape(out_ref.shape[1:]).astype(BF16)


def forecast(windows, arranged, inputs):
    shape = arranged.shape[1:]
    return pl.pallas_call(
        functools.partial(forecast_kernel, windows),
        grid=(windows,),
        in_specs=[pl.BlockSpec(memory_space=pl.ANY)] * (INPUTS + 1),
        out_specs=pl.BlockSpec((1,) + shape, lambda i: (i, 0, 0, 0)),
        out_shape=jax.ShapeDtypeStruct(arranged.shape, BF16),
        scratch_shapes=[pltpu.VMEM(a.shape, a.dtype) for a in inputs]
        + [
            pltpu.VMEM(shape, BF16),
            pltpu.VMEM((LEV * PATCHES, PIN), F32),
            pltpu.VMEM((PATCHES, LEV * PIN), F32),
            pltpu.SemaphoreType.DMA((INPUTS + 1,)),
        ],
        compiler_params=pltpu.CompilerParams(vmem_limit_bytes=VMEM_LIMIT),
    )(*inputs, arranged)


def turn_kernel(step, direction, x_ref, out_ref, *token_ref):
    count = x_ref.shape[0] if len(x_ref.shape) == 3 else out_ref.shape[0]
    for ref in token_ref:
        ref[...] = jnp.zeros_like(ref)
    turned = lax.axis_index("lon") < step
    blocks = x_ref[...].astype(F32).reshape(count, 2, LEV * PIN)

    @pl.when(turned)
    def _():
        if direction > 0:
            moved = jnp.concatenate([blocks[1:], blocks[:1]], axis=0)
        else:
            moved = jnp.concatenate([blocks[-1:], blocks[:-1]], axis=0)
        out_ref[...] = moved.reshape(out_ref.shape).astype(BF16)

    @pl.when(jnp.logical_not(turned))
    def _():
        out_ref[...] = blocks.reshape(out_ref.shape).astype(BF16)


def turn(array, shape, step, direction, token=False):
    shapes = [jax.ShapeDtypeStruct(shape, BF16)]
    if token:
        shapes.append(jax.ShapeDtypeStruct((8, LANES), F32))
    return pl.pallas_call(
        functools.partial(turn_kernel, step, direction), out_shape=shapes
    )(array)


def shards(
    fields,
    level_ids,
    embed_weight,
    level_embed,
    enc_gain,
    latent_query,
    kv_weight,
    pool_out,
    attn_gain,
    qkv_weight,
    attn_proj,
    mlp_gain,
    mlp_up,
    mlp_down,
    level_mix,
    dec_gain,
    dec_weight,
):
    devices = lax.axis_size("lon")
    width = fields.shape[2]
    local_count = fields.shape[1]
    piece_cols = local_count // devices
    lat_count = devices // ROW_PARTS
    bands = lat_count // W_LAT
    cut = (W_LON // 2 // piece_cols) * lat_count
    scalars = (level_ids, level_mix.T)
    rows = (
        level_embed,
        latent_query,
        enc_gain.reshape(1, D),
        attn_gain.reshape(1, D),
        mlp_gain.reshape(1, D),
        dec_gain.reshape(1, D),
    )
    outgoing, token = turn(
        fields.reshape(local_count, width), (devices, piece_cols, width), cut, 1, token=True
    )
    table, query, mean, spread, ones, half, allowed, dec = load(
        token, scalars, rows, dec_weight.T
    )
    inputs = (
        table,
        embed_weight,
        kv_weight,
        mean,
        query,
        spread,
        pool_out,
        qkv_weight,
        ones,
        allowed,
        half,
        attn_proj,
        mlp_up,
        mlp_down,
        dec,
    )
    got = lax.all_to_all(outgoing, "lon", split_axis=0, concat_axis=0, tiled=True)
    if bands > 1:
        got = got.reshape(ROW_PARTS, lat_count, piece_cols, width)
        got = jnp.roll(got, -(W_LAT // 2), axis=1)
        got = got.reshape(ROW_PARTS, bands, W_LAT, piece_cols, width).transpose(1, 0, 2, 3, 4)
    done = forecast(bands, got.reshape(bands, ROW_PARTS * W_LAT, piece_cols, width), inputs)
    if bands > 1:
        done = done.reshape(bands, ROW_PARTS, W_LAT, piece_cols, width).transpose(1, 0, 2, 3, 4)
        done = done.reshape(ROW_PARTS, lat_count, piece_cols, width)
        done = jnp.roll(done, W_LAT // 2, axis=1)
    done = done.reshape(devices, piece_cols, width)
    home = lax.all_to_all(done, "lon", split_axis=0, concat_axis=0, tiled=True)
    (forecast_here,) = turn(home, (local_count, width), cut, -1)
    return forecast_here.reshape(fields.shape)


def solution(mesh):
    placed = (P(("groups", "lon"), None, None), P("groups")) + (P(),) * 15
    return jax.shard_map(
        shards,
        mesh=mesh,
        in_specs=placed,
        out_specs=P(("groups", "lon"), None, None),
        check_vma=False,
    )
```

```python
import functools

import jax
import jax.numpy as jnp
from jax import lax
from jax.experimental import pallas as pl
from jax.experimental.pallas import tpu as pltpu
from jax.sharding import PartitionSpec as P

D = 512
HEADS = 8
HEAD_DIM = D // HEADS
PIN = 500
LEV = 3
LATL = 2
W_LAT = 4
W_LON = 8
STEPS = 2
ROW_PARTS = 4
MLP = 2048
PATCHES = W_LAT * W_LON
TOKENS = PATCHES * LATL
HALF = D // 2
PAIR = 2 * HEAD_DIM
EARLY, LATE = 11, 4
LANES = 128
LOAD_LIMIT = 56 * 1024 * 1024
MAIN_LIMIT = 56 * 1024 * 1024
EMBED_ROW, MIX_ROW, LATENT_ROW, GAIN_ROW, TABLE_ROWS = 0, 3, 9, 11, 16

norm_eps = 1e-05
head_eps = 1e-06

F32 = jnp.float32
BF16 = jnp.bfloat16


def mm(a, b):
    return jnp.dot(a, b, preferred_element_type=F32)


def mm_t(a, b):
    return lax.dot_general(a, b, (((1,), (1,)), ((), ())), preferred_element_type=F32)


def layer_norm(values, gain):
    average = jnp.mean(values, axis=-1, keepdims=True)
    centred = values - average
    spread = jnp.mean(centred * centred, axis=-1, keepdims=True)
    return centred * lax.rsqrt(spread + norm_eps) * gain


def iota(shape, dim):
    return lax.broadcasted_iota(jnp.int32, shape, dim)


def load_kernel(*refs):
    (
        ids_from,
        mix_from,
        level_embed_from,
        latent_query_from,
        enc_gain_from,
        attn_gain_from,
        mlp_gain_from,
        dec_gain_from,
        dec_from,
        embed_from,
        kv_from,
        pool_from,
        _,
        table_ref,
        query_ref,
        mean_ref,
        spread_ref,
        ones_ref,
        half_ref,
        allowed_ref,
        dec_ref,
        embed_ref,
        kv_ref,
        pool_ref,
        ids_ref,
        mix_ref,
        level_embed_ref,
        latent_query_ref,
        gain_refs,
        dec_rows_ref,
        arrivals,
    ) = refs
    pairs = [
        (ids_from, ids_ref),
        (mix_from, mix_ref),
        (level_embed_from, level_embed_ref),
        (latent_query_from, latent_query_ref),
        (enc_gain_from, gain_refs.at[0]),
        (attn_gain_from, gain_refs.at[1]),
        (mlp_gain_from, gain_refs.at[2]),
        (dec_gain_from, gain_refs.at[3]),
        (dec_from, dec_rows_ref),
        (embed_from, embed_ref),
        (kv_from, kv_ref),
        (pool_from, pool_ref),
    ]
    copies = [
        pltpu.make_async_copy(here, there, arrivals.at[i]) for i, (here, there) in enumerate(pairs)
    ]
    for copy in copies:
        copy.start()

    feature_head = iota((D, LANES), 0) // HEAD_DIM
    lane = iota((D, LANES), 1)
    on_head = (feature_head == lane % HEADS) & (lane < LATL * HEADS)
    mean_ref[...] = jnp.where(on_head, 1.0 / HEAD_DIM, 0.0).astype(BF16)
    spread_ref[...] = jnp.where(
        iota((LATL * HEADS, LATL * D), 0) == iota((LATL * HEADS, LATL * D), 1) // HEAD_DIM, 1.0, 0.0
    ).astype(BF16)
    ones_ref[...] = jnp.where(
        iota((HALF, HALF), 0) // HEAD_DIM == iota((HALF, HALF), 1) // HEAD_DIM, 1.0 / HEAD_DIM, 0.0
    ).astype(BF16)
    half_ref[...] = jnp.where(
        (iota((PAIR, PAIR), 0) < HEAD_DIM) == (iota((PAIR, PAIR), 1) < HEAD_DIM), 1.0, 0.0
    ).astype(BF16)
    row_bit = (iota((TOKENS, PAIR), 0) // 4) % 2
    lane_bit = (iota((TOKENS, PAIR), 1) // 4) % 2
    allowed_ref[...] = jnp.where(row_bit == lane_bit, 1.0, 0.0)

    for copy in copies[:8]:
        copy.wait()
    level_embed = level_embed_ref[...].astype(F32)
    for l in range(LEV):
        level = ids_ref[l]
        row = level_embed[LEV - 1 : LEV]
        for i in reversed(range(LEV - 1)):
            row = jnp.where(level == i, level_embed[i : i + 1], row)
        table_ref[EMBED_ROW + l : EMBED_ROW + l + 1, :] = row
        for j in range(LATL):
            at = MIX_ROW + l * LATL + j
            table_ref[at : at + 1, :] = jnp.full((1, D), mix_ref[j, level])
    latent = latent_query_ref[...].astype(F32)
    table_ref[LATENT_ROW : LATENT_ROW + LATL, :] = latent
    for i in range(4):
        table_ref[GAIN_ROW + i : GAIN_ROW + i + 1, :] = gain_refs[i]
    row_id = iota((LANES, D), 0)
    own_head = (row_id % HEADS) == iota((LANES, D), 1) // HEAD_DIM
    spots = jnp.zeros((LANES, D), F32)
    for j in range(LATL):
        mine = own_head & (row_id // HEADS == j)
        spots = jnp.where(mine, jnp.broadcast_to(latent[j : j + 1], (LANES, D)), spots)
    mean_square = jnp.sum(spots * spots, axis=-1, keepdims=True) / HEAD_DIM
    query_ref[...] = (spots * lax.rsqrt(mean_square + head_eps)).T.astype(BF16)

    copies[8].wait()
    dec_ref[...] = dec_rows_ref[...].astype(F32).T.astype(BF16)
    for copy in copies[9:]:
        copy.wait()


def load(after, scalars, rows, dec, early):
    far = pl.BlockSpec(memory_space=pl.ANY)
    made = [
        pltpu.VMEM((TABLE_ROWS, D), F32),
        pltpu.VMEM((D, LANES), BF16),
        pltpu.VMEM((D, LANES), BF16),
        pltpu.VMEM((LATL * HEADS, LATL * D), BF16),
        pltpu.VMEM((HALF, HALF), BF16),
        pltpu.VMEM((PAIR, PAIR), BF16),
        pltpu.VMEM((TOKENS, PAIR), F32),
        pltpu.VMEM(dec.shape[::-1], BF16),
    ] + [pltpu.VMEM(a.shape, a.dtype) for a in early]
    inputs = (*scalars, *rows, dec, *early)
    return pl.pallas_call(
        load_kernel,
        in_specs=[far] * (len(inputs) + 1),
        out_specs=[pl.BlockSpec(memory_space=pltpu.VMEM)] * len(made),
        out_shape=made,
        scratch_shapes=[pltpu.SMEM(a.shape, a.dtype) for a in scalars]
        + [
            pltpu.VMEM((LEV, D), BF16),
            pltpu.VMEM((LATL, D), BF16),
            pltpu.VMEM((4, 1, D), F32),
            pltpu.VMEM(dec.shape, BF16),
            pltpu.SemaphoreType.DMA((len(inputs),)),
        ],
        compiler_params=pltpu.CompilerParams(vmem_limit_bytes=LOAD_LIMIT),
        cost_estimate=pl.CostEstimate(flops=0, bytes_accessed=8_000_000, transcendentals=0),
    )(*inputs, after)


def forecast_kernel(windows, *refs):
    (
        table_ref,
        query_ref,
        mean_ref,
        spread_ref,
        ones_ref,
        half_ref,
        allowed_ref,
        dec_ref,
        embed_ref,
        kv_ref,
        pool_ref,
    ) = refs[:EARLY]
    far, (x_ref, out_ref), refs = refs[EARLY:][:LATE], refs[EARLY + LATE :][:2], refs[EARLY + LATE + 2 :]
    near, (state, wide, arrivals) = refs[:LATE], refs[LATE:]
    qkv_ref, proj_ref, up_ref, down_ref = near
    copies = [
        pltpu.make_async_copy(far[i], near[i], arrivals.at[i]) for i in range(LATE)
    ]

    def in_first_window(action):
        if windows == 1:
            action()
        else:
            pl.when(pl.program_id(0) == 0)(action)

    def start(*wanted):
        def action():
            for i in wanted:
                copies[i].start()

        in_first_window(action)

    def wait(turn_index, *wanted):
        def action():
            for i in wanted:
                copies[i].wait()

        if turn_index == 0:
            in_first_window(action)

    start(0, 1, 2, 3)

    def entry(at):
        return table_ref[at : at + 1, :]

    def embed(l):
        return entry(EMBED_ROW + l)

    def mixing(l, j):
        return entry(MIX_ROW + l * LATL + j)

    low = iota((1, PAIR), 1) < HEAD_DIM

    arrived = x_ref[0].astype(F32).reshape(PATCHES, LEV * PIN)
    for l in range(LEV):
        state[l * PATCHES : (l + 1) * PATCHES, :] = arrived[:, l * PIN : (l + 1) * PIN]

    def by_level(values):
        return [values[l * PATCHES : (l + 1) * PATCHES] for l in range(LEV)]

    for turn_index in range(STEPS):
        tokens = by_level(mm(state[...].astype(BF16), embed_ref[...]))
        tokens = jnp.concatenate([tokens[l] + embed(l) for l in range(LEV)], axis=0)
        tokens = layer_norm(tokens, entry(GAIN_ROW)).astype(BF16)
        keyval = mm(tokens, kv_ref[...])
        keys = keyval[:, :D]
        values = by_level(keyval[:, D:])
        mean_square = mm((keys * keys).astype(BF16), mean_ref[...])
        scores = mm(keys.astype(BF16), query_ref[...])
        scores = scores * lax.rsqrt(mean_square + head_eps) * HEAD_DIM ** (-0.5)
        scores = scores[:, : LATL * HEADS]
        parts = by_level(jnp.exp(scores))
        inverse = 1.0 / (parts[0] + parts[1] + parts[2])
        weights = jnp.concatenate([part * inverse for part in parts], axis=0).astype(BF16)
        wide_weights = by_level(mm(weights, spread_ref[...]))
        pooled = []
        for j in range(LATL):
            terms = [wide_weights[l][:, j * D : (j + 1) * D] * values[l] for l in range(LEV)]
            pooled.append(terms[0] + terms[1] + terms[2])
        latents = mm(jnp.concatenate(pooled, axis=0).astype(BF16), pool_ref[...])
        latents = jnp.concatenate(
            [
                latents[j * PATCHES : (j + 1) * PATCHES] + entry(LATENT_ROW + j)
                for j in range(LATL)
            ],
            axis=0,
        )
        normed = layer_norm(latents, entry(GAIN_ROW + 1)).astype(BF16)
        wait(turn_index, 0)
        projected = mm(normed, qkv_ref[...])
        allowed = allowed_ref[...]
        if windows > 1:
            cut = jnp.where(pl.program_id(0) == windows - 1, 1.0, 0.0)
            allowed = 1.0 - cut * (1.0 - allowed)
        halves = jnp.concatenate(
            [projected[:, i * HALF : (i + 1) * HALF] for i in range(4)], axis=0
        )
        mean_square = mm((halves * halves).astype(BF16), ones_ref[...])
        halves = halves * lax.rsqrt(mean_square + head_eps)
        win_values = projected[:, 2 * D :]
        mixed = []
        for pair in range(HEADS // 2):
            half, at = pair // 2, (pair % 2) * PAIR
            query = halves[half * TOKENS : (half + 1) * TOKENS, at : at + PAIR].astype(BF16)
            key = halves[(2 + half) * TOKENS : (3 + half) * TOKENS, at : at + PAIR]
            value = win_values[:, pair * PAIR : (pair + 1) * PAIR]
            key = jnp.concatenate(
                [jnp.where(low, key, 0.0), jnp.where(low, 0.0, key)], axis=0
            ).astype(BF16)
            value = jnp.concatenate(
                [jnp.where(low, value, 0.0), jnp.where(low, 0.0, value)], axis=0
            ).astype(BF16)
            weights = jnp.exp(mm_t(query, key) * HEAD_DIM ** (-0.5)) * allowed
            both = mm(weights.astype(BF16), jnp.concatenate([value, half_ref[...]], axis=1))
            mixed.append((both[:, :PAIR] / both[:, PAIR:]).astype(BF16))
        wait(turn_index, 1)
        attended = latents + mm(jnp.concatenate(mixed, axis=1), proj_ref[...])
        normed = layer_norm(attended, entry(GAIN_ROW + 2)).astype(BF16)
        wait(turn_index, 2)
        hidden = jax.nn.gelu(mm(normed, up_ref[...])).astype(BF16)
        wait(turn_index, 3)
        backbone = attended + mm(hidden, down_ref[...])
        first, second = backbone[:PATCHES], backbone[PATCHES:]
        blended = jnp.concatenate(
            [mixing(l, 0) * first + mixing(l, 1) * second + embed(l) for l in range(LEV)], axis=0
        )
        normed = layer_norm(blended, entry(GAIN_ROW + 3)).astype(BF16)
        state[...] = (state[...] + mm(normed, dec_ref[...])).astype(BF16).astype(F32)

    for l in range(LEV):
        wide[:, l * PIN : (l + 1) * PIN] = state[l * PATCHES : (l + 1) * PATCHES, :]
    out_ref[0] = wide[...].reshape(out_ref.shape[1:]).astype(BF16)


def forecast(windows, arranged, early, late):
    vmem = pl.BlockSpec(memory_space=pltpu.VMEM)
    if windows == 1:
        block, grid = vmem, ()
    else:
        block = pl.BlockSpec((1,) + arranged.shape[1:], lambda i: (i, 0, 0, 0))
        grid = (windows,)
    early = [pltpu.with_memory_space_constraint(a, pltpu.VMEM) for a in early]
    return pl.pallas_call(
        functools.partial(forecast_kernel, windows),
        grid=grid,
        in_specs=[vmem] * EARLY + [pl.BlockSpec(memory_space=pl.ANY)] * LATE + [block],
        out_specs=block,
        out_shape=jax.ShapeDtypeStruct(arranged.shape, BF16),
        scratch_shapes=[pltpu.VMEM(a.shape, a.dtype) for a in late]
        + [
            pltpu.VMEM((LEV * PATCHES, PIN), F32),
            pltpu.VMEM((PATCHES, LEV * PIN), F32),
            pltpu.SemaphoreType.DMA((LATE,)),
        ],
        compiler_params=pltpu.CompilerParams(vmem_limit_bytes=MAIN_LIMIT),
    )(*early, *late, arranged)


def turn_kernel(step, direction, x_ref, out_ref, *token_ref):
    count = x_ref.shape[0] if len(x_ref.shape) == 3 else out_ref.shape[0]
    for ref in token_ref:
        ref[...] = jnp.zeros_like(ref)
    turned = lax.axis_index("lon") < step
    blocks = x_ref[...].astype(F32).reshape(count, 2, LEV * PIN)

    @pl.when(turned)
    def _():
        if direction > 0:
            moved = jnp.concatenate([blocks[1:], blocks[:1]], axis=0)
        else:
            moved = jnp.concatenate([blocks[-1:], blocks[:-1]], axis=0)
        out_ref[...] = moved.reshape(out_ref.shape).astype(BF16)

    @pl.when(jnp.logical_not(turned))
    def _():
        out_ref[...] = blocks.reshape(out_ref.shape).astype(BF16)


def turn(array, shape, step, direction, token=False):
    shapes = [jax.ShapeDtypeStruct(shape, BF16)]
    if token:
        shapes.append(jax.ShapeDtypeStruct((8, LANES), F32))
    return pl.pallas_call(
        functools.partial(turn_kernel, step, direction), out_shape=shapes
    )(array)


def shards(
    fields,
    level_ids,
    embed_weight,
    level_embed,
    enc_gain,
    latent_query,
    kv_weight,
    pool_out,
    attn_gain,
    qkv_weight,
    attn_proj,
    mlp_gain,
    mlp_up,
    mlp_down,
    level_mix,
    dec_gain,
    dec_weight,
):
    devices = lax.axis_size("lon")
    width = fields.shape[2]
    local_count = fields.shape[1]
    piece_cols = local_count // devices
    lat_count = devices // ROW_PARTS
    bands = lat_count // W_LAT
    cut = (W_LON // 2 // piece_cols) * lat_count
    scalars = (level_ids, level_mix.T)
    rows = (
        level_embed,
        latent_query,
        enc_gain.reshape(1, D),
        attn_gain.reshape(1, D),
        mlp_gain.reshape(1, D),
        dec_gain.reshape(1, D),
    )
    outgoing, token = turn(
        fields.reshape(local_count, width), (devices, piece_cols, width), cut, 1, token=True
    )
    early = load(token, scalars, rows, dec_weight.T, (embed_weight, kv_weight, pool_out))
    late = (qkv_weight, attn_proj, mlp_up, mlp_down)
    got = lax.all_to_all(outgoing, "lon", split_axis=0, concat_axis=0, tiled=True)
    if bands > 1:
        got = got.reshape(ROW_PARTS, lat_count, piece_cols, width)
        got = jnp.roll(got, -(W_LAT // 2), axis=1)
        got = got.reshape(ROW_PARTS, bands, W_LAT, piece_cols, width).transpose(1, 0, 2, 3, 4)
    done = forecast(bands, got.reshape(bands, ROW_PARTS * W_LAT, piece_cols, width), early, late)
    if bands > 1:
        done = done.reshape(bands, ROW_PARTS, W_LAT, piece_cols, width).transpose(1, 0, 2, 3, 4)
        done = done.reshape(ROW_PARTS, lat_count, piece_cols, width)
        done = jnp.roll(done, W_LAT // 2, axis=1)
    done = done.reshape(devices, piece_cols, width)
    home = lax.all_to_all(done, "lon", split_axis=0, concat_axis=0, tiled=True)
    (forecast_here,) = turn(home, (local_count, width), cut, -1)
    return forecast_here.reshape(fields.shape)


def solution(mesh):
    placed = (P(("groups", "lon"), None, None), P("groups")) + (P(),) * 15
    return jax.shard_map(
        shards,
        mesh=mesh,
        in_specs=placed,
        out_specs=P(("groups", "lon"), None, None),
        check_vma=False,
    )
```

```python
import functools

import jax
import jax.numpy as jnp
from jax import lax
from jax.experimental import pallas as pl
from jax.experimental.pallas import tpu as pltpu
from jax.sharding import PartitionSpec as P

D = 512
HEADS = 8
HEAD_DIM = D // HEADS
PIN = 500
LEV = 3
LATL = 2
W_LAT = 4
W_LON = 8
STEPS = 2
ROW_PARTS = 4
MLP = 2048
PATCHES = W_LAT * W_LON
TOKENS = PATCHES * LATL
HALF = D // 2
PAIR = 2 * HEAD_DIM
EARLY, LATE = 11, 4
LANES = 128
LOAD_LIMIT = 56 * 1024 * 1024
MAIN_LIMIT = 56 * 1024 * 1024
EMBED_ROW, MIX_ROW, LATENT_ROW, GAIN_ROW, TABLE_ROWS = 0, 3, 9, 11, 16

norm_eps = 1e-05
head_eps = 1e-06

F32 = jnp.float32
BF16 = jnp.bfloat16


def mm(a, b):
    return jnp.dot(a, b, preferred_element_type=F32)


def mm_t(a, b):
    return lax.dot_general(a, b, (((1,), (1,)), ((), ())), preferred_element_type=F32)


def layer_norm(values, gain):
    average = jnp.mean(values, axis=-1, keepdims=True)
    centred = values - average
    spread = jnp.mean(centred * centred, axis=-1, keepdims=True)
    return centred * lax.rsqrt(spread + norm_eps) * gain


def iota(shape, dim):
    return lax.broadcasted_iota(jnp.int32, shape, dim)


def load_kernel(*refs):
    (
        ids_from,
        mix_from,
        level_embed_from,
        latent_query_from,
        enc_gain_from,
        attn_gain_from,
        mlp_gain_from,
        dec_gain_from,
        dec_from,
        embed_from,
        kv_from,
        pool_from,
        _,
        table_ref,
        query_ref,
        mean_ref,
        spread_ref,
        ones_ref,
        half_ref,
        allowed_ref,
        dec_ref,
        embed_ref,
        kv_ref,
        pool_ref,
        ids_ref,
        mix_ref,
        level_embed_ref,
        latent_query_ref,
        gain_refs,
        dec_rows_ref,
        arrivals,
    ) = refs
    pairs = [
        (ids_from, ids_ref),
        (mix_from, mix_ref),
        (level_embed_from, level_embed_ref),
        (latent_query_from, latent_query_ref),
        (enc_gain_from, gain_refs.at[0]),
        (attn_gain_from, gain_refs.at[1]),
        (mlp_gain_from, gain_refs.at[2]),
        (dec_gain_from, gain_refs.at[3]),
        (dec_from, dec_rows_ref),
        (embed_from, embed_ref),
        (kv_from, kv_ref),
        (pool_from, pool_ref),
    ]
    copies = [
        pltpu.make_async_copy(here, there, arrivals.at[i]) for i, (here, there) in enumerate(pairs)
    ]
    for copy in copies:
        copy.start()

    feature_head = iota((D, LANES), 0) // HEAD_DIM
    lane = iota((D, LANES), 1)
    on_head = (feature_head == lane % HEADS) & (lane < LATL * HEADS)
    mean_ref[...] = jnp.where(on_head, 1.0 / HEAD_DIM, 0.0).astype(BF16)
    spread_ref[...] = jnp.where(
        iota((LATL * HEADS, LATL * D), 0) == iota((LATL * HEADS, LATL * D), 1) // HEAD_DIM, 1.0, 0.0
    ).astype(BF16)
    ones_ref[...] = jnp.where(
        iota((HALF, HALF), 0) // HEAD_DIM == iota((HALF, HALF), 1) // HEAD_DIM, 1.0 / HEAD_DIM, 0.0
    ).astype(BF16)
    half_ref[...] = jnp.where(
        (iota((PAIR, PAIR), 0) < HEAD_DIM) == (iota((PAIR, PAIR), 1) < HEAD_DIM), 1.0, 0.0
    ).astype(BF16)
    row_bit = (iota((TOKENS, PAIR), 0) // 4) % 2
    lane_bit = (iota((TOKENS, PAIR), 1) // 4) % 2
    allowed_ref[...] = jnp.where(row_bit == lane_bit, 1.0, 0.0)

    for copy in copies[:8]:
        copy.wait()
    level_embed = level_embed_ref[...].astype(F32)
    for l in range(LEV):
        level = ids_ref[l]
        row = level_embed[LEV - 1 : LEV]
        for i in reversed(range(LEV - 1)):
            row = jnp.where(level == i, level_embed[i : i + 1], row)
        table_ref[EMBED_ROW + l : EMBED_ROW + l + 1, :] = row
        for j in range(LATL):
            at = MIX_ROW + l * LATL + j
            table_ref[at : at + 1, :] = jnp.full((1, D), mix_ref[j, level])
    latent = latent_query_ref[...].astype(F32)
    table_ref[LATENT_ROW : LATENT_ROW + LATL, :] = latent
    for i in range(4):
        table_ref[GAIN_ROW + i : GAIN_ROW + i + 1, :] = gain_refs[i]
    row_id = iota((LANES, D), 0)
    own_head = (row_id % HEADS) == iota((LANES, D), 1) // HEAD_DIM
    spots = jnp.zeros((LANES, D), F32)
    for j in range(LATL):
        mine = own_head & (row_id // HEADS == j)
        spots = jnp.where(mine, jnp.broadcast_to(latent[j : j + 1], (LANES, D)), spots)
    mean_square = jnp.sum(spots * spots, axis=-1, keepdims=True) / HEAD_DIM
    query_ref[...] = (spots * lax.rsqrt(mean_square + head_eps)).T.astype(BF16)

    copies[8].wait()
    dec_ref[...] = dec_rows_ref[...].astype(F32).T.astype(BF16)
    for copy in copies[9:]:
        copy.wait()


def load(after, scalars, rows, dec, early):
    far = pl.BlockSpec(memory_space=pl.ANY)
    made = [
        pltpu.VMEM((TABLE_ROWS, D), F32),
        pltpu.VMEM((D, LANES), BF16),
        pltpu.VMEM((D, LANES), BF16),
        pltpu.VMEM((LATL * HEADS, LATL * D), BF16),
        pltpu.VMEM((HALF, HALF), BF16),
        pltpu.VMEM((PAIR, PAIR), BF16),
        pltpu.VMEM((TOKENS, PAIR), F32),
        pltpu.VMEM(dec.shape[::-1], BF16),
    ] + [pltpu.VMEM(a.shape, a.dtype) for a in early]
    inputs = (*scalars, *rows, dec, *early)
    return pl.pallas_call(
        load_kernel,
        in_specs=[far] * (len(inputs) + 1),
        out_specs=[pl.BlockSpec(memory_space=pltpu.VMEM)] * len(made),
        out_shape=made,
        scratch_shapes=[pltpu.SMEM(a.shape, a.dtype) for a in scalars]
        + [
            pltpu.VMEM((LEV, D), BF16),
            pltpu.VMEM((LATL, D), BF16),
            pltpu.VMEM((4, 1, D), F32),
            pltpu.VMEM(dec.shape, BF16),
            pltpu.SemaphoreType.DMA((len(inputs),)),
        ],
        compiler_params=pltpu.CompilerParams(vmem_limit_bytes=LOAD_LIMIT),
        cost_estimate=pl.CostEstimate(flops=0, bytes_accessed=8_000_000, transcendentals=0),
    )(*inputs, after)


def forecast_kernel(windows, *refs):
    (
        table_ref,
        query_ref,
        mean_ref,
        spread_ref,
        ones_ref,
        half_ref,
        allowed_ref,
        dec_ref,
        embed_ref,
        kv_ref,
        pool_ref,
    ) = refs[:EARLY]
    far, (x_ref, out_ref), refs = refs[EARLY:][:LATE], refs[EARLY + LATE :][:2], refs[EARLY + LATE + 2 :]
    near, (state, wide, arrivals) = refs[:LATE], refs[LATE:]
    qkv_ref, proj_ref, up_ref, down_ref = near
    copies = [
        pltpu.make_async_copy(far[i], near[i], arrivals.at[i]) for i in range(LATE)
    ]

    def in_first_window(action):
        if windows == 1:
            action()
        else:
            pl.when(pl.program_id(0) == 0)(action)

    def start(*wanted):
        def action():
            for i in wanted:
                copies[i].start()

        in_first_window(action)

    def wait(turn_index, *wanted):
        def action():
            for i in wanted:
                copies[i].wait()

        if turn_index == 0:
            in_first_window(action)

    start(0, 1, 2, 3)

    def entry(at):
        return table_ref[at : at + 1, :]

    def embed(l):
        return entry(EMBED_ROW + l)

    def mixing(l, j):
        return entry(MIX_ROW + l * LATL + j)

    low = iota((1, PAIR), 1) < HEAD_DIM

    arrived = x_ref[0].astype(F32).reshape(PATCHES, LEV * PIN)
    for l in range(LEV):
        state[l * PATCHES : (l + 1) * PATCHES, :] = arrived[:, l * PIN : (l + 1) * PIN]

    def by_level(values):
        return [values[l * PATCHES : (l + 1) * PATCHES] for l in range(LEV)]

    for turn_index in range(STEPS):
        tokens = by_level(mm(state[...].astype(BF16), embed_ref[...]))
        tokens = jnp.concatenate([tokens[l] + embed(l) for l in range(LEV)], axis=0)
        tokens = layer_norm(tokens, entry(GAIN_ROW)).astype(BF16)
        keyval = mm(tokens, kv_ref[...])
        keys = keyval[:, :D]
        values = by_level(keyval[:, D:])
        mean_square = mm((keys * keys).astype(BF16), mean_ref[...])
        scores = mm(keys.astype(BF16), query_ref[...])
        scores = scores * lax.rsqrt(mean_square + head_eps) * HEAD_DIM ** (-0.5)
        scores = scores[:, : LATL * HEADS]
        parts = by_level(jnp.exp(scores))
        inverse = 1.0 / (parts[0] + parts[1] + parts[2])
        weights = jnp.concatenate([part * inverse for part in parts], axis=0).astype(BF16)
        wide_weights = by_level(mm(weights, spread_ref[...]))
        pooled = []
        for j in range(LATL):
            terms = [wide_weights[l][:, j * D : (j + 1) * D] * values[l] for l in range(LEV)]
            pooled.append(terms[0] + terms[1] + terms[2])
        latents = mm(jnp.concatenate(pooled, axis=0).astype(BF16), pool_ref[...])
        latents = jnp.concatenate(
            [
                latents[j * PATCHES : (j + 1) * PATCHES] + entry(LATENT_ROW + j)
                for j in range(LATL)
            ],
            axis=0,
        )
        normed = layer_norm(latents, entry(GAIN_ROW + 1)).astype(BF16)
        wait(turn_index, 0)
        projected = mm(normed, qkv_ref[...])
        allowed = allowed_ref[...]
        if windows > 1:
            cut = jnp.where(pl.program_id(0) == windows - 1, 1.0, 0.0)
            allowed = 1.0 - cut * (1.0 - allowed)
        halves = jnp.concatenate(
            [projected[:, i * HALF : (i + 1) * HALF] for i in range(4)], axis=0
        )
        mean_square = mm((halves * halves).astype(BF16), ones_ref[...])
        halves = halves * lax.rsqrt(mean_square + head_eps)
        win_values = projected[:, 2 * D :]
        mixed = []
        for pair in range(HEADS // 2):
            half, at = pair // 2, (pair % 2) * PAIR
            query = halves[half * TOKENS : (half + 1) * TOKENS, at : at + PAIR].astype(BF16)
            key = halves[(2 + half) * TOKENS : (3 + half) * TOKENS, at : at + PAIR]
            value = win_values[:, pair * PAIR : (pair + 1) * PAIR]
            key = jnp.concatenate(
                [jnp.where(low, key, 0.0), jnp.where(low, 0.0, key)], axis=0
            ).astype(BF16)
            value = jnp.concatenate(
                [jnp.where(low, value, 0.0), jnp.where(low, 0.0, value)], axis=0
            ).astype(BF16)
            weights = jnp.exp(mm_t(query, key) * HEAD_DIM ** (-0.5)) * allowed
            both = mm(weights.astype(BF16), jnp.concatenate([value, half_ref[...]], axis=1))
            mixed.append((both[:, :PAIR] / both[:, PAIR:]).astype(BF16))
        wait(turn_index, 1)
        attended = latents + mm(jnp.concatenate(mixed, axis=1), proj_ref[...])
        normed = layer_norm(attended, entry(GAIN_ROW + 2)).astype(BF16)
        wait(turn_index, 2)
        hidden = jax.nn.gelu(mm(normed, up_ref[...])).astype(BF16)
        wait(turn_index, 3)
        backbone = attended + mm(hidden, down_ref[...])
        first, second = backbone[:PATCHES], backbone[PATCHES:]
        blended = jnp.concatenate(
            [mixing(l, 0) * first + mixing(l, 1) * second + embed(l) for l in range(LEV)], axis=0
        )
        normed = layer_norm(blended, entry(GAIN_ROW + 3)).astype(BF16)
        state[...] = (state[...] + mm(normed, dec_ref[...])).astype(BF16).astype(F32)

    for l in range(LEV):
        wide[:, l * PIN : (l + 1) * PIN] = state[l * PATCHES : (l + 1) * PATCHES, :]
    out_ref[0] = wide[...].reshape(out_ref.shape[1:]).astype(BF16)


def forecast(windows, arranged, early, late):
    vmem = pl.BlockSpec(memory_space=pltpu.VMEM)
    if windows == 1:
        block, grid = vmem, ()
        result = pltpu.VMEM(arranged.shape, BF16)
        arranged = pltpu.with_memory_space_constraint(arranged, pltpu.VMEM)
    else:
        result = jax.ShapeDtypeStruct(arranged.shape, BF16)
        block = pl.BlockSpec((1,) + arranged.shape[1:], lambda i: (i, 0, 0, 0))
        grid = (windows,)
    early = [pltpu.with_memory_space_constraint(a, pltpu.VMEM) for a in early]
    return pl.pallas_call(
        functools.partial(forecast_kernel, windows),
        grid=grid,
        in_specs=[vmem] * EARLY + [pl.BlockSpec(memory_space=pl.ANY)] * LATE + [block],
        out_specs=block,
        out_shape=result,
        scratch_shapes=[pltpu.VMEM(a.shape, a.dtype) for a in late]
        + [
            pltpu.VMEM((LEV * PATCHES, PIN), F32),
            pltpu.VMEM((PATCHES, LEV * PIN), F32),
            pltpu.SemaphoreType.DMA((LATE,)),
        ],
        compiler_params=pltpu.CompilerParams(vmem_limit_bytes=MAIN_LIMIT),
    )(*early, *late, arranged)


def turn_kernel(step, direction, x_ref, out_ref, *token_ref):
    count = x_ref.shape[0] if len(x_ref.shape) == 3 else out_ref.shape[0]
    for ref in token_ref:
        ref[...] = jnp.zeros_like(ref)
    turned = lax.axis_index("lon") < step
    blocks = x_ref[...].astype(F32).reshape(count, 2, LEV * PIN)

    @pl.when(turned)
    def _():
        if direction > 0:
            moved = jnp.concatenate([blocks[1:], blocks[:1]], axis=0)
        else:
            moved = jnp.concatenate([blocks[-1:], blocks[:-1]], axis=0)
        out_ref[...] = moved.reshape(out_ref.shape).astype(BF16)

    @pl.when(jnp.logical_not(turned))
    def _():
        out_ref[...] = blocks.reshape(out_ref.shape).astype(BF16)


def turn(array, shape, step, direction, token=False):
    shapes = [jax.ShapeDtypeStruct(shape, BF16)]
    if token:
        shapes.append(jax.ShapeDtypeStruct((8, LANES), F32))
    return pl.pallas_call(
        functools.partial(turn_kernel, step, direction), out_shape=shapes
    )(array)


def shards(
    fields,
    level_ids,
    embed_weight,
    level_embed,
    enc_gain,
    latent_query,
    kv_weight,
    pool_out,
    attn_gain,
    qkv_weight,
    attn_proj,
    mlp_gain,
    mlp_up,
    mlp_down,
    level_mix,
    dec_gain,
    dec_weight,
):
    devices = lax.axis_size("lon")
    width = fields.shape[2]
    local_count = fields.shape[1]
    piece_cols = local_count // devices
    lat_count = devices // ROW_PARTS
    bands = lat_count // W_LAT
    cut = (W_LON // 2 // piece_cols) * lat_count
    scalars = (level_ids, level_mix.T)
    rows = (
        level_embed,
        latent_query,
        enc_gain.reshape(1, D),
        attn_gain.reshape(1, D),
        mlp_gain.reshape(1, D),
        dec_gain.reshape(1, D),
    )
    outgoing, token = turn(
        fields.reshape(local_count, width), (devices, piece_cols, width), cut, 1, token=True
    )
    early = load(token, scalars, rows, dec_weight.T, (embed_weight, kv_weight, pool_out))
    late = (qkv_weight, attn_proj, mlp_up, mlp_down)
    got = lax.all_to_all(outgoing, "lon", split_axis=0, concat_axis=0, tiled=True)
    if bands > 1:
        got = got.reshape(ROW_PARTS, lat_count, piece_cols, width)
        got = jnp.roll(got, -(W_LAT // 2), axis=1)
        got = got.reshape(ROW_PARTS, bands, W_LAT, piece_cols, width).transpose(1, 0, 2, 3, 4)
    done = forecast(bands, got.reshape(bands, ROW_PARTS * W_LAT, piece_cols, width), early, late)
    if bands > 1:
        done = done.reshape(bands, ROW_PARTS, W_LAT, piece_cols, width).transpose(1, 0, 2, 3, 4)
        done = done.reshape(ROW_PARTS, lat_count, piece_cols, width)
        done = jnp.roll(done, W_LAT // 2, axis=1)
    done = done.reshape(devices, piece_cols, width)
    home = lax.all_to_all(done, "lon", split_axis=0, concat_axis=0, tiled=True)
    (forecast_here,) = turn(home, (local_count, width), cut, -1)
    return forecast_here.reshape(fields.shape)


def solution(mesh):
    placed = (P(("groups", "lon"), None, None), P("groups")) + (P(),) * 15
    return jax.shard_map(
        shards,
        mesh=mesh,
        in_specs=placed,
        out_specs=P(("groups", "lon"), None, None),
        check_vma=False,
    )
```

```python
import functools

import jax
import jax.numpy as jnp
from jax import lax
from jax.experimental import pallas as pl
from jax.experimental.pallas import tpu as pltpu
from jax.sharding import PartitionSpec as P

D = 512
HEADS = 8
HEAD_DIM = D // HEADS
PIN = 500
LEV = 3
LATL = 2
W_LAT = 4
W_LON = 8
STEPS = 2
ROW_PARTS = 4
MLP = 2048
PATCHES = W_LAT * W_LON
TOKENS = PATCHES * LATL
HALF = D // 2
PAIR = 2 * HEAD_DIM
EARLY, LATE = 11, 4
LANES = 128
LOAD_LIMIT = 56 * 1024 * 1024
MAIN_LIMIT = 56 * 1024 * 1024
EMBED_ROW, MIX_ROW, LATENT_ROW, GAIN_ROW, TABLE_ROWS = 0, 3, 9, 11, 16

norm_eps = 1e-05
head_eps = 1e-06

F32 = jnp.float32
BF16 = jnp.bfloat16


def mm(a, b):
    return jnp.dot(a, b, preferred_element_type=F32)


def mm_t(a, b):
    return lax.dot_general(a, b, (((1,), (1,)), ((), ())), preferred_element_type=F32)


def layer_norm(values, gain):
    average = jnp.mean(values, axis=-1, keepdims=True)
    centred = values - average
    spread = jnp.mean(centred * centred, axis=-1, keepdims=True)
    return centred * lax.rsqrt(spread + norm_eps) * gain


def iota(shape, dim):
    return lax.broadcasted_iota(jnp.int32, shape, dim)


def load_kernel(row_tokens, *refs):
    (
        ids_from,
        mix_from,
        level_embed_from,
        latent_query_from,
        enc_gain_from,
        attn_gain_from,
        mlp_gain_from,
        dec_gain_from,
        dec_from,
        embed_from,
        kv_from,
        pool_from,
        _,
        table_ref,
        query_ref,
        mean_ref,
        spread_ref,
        ones_ref,
        half_ref,
        allowed_ref,
        dec_ref,
        embed_ref,
        kv_ref,
        pool_ref,
        ids_ref,
        mix_ref,
        level_embed_ref,
        latent_query_ref,
        gain_refs,
        dec_rows_ref,
        arrivals,
    ) = refs
    pairs = [
        (ids_from, ids_ref),
        (mix_from, mix_ref),
        (level_embed_from, level_embed_ref),
        (latent_query_from, latent_query_ref),
        (enc_gain_from, gain_refs.at[0]),
        (attn_gain_from, gain_refs.at[1]),
        (mlp_gain_from, gain_refs.at[2]),
        (dec_gain_from, gain_refs.at[3]),
        (dec_from, dec_rows_ref),
        (embed_from, embed_ref),
        (kv_from, kv_ref),
        (pool_from, pool_ref),
    ]
    copies = [
        pltpu.make_async_copy(here, there, arrivals.at[i]) for i, (here, there) in enumerate(pairs)
    ]
    for copy in copies:
        copy.start()

    feature_head = iota((D, LANES), 0) // HEAD_DIM
    lane = iota((D, LANES), 1)
    on_head = (feature_head == lane % HEADS) & (lane < LATL * HEADS)
    mean_ref[...] = jnp.where(on_head, 1.0 / HEAD_DIM, 0.0).astype(BF16)
    spread_ref[...] = jnp.where(
        iota((LATL * HEADS, LATL * D), 0) == iota((LATL * HEADS, LATL * D), 1) // HEAD_DIM, 1.0, 0.0
    ).astype(BF16)
    ones_ref[...] = jnp.where(
        iota((HALF, HALF), 0) // HEAD_DIM == iota((HALF, HALF), 1) // HEAD_DIM, 1.0 / HEAD_DIM, 0.0
    ).astype(BF16)
    half_ref[...] = jnp.where(
        (iota((PAIR, PAIR), 0) < HEAD_DIM) == (iota((PAIR, PAIR), 1) < HEAD_DIM), 1.0, 0.0
    ).astype(BF16)
    row_bit = (iota((TOKENS, PAIR), 0) // (2 * row_tokens)) % 2
    lane_bit = (iota((TOKENS, PAIR), 1) // (2 * row_tokens)) % 2
    allowed_ref[...] = jnp.where(row_bit == lane_bit, 1.0, 0.0)

    for copy in copies[:8]:
        copy.wait()
    level_embed = level_embed_ref[...].astype(F32)
    for l in range(LEV):
        level = ids_ref[l]
        row = level_embed[LEV - 1 : LEV]
        for i in reversed(range(LEV - 1)):
            row = jnp.where(level == i, level_embed[i : i + 1], row)
        table_ref[EMBED_ROW + l : EMBED_ROW + l + 1, :] = row
        for j in range(LATL):
            at = MIX_ROW + l * LATL + j
            table_ref[at : at + 1, :] = jnp.full((1, D), mix_ref[j, level])
    latent = latent_query_ref[...].astype(F32)
    table_ref[LATENT_ROW : LATENT_ROW + LATL, :] = latent
    for i in range(4):
        table_ref[GAIN_ROW + i : GAIN_ROW + i + 1, :] = gain_refs[i]
    row_id = iota((LANES, D), 0)
    own_head = (row_id % HEADS) == iota((LANES, D), 1) // HEAD_DIM
    spots = jnp.zeros((LANES, D), F32)
    for j in range(LATL):
        mine = own_head & (row_id // HEADS == j)
        spots = jnp.where(mine, jnp.broadcast_to(latent[j : j + 1], (LANES, D)), spots)
    mean_square = jnp.sum(spots * spots, axis=-1, keepdims=True) / HEAD_DIM
    query_ref[...] = (spots * lax.rsqrt(mean_square + head_eps)).T.astype(BF16)

    copies[8].wait()
    dec_ref[...] = dec_rows_ref[...].astype(F32).T.astype(BF16)
    for copy in copies[9:]:
        copy.wait()


def load(row_tokens, after, scalars, rows, dec, early):
    far = pl.BlockSpec(memory_space=pl.ANY)
    made = [
        pltpu.VMEM((TABLE_ROWS, D), F32),
        pltpu.VMEM((D, LANES), BF16),
        pltpu.VMEM((D, LANES), BF16),
        pltpu.VMEM((LATL * HEADS, LATL * D), BF16),
        pltpu.VMEM((HALF, HALF), BF16),
        pltpu.VMEM((PAIR, PAIR), BF16),
        pltpu.VMEM((TOKENS, PAIR), F32),
        pltpu.VMEM(dec.shape[::-1], BF16),
    ] + [pltpu.VMEM(a.shape, a.dtype) for a in early]
    inputs = (*scalars, *rows, dec, *early)
    return pl.pallas_call(
        functools.partial(load_kernel, row_tokens),
        in_specs=[far] * (len(inputs) + 1),
        out_specs=[pl.BlockSpec(memory_space=pltpu.VMEM)] * len(made),
        out_shape=made,
        scratch_shapes=[pltpu.SMEM(a.shape, a.dtype) for a in scalars]
        + [
            pltpu.VMEM((LEV, D), BF16),
            pltpu.VMEM((LATL, D), BF16),
            pltpu.VMEM((4, 1, D), F32),
            pltpu.VMEM(dec.shape, BF16),
            pltpu.SemaphoreType.DMA((len(inputs),)),
        ],
        compiler_params=pltpu.CompilerParams(vmem_limit_bytes=LOAD_LIMIT),
        cost_estimate=pl.CostEstimate(flops=0, bytes_accessed=8_000_000, transcendentals=0),
    )(*inputs, after)


def forecast_kernel(windows, *refs):
    (
        table_ref,
        query_ref,
        mean_ref,
        spread_ref,
        ones_ref,
        half_ref,
        allowed_ref,
        dec_ref,
        embed_ref,
        kv_ref,
        pool_ref,
    ) = refs[:EARLY]
    far, (x_ref, out_ref), refs = refs[EARLY:][:LATE], refs[EARLY + LATE :][:2], refs[EARLY + LATE + 2 :]
    near, (state, wide, arrivals) = refs[:LATE], refs[LATE:]
    qkv_ref, proj_ref, up_ref, down_ref = near
    copies = [
        pltpu.make_async_copy(far[i], near[i], arrivals.at[i]) for i in range(LATE)
    ]

    def in_first_window(action):
        if windows == 1:
            action()
        else:
            pl.when(pl.program_id(0) == 0)(action)

    def start(*wanted):
        def action():
            for i in wanted:
                copies[i].start()

        in_first_window(action)

    def wait(turn_index, *wanted):
        def action():
            for i in wanted:
                copies[i].wait()

        if turn_index == 0:
            in_first_window(action)

    start(0, 1, 2, 3)

    def entry(at):
        return table_ref[at : at + 1, :]

    def embed(l):
        return entry(EMBED_ROW + l)

    def mixing(l, j):
        return entry(MIX_ROW + l * LATL + j)

    low = iota((1, PAIR), 1) < HEAD_DIM

    arrived = x_ref[0].astype(F32).reshape(PATCHES, LEV * PIN)
    for l in range(LEV):
        state[l * PATCHES : (l + 1) * PATCHES, :] = arrived[:, l * PIN : (l + 1) * PIN]

    def by_level(values):
        return [values[l * PATCHES : (l + 1) * PATCHES] for l in range(LEV)]

    for turn_index in range(STEPS):
        tokens = by_level(mm(state[...].astype(BF16), embed_ref[...]))
        tokens = jnp.concatenate([tokens[l] + embed(l) for l in range(LEV)], axis=0)
        tokens = layer_norm(tokens, entry(GAIN_ROW)).astype(BF16)
        keyval = mm(tokens, kv_ref[...])
        keys = keyval[:, :D]
        values = by_level(keyval[:, D:])
        mean_square = mm((keys * keys).astype(BF16), mean_ref[...])
        scores = mm(keys.astype(BF16), query_ref[...])
        scores = scores * lax.rsqrt(mean_square + head_eps) * HEAD_DIM ** (-0.5)
        scores = scores[:, : LATL * HEADS]
        parts = by_level(jnp.exp(scores))
        inverse = 1.0 / (parts[0] + parts[1] + parts[2])
        weights = jnp.concatenate([part * inverse for part in parts], axis=0).astype(BF16)
        wide_weights = by_level(mm(weights, spread_ref[...]))
        pooled = []
        for j in range(LATL):
            terms = [wide_weights[l][:, j * D : (j + 1) * D] * values[l] for l in range(LEV)]
            pooled.append(terms[0] + terms[1] + terms[2])
        latents = mm(jnp.concatenate(pooled, axis=0).astype(BF16), pool_ref[...])
        latents = jnp.concatenate(
            [
                latents[j * PATCHES : (j + 1) * PATCHES] + entry(LATENT_ROW + j)
                for j in range(LATL)
            ],
            axis=0,
        )
        normed = layer_norm(latents, entry(GAIN_ROW + 1)).astype(BF16)
        wait(turn_index, 0)
        projected = mm(normed, qkv_ref[...])
        allowed = allowed_ref[...]
        if windows > 1:
            cut = jnp.where(pl.program_id(0) == windows - 1, 1.0, 0.0)
            allowed = 1.0 - cut * (1.0 - allowed)
        halves = jnp.concatenate(
            [projected[:, i * HALF : (i + 1) * HALF] for i in range(4)], axis=0
        )
        mean_square = mm((halves * halves).astype(BF16), ones_ref[...])
        halves = halves * lax.rsqrt(mean_square + head_eps)
        win_values = projected[:, 2 * D :]
        mixed = []
        for pair in range(HEADS // 2):
            half, at = pair // 2, (pair % 2) * PAIR
            query = halves[half * TOKENS : (half + 1) * TOKENS, at : at + PAIR].astype(BF16)
            key = halves[(2 + half) * TOKENS : (3 + half) * TOKENS, at : at + PAIR]
            value = win_values[:, pair * PAIR : (pair + 1) * PAIR]
            key = jnp.concatenate(
                [jnp.where(low, key, 0.0), jnp.where(low, 0.0, key)], axis=0
            ).astype(BF16)
            value = jnp.concatenate(
                [jnp.where(low, value, 0.0), jnp.where(low, 0.0, value)], axis=0
            ).astype(BF16)
            weights = jnp.exp(mm_t(query, key) * HEAD_DIM ** (-0.5)) * allowed
            both = mm(weights.astype(BF16), jnp.concatenate([value, half_ref[...]], axis=1))
            mixed.append((both[:, :PAIR] / both[:, PAIR:]).astype(BF16))
        wait(turn_index, 1)
        attended = latents + mm(jnp.concatenate(mixed, axis=1), proj_ref[...])
        normed = layer_norm(attended, entry(GAIN_ROW + 2)).astype(BF16)
        wait(turn_index, 2)
        hidden = jax.nn.gelu(mm(normed, up_ref[...])).astype(BF16)
        wait(turn_index, 3)
        backbone = attended + mm(hidden, down_ref[...])
        first, second = backbone[:PATCHES], backbone[PATCHES:]
        blended = jnp.concatenate(
            [mixing(l, 0) * first + mixing(l, 1) * second + embed(l) for l in range(LEV)], axis=0
        )
        normed = layer_norm(blended, entry(GAIN_ROW + 3)).astype(BF16)
        state[...] = (state[...] + mm(normed, dec_ref[...])).astype(BF16).astype(F32)

    for l in range(LEV):
        wide[:, l * PIN : (l + 1) * PIN] = state[l * PATCHES : (l + 1) * PATCHES, :]
    out_ref[0] = wide[...].reshape(out_ref.shape[1:]).astype(BF16)


def forecast(windows, arranged, early, late):
    vmem = pl.BlockSpec(memory_space=pltpu.VMEM)
    if windows == 1:
        block, grid = vmem, ()
        result = pltpu.VMEM(arranged.shape, BF16)
        arranged = pltpu.with_memory_space_constraint(arranged, pltpu.VMEM)
    else:
        result = jax.ShapeDtypeStruct(arranged.shape, BF16)
        block = pl.BlockSpec((1,) + arranged.shape[1:], lambda i: (i, 0, 0, 0))
        grid = (windows,)
    early = [pltpu.with_memory_space_constraint(a, pltpu.VMEM) for a in early]
    return pl.pallas_call(
        functools.partial(forecast_kernel, windows),
        grid=grid,
        in_specs=[vmem] * EARLY + [pl.BlockSpec(memory_space=pl.ANY)] * LATE + [block],
        out_specs=block,
        out_shape=result,
        scratch_shapes=[pltpu.VMEM(a.shape, a.dtype) for a in late]
        + [
            pltpu.VMEM((LEV * PATCHES, PIN), F32),
            pltpu.VMEM((PATCHES, LEV * PIN), F32),
            pltpu.SemaphoreType.DMA((LATE,)),
        ],
        compiler_params=pltpu.CompilerParams(vmem_limit_bytes=MAIN_LIMIT),
    )(*early, *late, arranged)


def turn_kernel(step, direction, x_ref, out_ref, *token_ref):
    count = x_ref.shape[0] if len(x_ref.shape) == 3 else out_ref.shape[0]
    for ref in token_ref:
        ref[...] = jnp.zeros_like(ref)
    turned = lax.axis_index("lon") < step
    blocks = x_ref[...].astype(F32).reshape(count, 2, LEV * PIN)

    @pl.when(turned)
    def _():
        if direction > 0:
            moved = jnp.concatenate([blocks[1:], blocks[:1]], axis=0)
        else:
            moved = jnp.concatenate([blocks[-1:], blocks[:-1]], axis=0)
        out_ref[...] = moved.reshape(out_ref.shape).astype(BF16)

    @pl.when(jnp.logical_not(turned))
    def _():
        out_ref[...] = blocks.reshape(out_ref.shape).astype(BF16)


def turn(array, shape, step, direction, token=False):
    shapes = [jax.ShapeDtypeStruct(shape, BF16)]
    if token:
        shapes.append(jax.ShapeDtypeStruct((8, LANES), F32))
    return pl.pallas_call(
        functools.partial(turn_kernel, step, direction), out_shape=shapes
    )(array)


def across_pieces(blocks):
    rows = W_LAT
    groups = [[q * rows + r for q in range(ROW_PARTS)] for r in range(rows)]
    return lax.all_to_all(
        blocks, "lon", split_axis=0, concat_axis=0, tiled=True, axis_index_groups=groups
    )


def across_rows(blocks):
    rows = W_LAT
    groups = [[q * rows + r for r in range(rows)] for q in range(ROW_PARTS)]
    return lax.all_to_all(
        blocks, "lon", split_axis=0, concat_axis=0, tiled=True, axis_index_groups=groups
    )


def shards(
    fields,
    level_ids,
    embed_weight,
    level_embed,
    enc_gain,
    latent_query,
    kv_weight,
    pool_out,
    attn_gain,
    qkv_weight,
    attn_proj,
    mlp_gain,
    mlp_up,
    mlp_down,
    level_mix,
    dec_gain,
    dec_weight,
):
    devices = lax.axis_size("lon")
    width = fields.shape[2]
    local_count = fields.shape[1]
    piece_cols = local_count // devices
    lat_count = devices // ROW_PARTS
    bands = lat_count // W_LAT
    cut = (W_LON // 2 // piece_cols) * lat_count
    scalars = (level_ids, level_mix.T)
    rows = (
        level_embed,
        latent_query,
        enc_gain.reshape(1, D),
        attn_gain.reshape(1, D),
        mlp_gain.reshape(1, D),
        dec_gain.reshape(1, D),
    )
    row_tokens = piece_cols * ROW_PARTS if bands == 1 else piece_cols
    outgoing, token = turn(
        fields.reshape(local_count, width), (devices, piece_cols, width), cut, 1, token=True
    )
    early = load(row_tokens, token, scalars, rows, dec_weight.T, (embed_weight, kv_weight, pool_out))
    late = (qkv_weight, attn_proj, mlp_up, mlp_down)
    if bands == 1:
        got = outgoing.reshape(ROW_PARTS, lat_count, piece_cols, width)
        got = across_rows(across_pieces(got).swapaxes(0, 1))
    else:
        got = lax.all_to_all(outgoing, "lon", split_axis=0, concat_axis=0, tiled=True)
        got = got.reshape(ROW_PARTS, lat_count, piece_cols, width)
        got = jnp.roll(got, -(W_LAT // 2), axis=1)
        got = got.reshape(ROW_PARTS, bands, W_LAT, piece_cols, width).transpose(1, 0, 2, 3, 4)
    done = forecast(bands, got.reshape(bands, ROW_PARTS * W_LAT, piece_cols, width), early, late)
    if bands == 1:
        home = done.reshape(lat_count, ROW_PARTS, piece_cols, width)
        home = across_pieces(across_rows(home).swapaxes(0, 1))
        home = home.reshape(devices, piece_cols, width)
    else:
        done = done.reshape(bands, ROW_PARTS, W_LAT, piece_cols, width).transpose(1, 0, 2, 3, 4)
        done = done.reshape(ROW_PARTS, lat_count, piece_cols, width)
        done = jnp.roll(done, W_LAT // 2, axis=1).reshape(devices, piece_cols, width)
        home = lax.all_to_all(done, "lon", split_axis=0, concat_axis=0, tiled=True)
    (forecast_here,) = turn(home, (local_count, width), cut, -1)
    return forecast_here.reshape(fields.shape)


def solution(mesh):
    placed = (P(("groups", "lon"), None, None), P("groups")) + (P(),) * 15
    return jax.shard_map(
        shards,
        mesh=mesh,
        in_specs=placed,
        out_specs=P(("groups", "lon"), None, None),
        check_vma=False,
    )
```

```python
import functools

import jax
import jax.numpy as jnp
from jax import lax
from jax.experimental import pallas as pl
from jax.experimental.pallas import tpu as pltpu
from jax.sharding import PartitionSpec as P

D = 512
HEADS = 8
HEAD_DIM = D // HEADS
PIN = 500
LEV = 3
LATL = 2
W_LAT = 4
W_LON = 8
STEPS = 2
ROW_PARTS = 4
MLP = 2048
PATCHES = W_LAT * W_LON
TOKENS = PATCHES * LATL
HALF = D // 2
PAIR = 2 * HEAD_DIM
EARLY, LATE = 11, 4
LANES = 128
LOAD_LIMIT = 56 * 1024 * 1024
MAIN_LIMIT = 56 * 1024 * 1024
EMBED_ROW, MIX_ROW, LATENT_ROW, GAIN_ROW, TABLE_ROWS = 0, 3, 9, 11, 16

norm_eps = 1e-05
head_eps = 1e-06

F32 = jnp.float32
BF16 = jnp.bfloat16


def mm(a, b):
    return jnp.dot(a, b, preferred_element_type=F32)


def mm_t(a, b):
    return lax.dot_general(a, b, (((1,), (1,)), ((), ())), preferred_element_type=F32)


def layer_norm(values, gain):
    average = jnp.mean(values, axis=-1, keepdims=True)
    centred = values - average
    spread = jnp.mean(centred * centred, axis=-1, keepdims=True)
    return (centred * gain).astype(BF16), lax.rsqrt(spread + norm_eps)


def iota(shape, dim):
    return lax.broadcasted_iota(jnp.int32, shape, dim)


def load_kernel(*refs):
    (
        ids_from,
        mix_from,
        level_embed_from,
        latent_query_from,
        enc_gain_from,
        attn_gain_from,
        mlp_gain_from,
        dec_gain_from,
        dec_from,
        embed_from,
        kv_from,
        pool_from,
        _,
        table_ref,
        query_ref,
        mean_ref,
        spread_ref,
        ones_ref,
        half_ref,
        allowed_ref,
        dec_ref,
        embed_ref,
        kv_ref,
        pool_ref,
        ids_ref,
        mix_ref,
        level_embed_ref,
        latent_query_ref,
        gain_refs,
        dec_rows_ref,
        arrivals,
    ) = refs
    pairs = [
        (ids_from, ids_ref),
        (mix_from, mix_ref),
        (level_embed_from, level_embed_ref),
        (latent_query_from, latent_query_ref),
        (enc_gain_from, gain_refs.at[0]),
        (attn_gain_from, gain_refs.at[1]),
        (mlp_gain_from, gain_refs.at[2]),
        (dec_gain_from, gain_refs.at[3]),
        (dec_from, dec_rows_ref),
        (embed_from, embed_ref),
        (kv_from, kv_ref),
        (pool_from, pool_ref),
    ]
    copies = [
        pltpu.make_async_copy(here, there, arrivals.at[i]) for i, (here, there) in enumerate(pairs)
    ]
    for copy in copies:
        copy.start()

    feature_head = iota((D, LANES), 0) // HEAD_DIM
    lane = iota((D, LANES), 1)
    on_head = (feature_head == lane % HEADS) & (lane < LATL * HEADS)
    mean_ref[...] = jnp.where(on_head, 1.0 / HEAD_DIM, 0.0).astype(BF16)
    spread_ref[...] = jnp.where(
        iota((LATL * HEADS, LATL * D), 0) == iota((LATL * HEADS, LATL * D), 1) // HEAD_DIM, 1.0, 0.0
    ).astype(BF16)
    ones_ref[...] = jnp.where(
        iota((HALF, HALF), 0) // HEAD_DIM == iota((HALF, HALF), 1) // HEAD_DIM, 1.0 / HEAD_DIM, 0.0
    ).astype(BF16)
    half_ref[...] = jnp.where(
        (iota((PAIR, PAIR), 0) < HEAD_DIM) == (iota((PAIR, PAIR), 1) < HEAD_DIM), 1.0, 0.0
    ).astype(BF16)
    row_bit = (iota((TOKENS, PAIR), 0) // 4) % 2
    lane_bit = (iota((TOKENS, PAIR), 1) // 4) % 2
    allowed_ref[...] = jnp.where(row_bit == lane_bit, 1.0, 0.0)

    for copy in copies[:8]:
        copy.wait()
    level_embed = level_embed_ref[...].astype(F32)
    for l in range(LEV):
        level = ids_ref[l]
        row = level_embed[LEV - 1 : LEV]
        for i in reversed(range(LEV - 1)):
            row = jnp.where(level == i, level_embed[i : i + 1], row)
        table_ref[EMBED_ROW + l : EMBED_ROW + l + 1, :] = row
        for j in range(LATL):
            at = MIX_ROW + l * LATL + j
            table_ref[at : at + 1, :] = jnp.full((1, D), mix_ref[j, level])
    latent = latent_query_ref[...].astype(F32)
    table_ref[LATENT_ROW : LATENT_ROW + LATL, :] = latent
    for i in range(4):
        table_ref[GAIN_ROW + i : GAIN_ROW + i + 1, :] = gain_refs[i]
    row_id = iota((LANES, D), 0)
    own_head = (row_id % HEADS) == iota((LANES, D), 1) // HEAD_DIM
    spots = jnp.zeros((LANES, D), F32)
    for j in range(LATL):
        mine = own_head & (row_id // HEADS == j)
        spots = jnp.where(mine, jnp.broadcast_to(latent[j : j + 1], (LANES, D)), spots)
    mean_square = jnp.sum(spots * spots, axis=-1, keepdims=True) / HEAD_DIM
    query_ref[...] = (spots * lax.rsqrt(mean_square + head_eps)).T.astype(BF16)

    copies[8].wait()
    dec_ref[...] = dec_rows_ref[...].astype(F32).T.astype(BF16)
    for copy in copies[9:]:
        copy.wait()


def load(after, scalars, rows, dec, early):
    far = pl.BlockSpec(memory_space=pl.ANY)
    made = [
        pltpu.VMEM((TABLE_ROWS, D), F32),
        pltpu.VMEM((D, LANES), BF16),
        pltpu.VMEM((D, LANES), BF16),
        pltpu.VMEM((LATL * HEADS, LATL * D), BF16),
        pltpu.VMEM((HALF, HALF), BF16),
        pltpu.VMEM((PAIR, PAIR), BF16),
        pltpu.VMEM((TOKENS, PAIR), F32),
        pltpu.VMEM(dec.shape[::-1], BF16),
    ] + [pltpu.VMEM(a.shape, a.dtype) for a in early]
    inputs = (*scalars, *rows, dec, *early)
    return pl.pallas_call(
        load_kernel,
        in_specs=[far] * (len(inputs) + 1),
        out_specs=[pl.BlockSpec(memory_space=pltpu.VMEM)] * len(made),
        out_shape=made,
        scratch_shapes=[pltpu.SMEM(a.shape, a.dtype) for a in scalars]
        + [
            pltpu.VMEM((LEV, D), BF16),
            pltpu.VMEM((LATL, D), BF16),
            pltpu.VMEM((4, 1, D), F32),
            pltpu.VMEM(dec.shape, BF16),
            pltpu.SemaphoreType.DMA((len(inputs),)),
        ],
        compiler_params=pltpu.CompilerParams(vmem_limit_bytes=LOAD_LIMIT),
        cost_estimate=pl.CostEstimate(flops=0, bytes_accessed=8_000_000, transcendentals=0),
    )(*inputs, after)


def forecast_kernel(windows, *refs):
    (
        table_ref,
        query_ref,
        mean_ref,
        spread_ref,
        ones_ref,
        half_ref,
        allowed_ref,
        dec_ref,
        embed_ref,
        kv_ref,
        pool_ref,
    ) = refs[:EARLY]
    far, (x_ref, out_ref), refs = refs[EARLY:][:LATE], refs[EARLY + LATE :][:2], refs[EARLY + LATE + 2 :]
    near, (state, wide, arrivals) = refs[:LATE], refs[LATE:]
    qkv_ref, proj_ref, up_ref, down_ref = near
    copies = [
        pltpu.make_async_copy(far[i], near[i], arrivals.at[i]) for i in range(LATE)
    ]

    def in_first_window(action):
        if windows == 1:
            action()
        else:
            pl.when(pl.program_id(0) == 0)(action)

    def start(*wanted):
        def action():
            for i in wanted:
                copies[i].start()

        in_first_window(action)

    def wait(turn_index, *wanted):
        def action():
            for i in wanted:
                copies[i].wait()

        if turn_index == 0:
            in_first_window(action)

    start(0, 1, 2, 3)

    def entry(at):
        return table_ref[at : at + 1, :]

    def embed(l):
        return entry(EMBED_ROW + l)

    def mixing(l, j):
        return entry(MIX_ROW + l * LATL + j)

    low = iota((1, PAIR), 1) < HEAD_DIM
    each = jnp.full((16, PAIR), 1.0 / HEAD_DIM, BF16)

    arrived = x_ref[0].astype(F32).reshape(PATCHES, LEV * PIN)
    for l in range(LEV):
        state[l * PATCHES : (l + 1) * PATCHES, :] = arrived[:, l * PIN : (l + 1) * PIN]

    def by_level(values):
        return [values[l * PATCHES : (l + 1) * PATCHES] for l in range(LEV)]

    for turn_index in range(STEPS):
        tokens = by_level(mm(state[...].astype(BF16), embed_ref[...]))
        tokens = jnp.concatenate([tokens[l] + embed(l) for l in range(LEV)], axis=0)
        tokens, factor = layer_norm(tokens, entry(GAIN_ROW))
        keyval = mm(tokens, kv_ref[...])
        keys = keyval[:, :D]
        values = by_level(keyval[:, D:])
        mean_square = mm((keys * keys).astype(BF16), mean_ref[...])[:, : LATL * HEADS]
        scores = mm(keys.astype(BF16), query_ref[...])[:, : LATL * HEADS]
        scale = factor * lax.rsqrt(factor * factor * mean_square + head_eps)
        parts = by_level(jnp.exp(scores * scale * HEAD_DIM ** (-0.5)))
        inverse = 1.0 / (parts[0] + parts[1] + parts[2])
        factors = by_level(factor)
        weights = jnp.concatenate(
            [parts[l] * (inverse * factors[l]) for l in range(LEV)], axis=0
        ).astype(BF16)
        wide_weights = by_level(mm(weights, spread_ref[...]))
        pooled = []
        for j in range(LATL):
            terms = [wide_weights[l][:, j * D : (j + 1) * D] * values[l] for l in range(LEV)]
            pooled.append(terms[0] + terms[1] + terms[2])
        latents = mm(jnp.concatenate(pooled, axis=0).astype(BF16), pool_ref[...])
        latents = jnp.concatenate(
            [
                latents[j * PATCHES : (j + 1) * PATCHES] + entry(LATENT_ROW + j)
                for j in range(LATL)
            ],
            axis=0,
        )
        normed, factor = layer_norm(latents, entry(GAIN_ROW + 1))
        wait(turn_index, 0)
        projected = mm(normed, qkv_ref[...])
        allowed = allowed_ref[...]
        if windows > 1:
            cut = jnp.where(pl.program_id(0) == windows - 1, 1.0, 0.0)
            allowed = 1.0 - cut * (1.0 - allowed)
        queries = jnp.concatenate([projected[:, :HALF], projected[:, HALF:D]], axis=0)
        mean_square = mm((queries * queries).astype(BF16), ones_ref[...])
        twice = jnp.concatenate([factor, factor], axis=0)
        query_scale = lax.rsqrt(twice * twice * mean_square + head_eps)
        query_scale = query_scale * (twice * HEAD_DIM ** (-0.5))
        win_keys = projected[:, D : 2 * D] * factor
        win_values = projected[:, 2 * D :] * factor
        mixed = []
        for pair in range(HEADS // 2):
            half, at = pair // 2, (pair % 2) * PAIR
            rows = slice(half * TOKENS, (half + 1) * TOKENS)
            query = queries[rows, at : at + PAIR].astype(BF16)
            key = win_keys[:, pair * PAIR : (pair + 1) * PAIR]
            value = win_values[:, pair * PAIR : (pair + 1) * PAIR]
            key = jnp.concatenate([jnp.where(low, key, 0.0), jnp.where(low, 0.0, key)], axis=0)
            value = jnp.concatenate(
                [jnp.where(low, value, 0.0), jnp.where(low, 0.0, value)], axis=0
            ).astype(BF16)
            key_square = mm_t(each, (key * key).astype(BF16))[:1]
            scale = query_scale[rows, at : at + PAIR] * lax.rsqrt(key_square + head_eps)
            weights = jnp.exp(mm_t(query, key.astype(BF16)) * scale) * allowed
            both = mm(weights.astype(BF16), jnp.concatenate([value, half_ref[...]], axis=1))
            mixed.append((both[:, :PAIR] / both[:, PAIR:]).astype(BF16))
        wait(turn_index, 1)
        attended = latents + mm(jnp.concatenate(mixed, axis=1), proj_ref[...])
        normed, factor = layer_norm(attended, entry(GAIN_ROW + 2))
        wait(turn_index, 2)
        hidden = jax.nn.gelu(mm(normed, up_ref[...]) * factor).astype(BF16)
        wait(turn_index, 3)
        backbone = attended + mm(hidden, down_ref[...])
        first, second = backbone[:PATCHES], backbone[PATCHES:]
        blended = jnp.concatenate(
            [mixing(l, 0) * first + mixing(l, 1) * second + embed(l) for l in range(LEV)], axis=0
        )
        normed, factor = layer_norm(blended, entry(GAIN_ROW + 3))
        state[...] = (state[...] + mm(normed, dec_ref[...]) * factor).astype(BF16).astype(F32)

    for l in range(LEV):
        wide[:, l * PIN : (l + 1) * PIN] = state[l * PATCHES : (l + 1) * PATCHES, :]
    out_ref[0] = wide[...].reshape(out_ref.shape[1:]).astype(BF16)


def forecast(windows, arranged, early, late):
    vmem = pl.BlockSpec(memory_space=pltpu.VMEM)
    if windows == 1:
        block, grid = vmem, ()
        result = pltpu.VMEM(arranged.shape, BF16)
        arranged = pltpu.with_memory_space_constraint(arranged, pltpu.VMEM)
    else:
        result = jax.ShapeDtypeStruct(arranged.shape, BF16)
        block = pl.BlockSpec((1,) + arranged.shape[1:], lambda i: (i, 0, 0, 0))
        grid = (windows,)
    early = [pltpu.with_memory_space_constraint(a, pltpu.VMEM) for a in early]
    return pl.pallas_call(
        functools.partial(forecast_kernel, windows),
        grid=grid,
        in_specs=[vmem] * EARLY + [pl.BlockSpec(memory_space=pl.ANY)] * LATE + [block],
        out_specs=block,
        out_shape=result,
        scratch_shapes=[pltpu.VMEM(a.shape, a.dtype) for a in late]
        + [
            pltpu.VMEM((LEV * PATCHES, PIN), F32),
            pltpu.VMEM((PATCHES, LEV * PIN), F32),
            pltpu.SemaphoreType.DMA((LATE,)),
        ],
        compiler_params=pltpu.CompilerParams(vmem_limit_bytes=MAIN_LIMIT),
    )(*early, *late, arranged)


def turn_kernel(step, direction, x_ref, out_ref, *token_ref):
    count = x_ref.shape[0] if len(x_ref.shape) == 3 else out_ref.shape[0]
    for ref in token_ref:
        ref[...] = jnp.zeros_like(ref)
    turned = lax.axis_index("lon") < step
    blocks = x_ref[...].astype(F32).reshape(count, 2, LEV * PIN)

    @pl.when(turned)
    def _():
        if direction > 0:
            moved = jnp.concatenate([blocks[1:], blocks[:1]], axis=0)
        else:
            moved = jnp.concatenate([blocks[-1:], blocks[:-1]], axis=0)
        out_ref[...] = moved.reshape(out_ref.shape).astype(BF16)

    @pl.when(jnp.logical_not(turned))
    def _():
        out_ref[...] = blocks.reshape(out_ref.shape).astype(BF16)


def turn(array, shape, step, direction, token=False):
    shapes = [jax.ShapeDtypeStruct(shape, BF16)]
    if token:
        shapes.append(jax.ShapeDtypeStruct((8, LANES), F32))
    return pl.pallas_call(
        functools.partial(turn_kernel, step, direction), out_shape=shapes
    )(array)


def shards(
    fields,
    level_ids,
    embed_weight,
    level_embed,
    enc_gain,
    latent_query,
    kv_weight,
    pool_out,
    attn_gain,
    qkv_weight,
    attn_proj,
    mlp_gain,
    mlp_up,
    mlp_down,
    level_mix,
    dec_gain,
    dec_weight,
):
    devices = lax.axis_size("lon")
    width = fields.shape[2]
    local_count = fields.shape[1]
    piece_cols = local_count // devices
    lat_count = devices // ROW_PARTS
    bands = lat_count // W_LAT
    cut = (W_LON // 2 // piece_cols) * lat_count
    scalars = (level_ids, level_mix.T)
    rows = (
        level_embed,
        latent_query,
        enc_gain.reshape(1, D),
        attn_gain.reshape(1, D),
        mlp_gain.reshape(1, D),
        dec_gain.reshape(1, D),
    )
    outgoing, token = turn(
        fields.reshape(local_count, width), (devices, piece_cols, width), cut, 1, token=True
    )
    early = load(token, scalars, rows, dec_weight.T, (embed_weight, kv_weight, pool_out))
    late = (qkv_weight, attn_proj, mlp_up, mlp_down)
    got = lax.all_to_all(outgoing, "lon", split_axis=0, concat_axis=0, tiled=True)
    if bands > 1:
        got = got.reshape(ROW_PARTS, lat_count, piece_cols, width)
        got = jnp.roll(got, -(W_LAT // 2), axis=1)
        got = got.reshape(ROW_PARTS, bands, W_LAT, piece_cols, width).transpose(1, 0, 2, 3, 4)
    done = forecast(bands, got.reshape(bands, ROW_PARTS * W_LAT, piece_cols, width), early, late)
    if bands > 1:
        done = done.reshape(bands, ROW_PARTS, W_LAT, piece_cols, width).transpose(1, 0, 2, 3, 4)
        done = done.reshape(ROW_PARTS, lat_count, piece_cols, width)
        done = jnp.roll(done, W_LAT // 2, axis=1)
    done = done.reshape(devices, piece_cols, width)
    home = lax.all_to_all(done, "lon", split_axis=0, concat_axis=0, tiled=True)
    (forecast_here,) = turn(home, (local_count, width), cut, -1)
    return forecast_here.reshape(fields.shape)


def solution(mesh):
    placed = (P(("groups", "lon"), None, None), P("groups")) + (P(),) * 15
    return jax.shard_map(
        shards,
        mesh=mesh,
        in_specs=placed,
        out_specs=P(("groups", "lon"), None, None),
        check_vma=False,
    )
```

```python
import functools
import math

import jax
import jax.numpy as jnp
from jax import lax
from jax.experimental import pallas as pl
from jax.experimental.pallas import tpu as pltpu
from jax.sharding import PartitionSpec as P

D = 512
HEADS = 8
HEAD_DIM = D // HEADS
PIN = 500
LEV = 3
LATL = 2
W_LAT = 4
W_LON = 8
STEPS = 2
ROW_PARTS = 4
MLP = 2048
PATCHES = W_LAT * W_LON
TOKENS = PATCHES * LATL
HALF = D // 2
PAIR = 2 * HEAD_DIM
EARLY, LATE = 11, 4
LANES = 128
LOAD_LIMIT = 56 * 1024 * 1024
MAIN_LIMIT = 56 * 1024 * 1024
EMBED_ROW, MIX_ROW, LATENT_ROW, GAIN_ROW, TABLE_ROWS = 0, 3, 9, 11, 16

GELU_FIRST = math.sqrt(2.0 / math.pi)
GELU_THIRD = 0.044715 * GELU_FIRST
SCORE_SCALE = HEAD_DIM ** (-0.5) * math.log2(math.e)

norm_eps = 1e-05
head_eps = 1e-06

F32 = jnp.float32
BF16 = jnp.bfloat16


def mm(a, b):
    return jnp.dot(a, b, preferred_element_type=F32)


def mm_t(a, b):
    return lax.dot_general(a, b, (((1,), (1,)), ((), ())), preferred_element_type=F32)


def layer_norm(values, gain, centred=False):
    if not centred:
        values = values - jnp.mean(values, axis=-1, keepdims=True)
    spread = jnp.mean(values * values, axis=-1, keepdims=True)
    return (values * gain).astype(BF16), lax.rsqrt(spread + norm_eps)


def centre(rows):
    return rows - jnp.mean(rows, axis=-1, keepdims=True)


def gelu(values):
    curve = values * (GELU_FIRST + GELU_THIRD * (values * values))
    half = 0.5 * values
    return half + half * jnp.tanh(curve)


def iota(shape, dim):
    return lax.broadcasted_iota(jnp.int32, shape, dim)


def load_kernel(*refs):
    (
        ids_from,
        mix_from,
        level_embed_from,
        latent_query_from,
        enc_gain_from,
        attn_gain_from,
        mlp_gain_from,
        dec_gain_from,
        dec_from,
        embed_from,
        kv_from,
        pool_from,
        _,
        table_ref,
        query_ref,
        mean_ref,
        spread_ref,
        ones_ref,
        half_ref,
        allowed_ref,
        dec_ref,
        embed_ref,
        kv_ref,
        pool_ref,
        ids_ref,
        mix_ref,
        level_embed_ref,
        latent_query_ref,
        gain_refs,
        dec_rows_ref,
        embed_rows_ref,
        pool_rows_ref,
        arrivals,
    ) = refs
    pairs = [
        (ids_from, ids_ref),
        (mix_from, mix_ref),
        (level_embed_from, level_embed_ref),
        (latent_query_from, latent_query_ref),
        (enc_gain_from, gain_refs.at[0]),
        (attn_gain_from, gain_refs.at[1]),
        (mlp_gain_from, gain_refs.at[2]),
        (dec_gain_from, gain_refs.at[3]),
        (dec_from, dec_rows_ref),
        (embed_from, embed_rows_ref),
        (pool_from, pool_rows_ref),
        (kv_from, kv_ref),
    ]
    copies = [
        pltpu.make_async_copy(here, there, arrivals.at[i]) for i, (here, there) in enumerate(pairs)
    ]
    for copy in copies:
        copy.start()

    feature_head = iota((D, LANES), 0) // HEAD_DIM
    lane = iota((D, LANES), 1)
    on_head = (feature_head == lane % HEADS) & (lane < LATL * HEADS)
    mean_ref[...] = jnp.where(on_head, 1.0 / HEAD_DIM, 0.0).astype(BF16)
    spread_ref[...] = jnp.where(
        iota((LATL * HEADS, LATL * D), 0) == iota((LATL * HEADS, LATL * D), 1) // HEAD_DIM, 1.0, 0.0
    ).astype(BF16)
    ones_ref[...] = jnp.where(
        iota((HALF, HALF), 0) // HEAD_DIM == iota((HALF, HALF), 1) // HEAD_DIM, 1.0 / HEAD_DIM, 0.0
    ).astype(BF16)
    half_ref[...] = jnp.where(
        (iota((PAIR, PAIR), 0) < HEAD_DIM) == (iota((PAIR, PAIR), 1) < HEAD_DIM), 1.0, 0.0
    ).astype(BF16)
    row_bit = (iota((TOKENS, PAIR), 0) // 4) % 2
    lane_bit = (iota((TOKENS, PAIR), 1) // 4) % 2
    allowed_ref[...] = jnp.where(row_bit == lane_bit, 1.0, 0.0)

    for copy in copies[:8]:
        copy.wait()
    level_embed = centre(level_embed_ref[...].astype(F32))
    for l in range(LEV):
        level = ids_ref[l]
        row = level_embed[LEV - 1 : LEV]
        for i in reversed(range(LEV - 1)):
            row = jnp.where(level == i, level_embed[i : i + 1], row)
        table_ref[EMBED_ROW + l : EMBED_ROW + l + 1, :] = row
        for j in range(LATL):
            at = MIX_ROW + l * LATL + j
            table_ref[at : at + 1, :] = jnp.full((1, D), mix_ref[j, level])
    latent = latent_query_ref[...].astype(F32)
    table_ref[LATENT_ROW : LATENT_ROW + LATL, :] = centre(latent)
    for i in range(4):
        table_ref[GAIN_ROW + i : GAIN_ROW + i + 1, :] = gain_refs[i]
    row_id = iota((LANES, D), 0)
    own_head = (row_id % HEADS) == iota((LANES, D), 1) // HEAD_DIM
    spots = jnp.zeros((LANES, D), F32)
    for j in range(LATL):
        mine = own_head & (row_id // HEADS == j)
        spots = jnp.where(mine, jnp.broadcast_to(latent[j : j + 1], (LANES, D)), spots)
    mean_square = jnp.sum(spots * spots, axis=-1, keepdims=True) / HEAD_DIM
    query_ref[...] = (spots * lax.rsqrt(mean_square + head_eps)).T.astype(BF16)

    copies[8].wait()
    dec_ref[...] = dec_rows_ref[...].astype(F32).T.astype(BF16)
    copies[9].wait()
    embed_ref[...] = centre(embed_rows_ref[...].astype(F32)).astype(BF16)
    copies[10].wait()
    pool_ref[...] = centre(pool_rows_ref[...].astype(F32)).astype(BF16)
    copies[11].wait()


def load(after, scalars, rows, dec, early):
    far = pl.BlockSpec(memory_space=pl.ANY)
    made = [
        pltpu.VMEM((TABLE_ROWS, D), F32),
        pltpu.VMEM((D, LANES), BF16),
        pltpu.VMEM((D, LANES), BF16),
        pltpu.VMEM((LATL * HEADS, LATL * D), BF16),
        pltpu.VMEM((HALF, HALF), BF16),
        pltpu.VMEM((PAIR, PAIR), BF16),
        pltpu.VMEM((TOKENS, PAIR), F32),
        pltpu.VMEM(dec.shape[::-1], BF16),
    ] + [pltpu.VMEM(a.shape, a.dtype) for a in early]
    inputs = (*scalars, *rows, dec, *early)
    return pl.pallas_call(
        load_kernel,
        in_specs=[far] * (len(inputs) + 1),
        out_specs=[pl.BlockSpec(memory_space=pltpu.VMEM)] * len(made),
        out_shape=made,
        scratch_shapes=[pltpu.SMEM(a.shape, a.dtype) for a in scalars]
        + [
            pltpu.VMEM((LEV, D), BF16),
            pltpu.VMEM((LATL, D), BF16),
            pltpu.VMEM((4, 1, D), F32),
            pltpu.VMEM(dec.shape, BF16),
            pltpu.VMEM(early[0].shape, BF16),
            pltpu.VMEM(early[2].shape, BF16),
            pltpu.SemaphoreType.DMA((len(inputs),)),
        ],
        compiler_params=pltpu.CompilerParams(vmem_limit_bytes=LOAD_LIMIT),
        cost_estimate=pl.CostEstimate(flops=0, bytes_accessed=8_000_000, transcendentals=0),
    )(*inputs, after)


def forecast_kernel(windows, *refs):
    (
        table_ref,
        query_ref,
        mean_ref,
        spread_ref,
        ones_ref,
        half_ref,
        allowed_ref,
        dec_ref,
        embed_ref,
        kv_ref,
        pool_ref,
    ) = refs[:EARLY]
    far, (x_ref, out_ref), refs = refs[EARLY:][:LATE], refs[EARLY + LATE :][:2], refs[EARLY + LATE + 2 :]
    near, (wide, arrivals) = refs[:LATE], refs[LATE:]
    qkv_ref, proj_ref, up_ref, down_ref = near
    copies = [
        pltpu.make_async_copy(far[i], near[i], arrivals.at[i]) for i in range(LATE)
    ]

    def in_first_window(action):
        if windows == 1:
            action()
        else:
            pl.when(pl.program_id(0) == 0)(action)

    def start(*wanted):
        def action():
            for i in wanted:
                copies[i].start()

        in_first_window(action)

    def wait(turn_index, *wanted):
        def action():
            for i in wanted:
                copies[i].wait()

        if turn_index == 0:
            in_first_window(action)

    start(0, 1, 2, 3)

    def entry(at):
        return table_ref[at : at + 1, :]

    def embed(l):
        return entry(EMBED_ROW + l)

    def mixing(l, j):
        return entry(MIX_ROW + l * LATL + j)

    low = iota((1, PAIR), 1) < HEAD_DIM
    each = jnp.full((16, PAIR), 1.0 / HEAD_DIM, BF16)

    arrived = x_ref[0].astype(F32).reshape(PATCHES, LEV * PIN)
    current = jnp.concatenate(
        [arrived[:, l * PIN : (l + 1) * PIN] for l in range(LEV)], axis=0
    )

    def by_level(values):
        return [values[l * PATCHES : (l + 1) * PATCHES] for l in range(LEV)]

    for turn_index in range(STEPS):
        tokens = by_level(mm(current.astype(BF16), embed_ref[...]))
        tokens = jnp.concatenate([tokens[l] + embed(l) for l in range(LEV)], axis=0)
        tokens, factor = layer_norm(tokens, entry(GAIN_ROW), centred=True)
        keyval = mm(tokens, kv_ref[...])
        keys = keyval[:, :D]
        values = by_level(keyval[:, D:])
        mean_square = mm((keys * keys).astype(BF16), mean_ref[...])[:, : LATL * HEADS]
        scores = mm(keys.astype(BF16), query_ref[...])[:, : LATL * HEADS]
        scale = factor * lax.rsqrt(factor * factor * mean_square + head_eps)
        parts = by_level(jnp.exp2(scores * (scale * SCORE_SCALE)))
        inverse = 1.0 / (parts[0] + parts[1] + parts[2])
        factors = by_level(factor)
        weights = jnp.concatenate(
            [parts[l] * (inverse * factors[l]) for l in range(LEV)], axis=0
        ).astype(BF16)
        wide_weights = by_level(mm(weights, spread_ref[...]))
        pooled = []
        for j in range(LATL):
            terms = [wide_weights[l][:, j * D : (j + 1) * D] * values[l] for l in range(LEV)]
            pooled.append(terms[0] + terms[1] + terms[2])
        latents = mm(jnp.concatenate(pooled, axis=0).astype(BF16), pool_ref[...])
        latents = jnp.concatenate(
            [
                latents[j * PATCHES : (j + 1) * PATCHES] + entry(LATENT_ROW + j)
                for j in range(LATL)
            ],
            axis=0,
        )
        normed, factor = layer_norm(latents, entry(GAIN_ROW + 1), centred=True)
        wait(turn_index, 0)
        projected = mm(normed, qkv_ref[...])
        allowed = allowed_ref[...]
        if windows > 1:
            cut = jnp.where(pl.program_id(0) == windows - 1, 1.0, 0.0)
            allowed = 1.0 - cut * (1.0 - allowed)
        queries = jnp.concatenate([projected[:, :HALF], projected[:, HALF:D]], axis=0)
        mean_square = mm((queries * queries).astype(BF16), ones_ref[...])
        twice = jnp.concatenate([factor, factor], axis=0)
        query_scale = lax.rsqrt(twice * twice * mean_square + head_eps)
        query_scale = query_scale * (twice * SCORE_SCALE)
        win_keys = projected[:, D : 2 * D] * factor
        win_values = projected[:, 2 * D :] * factor
        mixed = []
        for pair in range(HEADS // 2):
            half, at = pair // 2, (pair % 2) * PAIR
            rows = slice(half * TOKENS, (half + 1) * TOKENS)
            query = queries[rows, at : at + PAIR].astype(BF16)
            key = win_keys[:, pair * PAIR : (pair + 1) * PAIR]
            value = win_values[:, pair * PAIR : (pair + 1) * PAIR]
            key = jnp.concatenate([jnp.where(low, key, 0.0), jnp.where(low, 0.0, key)], axis=0)
            value = jnp.concatenate(
                [jnp.where(low, value, 0.0), jnp.where(low, 0.0, value)], axis=0
            ).astype(BF16)
            key_square = mm_t(each, (key * key).astype(BF16))[:1]
            scale = query_scale[rows, at : at + PAIR] * lax.rsqrt(key_square + head_eps)
            weights = jnp.exp2(mm_t(query, key.astype(BF16)) * scale) * allowed
            both = mm(weights.astype(BF16), jnp.concatenate([value, half_ref[...]], axis=1))
            mixed.append((both[:, :PAIR] / both[:, PAIR:]).astype(BF16))
        wait(turn_index, 1)
        attended = latents + mm(jnp.concatenate(mixed, axis=1), proj_ref[...])
        normed, factor = layer_norm(attended, entry(GAIN_ROW + 2))
        wait(turn_index, 2)
        hidden = gelu(mm(normed, up_ref[...]) * factor).astype(BF16)
        wait(turn_index, 3)
        backbone = attended + mm(hidden, down_ref[...])
        first, second = backbone[:PATCHES], backbone[PATCHES:]
        blended = jnp.concatenate(
            [mixing(l, 0) * first + mixing(l, 1) * second + embed(l) for l in range(LEV)], axis=0
        )
        normed, factor = layer_norm(blended, entry(GAIN_ROW + 3))
        current = (current + mm(normed, dec_ref[...]) * factor).astype(BF16).astype(F32)

    for l in range(LEV):
        wide[:, l * PIN : (l + 1) * PIN] = current[l * PATCHES : (l + 1) * PATCHES]
    out_ref[0] = wide[...].reshape(out_ref.shape[1:]).astype(BF16)


def forecast(windows, arranged, early, late):
    vmem = pl.BlockSpec(memory_space=pltpu.VMEM)
    if windows == 1:
        block, grid = vmem, ()
        result = pltpu.VMEM(arranged.shape, BF16)
        arranged = pltpu.with_memory_space_constraint(arranged, pltpu.VMEM)
    else:
        result = jax.ShapeDtypeStruct(arranged.shape, BF16)
        block = pl.BlockSpec((1,) + arranged.shape[1:], lambda i: (i, 0, 0, 0))
        grid = (windows,)
    early = [pltpu.with_memory_space_constraint(a, pltpu.VMEM) for a in early]
    return pl.pallas_call(
        functools.partial(forecast_kernel, windows),
        grid=grid,
        in_specs=[vmem] * EARLY + [pl.BlockSpec(memory_space=pl.ANY)] * LATE + [block],
        out_specs=block,
        out_shape=result,
        scratch_shapes=[pltpu.VMEM(a.shape, a.dtype) for a in late]
        + [
            pltpu.VMEM((PATCHES, LEV * PIN), F32),
            pltpu.SemaphoreType.DMA((LATE,)),
        ],
        compiler_params=pltpu.CompilerParams(vmem_limit_bytes=MAIN_LIMIT),
    )(*early, *late, arranged)


def turn_kernel(step, direction, x_ref, out_ref, *token_ref):
    for ref in token_ref:
        ref[...] = jnp.zeros_like(ref)
    shift = jnp.where(lax.axis_index("lon") < step, 1, 0)
    if direction > 0:
        count = out_ref.shape[0]
        blocks = x_ref[...].astype(F32).reshape(out_ref.shape)
        for i in range(count):
            out_ref[lax.rem(i + count - shift, count)] = blocks[i].astype(BF16)
    else:
        count = x_ref.shape[0]
        blocks = [x_ref[lax.rem(i + count - shift, count)].astype(F32) for i in range(count)]
        out_ref[...] = jnp.stack(blocks).reshape(out_ref.shape).astype(BF16)


def turn(array, shape, step, direction, token=False):
    shapes = [jax.ShapeDtypeStruct(shape, BF16)]
    if token:
        shapes.append(jax.ShapeDtypeStruct((8, LANES), F32))
    return pl.pallas_call(
        functools.partial(turn_kernel, step, direction), out_shape=shapes
    )(array)


def shards(
    fields,
    level_ids,
    embed_weight,
    level_embed,
    enc_gain,
    latent_query,
    kv_weight,
    pool_out,
    attn_gain,
    qkv_weight,
    attn_proj,
    mlp_gain,
    mlp_up,
    mlp_down,
    level_mix,
    dec_gain,
    dec_weight,
):
    devices = lax.axis_size("lon")
    width = fields.shape[2]
    local_count = fields.shape[1]
    piece_cols = local_count // devices
    lat_count = devices // ROW_PARTS
    bands = lat_count // W_LAT
    cut = (W_LON // 2 // piece_cols) * lat_count
    scalars = (level_ids, level_mix.T)
    rows = (
        level_embed,
        latent_query,
        enc_gain.reshape(1, D),
        attn_gain.reshape(1, D),
        mlp_gain.reshape(1, D),
        dec_gain.reshape(1, D),
    )
    outgoing, token = turn(
        fields.reshape(local_count, width), (devices, piece_cols, width), cut, 1, token=True
    )
    early = load(token, scalars, rows, dec_weight.T, (embed_weight, kv_weight, pool_out))
    late = (qkv_weight, attn_proj, mlp_up, mlp_down)
    got = lax.all_to_all(outgoing, "lon", split_axis=0, concat_axis=0, tiled=True)
    if bands > 1:
        got = got.reshape(ROW_PARTS, lat_count, piece_cols, width)
        got = jnp.roll(got, -(W_LAT // 2), axis=1)
        got = got.reshape(ROW_PARTS, bands, W_LAT, piece_cols, width).transpose(1, 0, 2, 3, 4)
    done = forecast(bands, got.reshape(bands, ROW_PARTS * W_LAT, piece_cols, width), early, late)
    if bands > 1:
        done = done.reshape(bands, ROW_PARTS, W_LAT, piece_cols, width).transpose(1, 0, 2, 3, 4)
        done = done.reshape(ROW_PARTS, lat_count, piece_cols, width)
        done = jnp.roll(done, W_LAT // 2, axis=1)
    done = done.reshape(devices, piece_cols, width)
    home = lax.all_to_all(done, "lon", split_axis=0, concat_axis=0, tiled=True)
    (forecast_here,) = turn(home, (local_count, width), cut, -1)
    return forecast_here.reshape(fields.shape)


def solution(mesh):
    placed = (P(("groups", "lon"), None, None), P("groups")) + (P(),) * 15
    return jax.shard_map(
        shards,
        mesh=mesh,
        in_specs=placed,
        out_specs=P(("groups", "lon"), None, None),
        check_vma=False,
    )
```

```python
import functools
import math

import jax
import jax.numpy as jnp
from jax import lax
from jax.experimental import pallas as pl
from jax.experimental.pallas import tpu as pltpu
from jax.sharding import PartitionSpec as P

D = 512
HEADS = 8
HEAD_DIM = D // HEADS
PIN = 500
LEV = 3
LATL = 2
W_LAT = 4
W_LON = 8
STEPS = 2
ROW_PARTS = 4
MLP = 2048
PATCHES = W_LAT * W_LON
TOKENS = PATCHES * LATL
HALF = D // 2
PAIR = 2 * HEAD_DIM
EARLY, LATE = 11, 4
PARTS = 4
PART = MLP // PARTS
LANES = 128
LOAD_LIMIT = 56 * 1024 * 1024
MAIN_LIMIT = 56 * 1024 * 1024
EMBED_ROW, MIX_ROW, LATENT_ROW, GAIN_ROW, TABLE_ROWS = 0, 3, 9, 11, 16

GELU_FIRST = math.sqrt(2.0 / math.pi)
GELU_THIRD = 0.044715 * GELU_FIRST
SCORE_SCALE = HEAD_DIM ** (-0.5) * math.log2(math.e)

norm_eps = 1e-05
head_eps = 1e-06

F32 = jnp.float32
BF16 = jnp.bfloat16


def mm(a, b):
    return jnp.dot(a, b, preferred_element_type=F32)


def mm_t(a, b):
    return lax.dot_general(a, b, (((1,), (1,)), ((), ())), preferred_element_type=F32)


def layer_norm(values, gain, centred=False):
    if not centred:
        values = values - jnp.mean(values, axis=-1, keepdims=True)
    spread = jnp.mean(values * values, axis=-1, keepdims=True)
    return (values * gain).astype(BF16), lax.rsqrt(spread + norm_eps)


def centre(rows):
    return rows - jnp.mean(rows, axis=-1, keepdims=True)


def gelu(values):
    curve = values * (GELU_FIRST + GELU_THIRD * (values * values))
    half = 0.5 * values
    return half + half * jnp.tanh(curve)


def iota(shape, dim):
    return lax.broadcasted_iota(jnp.int32, shape, dim)


def load_kernel(*refs):
    (
        ids_from,
        mix_from,
        level_embed_from,
        latent_query_from,
        enc_gain_from,
        attn_gain_from,
        mlp_gain_from,
        dec_gain_from,
        dec_from,
        embed_from,
        kv_from,
        pool_from,
        _,
        table_ref,
        query_ref,
        mean_ref,
        spread_ref,
        ones_ref,
        half_ref,
        allowed_ref,
        dec_ref,
        embed_ref,
        kv_ref,
        pool_ref,
        ids_ref,
        mix_ref,
        level_embed_ref,
        latent_query_ref,
        gain_refs,
        dec_rows_ref,
        embed_rows_ref,
        pool_rows_ref,
        arrivals,
    ) = refs
    pairs = [
        (ids_from, ids_ref),
        (mix_from, mix_ref),
        (level_embed_from, level_embed_ref),
        (latent_query_from, latent_query_ref),
        (enc_gain_from, gain_refs.at[0]),
        (attn_gain_from, gain_refs.at[1]),
        (mlp_gain_from, gain_refs.at[2]),
        (dec_gain_from, gain_refs.at[3]),
        (dec_from, dec_rows_ref),
        (embed_from, embed_rows_ref),
        (pool_from, pool_rows_ref),
        (kv_from, kv_ref),
    ]
    copies = [
        pltpu.make_async_copy(here, there, arrivals.at[i]) for i, (here, there) in enumerate(pairs)
    ]
    for copy in copies:
        copy.start()

    feature_head = iota((D, LANES), 0) // HEAD_DIM
    lane = iota((D, LANES), 1)
    on_head = (feature_head == lane % HEADS) & (lane < LATL * HEADS)
    mean_ref[...] = jnp.where(on_head, 1.0 / HEAD_DIM, 0.0).astype(BF16)
    spread_ref[...] = jnp.where(
        iota((LATL * HEADS, LATL * D), 0) == iota((LATL * HEADS, LATL * D), 1) // HEAD_DIM, 1.0, 0.0
    ).astype(BF16)
    ones_ref[...] = jnp.where(
        iota((HALF, HALF), 0) // HEAD_DIM == iota((HALF, HALF), 1) // HEAD_DIM, 1.0 / HEAD_DIM, 0.0
    ).astype(BF16)
    half_ref[...] = jnp.where(
        (iota((PAIR, PAIR), 0) < HEAD_DIM) == (iota((PAIR, PAIR), 1) < HEAD_DIM), 1.0, 0.0
    ).astype(BF16)
    row_bit = (iota((TOKENS, PAIR), 0) // 4) % 2
    lane_bit = (iota((TOKENS, PAIR), 1) // 4) % 2
    allowed_ref[...] = jnp.where(row_bit == lane_bit, 1.0, 0.0)

    for copy in copies[:8]:
        copy.wait()
    level_embed = centre(level_embed_ref[...].astype(F32))
    for l in range(LEV):
        level = ids_ref[l]
        row = level_embed[LEV - 1 : LEV]
        for i in reversed(range(LEV - 1)):
            row = jnp.where(level == i, level_embed[i : i + 1], row)
        table_ref[EMBED_ROW + l : EMBED_ROW + l + 1, :] = row
        for j in range(LATL):
            at = MIX_ROW + l * LATL + j
            table_ref[at : at + 1, :] = jnp.full((1, D), mix_ref[j, level])
    latent = latent_query_ref[...].astype(F32)
    table_ref[LATENT_ROW : LATENT_ROW + LATL, :] = centre(latent)
    for i in range(4):
        table_ref[GAIN_ROW + i : GAIN_ROW + i + 1, :] = gain_refs[i]
    row_id = iota((LANES, D), 0)
    own_head = (row_id % HEADS) == iota((LANES, D), 1) // HEAD_DIM
    spots = jnp.zeros((LANES, D), F32)
    for j in range(LATL):
        mine = own_head & (row_id // HEADS == j)
        spots = jnp.where(mine, jnp.broadcast_to(latent[j : j + 1], (LANES, D)), spots)
    mean_square = jnp.sum(spots * spots, axis=-1, keepdims=True) / HEAD_DIM
    query_ref[...] = (spots * lax.rsqrt(mean_square + head_eps)).T.astype(BF16)

    copies[8].wait()
    dec_ref[...] = dec_rows_ref[...].astype(F32).T.astype(BF16)
    copies[9].wait()
    embed_ref[...] = centre(embed_rows_ref[...].astype(F32)).astype(BF16)
    copies[10].wait()
    pool_ref[...] = centre(pool_rows_ref[...].astype(F32)).astype(BF16)
    copies[11].wait()


def load(after, scalars, rows, dec, early):
    far = pl.BlockSpec(memory_space=pl.ANY)
    made = [
        pltpu.VMEM((TABLE_ROWS, D), F32),
        pltpu.VMEM((D, LANES), BF16),
        pltpu.VMEM((D, LANES), BF16),
        pltpu.VMEM((LATL * HEADS, LATL * D), BF16),
        pltpu.VMEM((HALF, HALF), BF16),
        pltpu.VMEM((PAIR, PAIR), BF16),
        pltpu.VMEM((TOKENS, PAIR), F32),
        pltpu.VMEM(dec.shape[::-1], BF16),
    ] + [pltpu.VMEM(a.shape, a.dtype) for a in early]
    inputs = (*scalars, *rows, dec, *early)
    return pl.pallas_call(
        load_kernel,
        in_specs=[far] * (len(inputs) + 1),
        out_specs=[pl.BlockSpec(memory_space=pltpu.VMEM)] * len(made),
        out_shape=made,
        scratch_shapes=[pltpu.SMEM(a.shape, a.dtype) for a in scalars]
        + [
            pltpu.VMEM((LEV, D), BF16),
            pltpu.VMEM((LATL, D), BF16),
            pltpu.VMEM((4, 1, D), F32),
            pltpu.VMEM(dec.shape, BF16),
            pltpu.VMEM(early[0].shape, BF16),
            pltpu.VMEM(early[2].shape, BF16),
            pltpu.SemaphoreType.DMA((len(inputs),)),
        ],
        compiler_params=pltpu.CompilerParams(vmem_limit_bytes=LOAD_LIMIT),
        cost_estimate=pl.CostEstimate(flops=0, bytes_accessed=8_000_000, transcendentals=0),
    )(*inputs, after)


def forecast_kernel(windows, *refs):
    (
        table_ref,
        query_ref,
        mean_ref,
        spread_ref,
        ones_ref,
        half_ref,
        allowed_ref,
        dec_ref,
        embed_ref,
        kv_ref,
        pool_ref,
    ) = refs[:EARLY]
    far, (x_ref, out_ref), refs = refs[EARLY:][:LATE], refs[EARLY + LATE :][:2], refs[EARLY + LATE + 2 :]
    near, (wide, arrivals) = refs[:LATE], refs[LATE:]
    qkv_ref, proj_ref, up_ref, down_ref = near
    moves = [(far[0], qkv_ref), (far[1], proj_ref)]
    for part in range(PARTS):
        units = pl.ds(part * PART, PART)
        moves.append((far[2].at[:, units], up_ref.at[:, units]))
        moves.append((far[3].at[units], down_ref.at[units]))
    copies = [
        pltpu.make_async_copy(here, there, arrivals.at[i])
        for i, (here, there) in enumerate(moves)
    ]

    def in_first_window(action):
        if windows == 1:
            action()
        else:
            pl.when(pl.program_id(0) == 0)(action)

    def start(*wanted):
        def action():
            for i in wanted:
                copies[i].start()

        in_first_window(action)

    def wait(turn_index, *wanted):
        def action():
            for i in wanted:
                copies[i].wait()

        if turn_index == 0:
            in_first_window(action)

    start(*range(len(copies)))

    def entry(at):
        return table_ref[at : at + 1, :]

    def embed(l):
        return entry(EMBED_ROW + l)

    def mixing(l, j):
        return entry(MIX_ROW + l * LATL + j)

    low = iota((1, PAIR), 1) < HEAD_DIM
    each = jnp.full((16, PAIR), 1.0 / HEAD_DIM, BF16)

    arrived = x_ref[0].reshape(PATCHES, LEV * PIN).astype(F32)
    current = jnp.concatenate(
        [arrived[:, l * PIN : (l + 1) * PIN] for l in range(LEV)], axis=0
    )

    def by_level(values):
        return [values[l * PATCHES : (l + 1) * PATCHES] for l in range(LEV)]

    for turn_index in range(STEPS):
        tokens = by_level(mm(current.astype(BF16), embed_ref[...]))
        tokens = jnp.concatenate([tokens[l] + embed(l) for l in range(LEV)], axis=0)
        tokens, factor = layer_norm(tokens, entry(GAIN_ROW), centred=True)
        keyval = mm(tokens, kv_ref[...])
        keys = keyval[:, :D]
        values = by_level(keyval[:, D:])
        mean_square = mm((keys * keys).astype(BF16), mean_ref[...])[:, : LATL * HEADS]
        scores = mm(keys.astype(BF16), query_ref[...])[:, : LATL * HEADS]
        scale = factor * lax.rsqrt(factor * factor * mean_square + head_eps)
        parts = by_level(jnp.exp2(scores * (scale * SCORE_SCALE)))
        inverse = 1.0 / (parts[0] + parts[1] + parts[2])
        factors = by_level(factor)
        weights = jnp.concatenate(
            [parts[l] * (inverse * factors[l]) for l in range(LEV)], axis=0
        ).astype(BF16)
        wide_weights = by_level(mm(weights, spread_ref[...]))
        pooled = []
        for j in range(LATL):
            terms = [wide_weights[l][:, j * D : (j + 1) * D] * values[l] for l in range(LEV)]
            pooled.append(terms[0] + terms[1] + terms[2])
        latents = mm(jnp.concatenate(pooled, axis=0).astype(BF16), pool_ref[...])
        latents = jnp.concatenate(
            [
                latents[j * PATCHES : (j + 1) * PATCHES] + entry(LATENT_ROW + j)
                for j in range(LATL)
            ],
            axis=0,
        )
        normed, factor = layer_norm(latents, entry(GAIN_ROW + 1), centred=True)
        wait(turn_index, 0)
        projected = mm(normed, qkv_ref[...])
        allowed = allowed_ref[...]
        if windows > 1:
            cut = jnp.where(pl.program_id(0) == windows - 1, 1.0, 0.0)
            allowed = 1.0 - cut * (1.0 - allowed)
        queries = jnp.concatenate([projected[:, :HALF], projected[:, HALF:D]], axis=0)
        mean_square = mm((queries * queries).astype(BF16), ones_ref[...])
        twice = jnp.concatenate([factor, factor], axis=0)
        query_scale = lax.rsqrt(twice * twice * mean_square + head_eps)
        query_scale = query_scale * (twice * SCORE_SCALE)
        win_keys = projected[:, D : 2 * D] * factor
        win_values = projected[:, 2 * D :] * factor
        mixed = []
        for pair in range(HEADS // 2):
            half, at = pair // 2, (pair % 2) * PAIR
            rows = slice(half * TOKENS, (half + 1) * TOKENS)
            query = queries[rows, at : at + PAIR].astype(BF16)
            key = win_keys[:, pair * PAIR : (pair + 1) * PAIR]
            value = win_values[:, pair * PAIR : (pair + 1) * PAIR]
            key = jnp.concatenate([jnp.where(low, key, 0.0), jnp.where(low, 0.0, key)], axis=0)
            value = jnp.concatenate(
                [jnp.where(low, value, 0.0), jnp.where(low, 0.0, value)], axis=0
            ).astype(BF16)
            key_square = mm_t(each, (key * key).astype(BF16))[:1]
            scale = query_scale[rows, at : at + PAIR] * lax.rsqrt(key_square + head_eps)
            weights = jnp.exp2(mm_t(query, key.astype(BF16)) * scale) * allowed
            both = mm(weights.astype(BF16), jnp.concatenate([value, half_ref[...]], axis=1))
            mixed.append((both[:, :PAIR] / both[:, PAIR:]).astype(BF16))
        wait(turn_index, 1)
        attended = latents + mm(jnp.concatenate(mixed, axis=1), proj_ref[...])
        normed, factor = layer_norm(attended, entry(GAIN_ROW + 2))
        backbone = attended
        for part in range(PARTS):
            units = slice(part * PART, (part + 1) * PART)
            wait(turn_index, 2 + 2 * part)
            hidden = gelu(mm(normed, up_ref[:, units]) * factor).astype(BF16)
            wait(turn_index, 3 + 2 * part)
            backbone = backbone + mm(hidden, down_ref[units, :])
        first, second = backbone[:PATCHES], backbone[PATCHES:]
        blended = jnp.concatenate(
            [mixing(l, 0) * first + mixing(l, 1) * second + embed(l) for l in range(LEV)], axis=0
        )
        normed, factor = layer_norm(blended, entry(GAIN_ROW + 3))
        current = (current + mm(normed, dec_ref[...]) * factor).astype(BF16).astype(F32)

    for l in range(LEV):
        wide[:, l * PIN : (l + 1) * PIN] = current[l * PATCHES : (l + 1) * PATCHES]
    out_ref[0] = wide[...].astype(BF16).reshape(out_ref.shape[1:])


def forecast(windows, arranged, early, late):
    vmem = pl.BlockSpec(memory_space=pltpu.VMEM)
    if windows == 1:
        block, grid = vmem, ()
        result = pltpu.VMEM(arranged.shape, BF16)
        arranged = pltpu.with_memory_space_constraint(arranged, pltpu.VMEM)
    else:
        result = jax.ShapeDtypeStruct(arranged.shape, BF16)
        block = pl.BlockSpec((1,) + arranged.shape[1:], lambda i: (i, 0, 0, 0))
        grid = (windows,)
    early = [pltpu.with_memory_space_constraint(a, pltpu.VMEM) for a in early]
    return pl.pallas_call(
        functools.partial(forecast_kernel, windows),
        grid=grid,
        in_specs=[vmem] * EARLY + [pl.BlockSpec(memory_space=pl.ANY)] * LATE + [block],
        out_specs=block,
        out_shape=result,
        scratch_shapes=[pltpu.VMEM(a.shape, a.dtype) for a in late]
        + [
            pltpu.VMEM((PATCHES, LEV * PIN), F32),
            pltpu.SemaphoreType.DMA((2 + 2 * PARTS,)),
        ],
        compiler_params=pltpu.CompilerParams(vmem_limit_bytes=MAIN_LIMIT),
    )(*early, *late, arranged)


def turn_kernel(step, direction, x_ref, out_ref, *token_ref):
    for ref in token_ref:
        ref[...] = jnp.zeros_like(ref)
    shift = jnp.where(lax.axis_index("lon") < step, 1, 0)
    if direction > 0:
        count = out_ref.shape[0]
        blocks = x_ref[...].reshape(out_ref.shape)
        for i in range(count):
            out_ref[lax.rem(i + count - shift, count)] = blocks[i]
    else:
        count = x_ref.shape[0]
        blocks = [x_ref[lax.rem(i + count - shift, count)] for i in range(count)]
        out_ref[...] = jnp.stack(blocks).reshape(out_ref.shape)


def turn(array, shape, step, direction, token=False):
    shapes = [jax.ShapeDtypeStruct(shape, BF16)]
    if token:
        shapes.append(jax.ShapeDtypeStruct((8, LANES), F32))
    return pl.pallas_call(
        functools.partial(turn_kernel, step, direction), out_shape=shapes
    )(array)


def shards(
    fields,
    level_ids,
    embed_weight,
    level_embed,
    enc_gain,
    latent_query,
    kv_weight,
    pool_out,
    attn_gain,
    qkv_weight,
    attn_proj,
    mlp_gain,
    mlp_up,
    mlp_down,
    level_mix,
    dec_gain,
    dec_weight,
):
    devices = lax.axis_size("lon")
    width = fields.shape[2]
    local_count = fields.shape[1]
    piece_cols = local_count // devices
    lat_count = devices // ROW_PARTS
    bands = lat_count // W_LAT
    cut = (W_LON // 2 // piece_cols) * lat_count
    scalars = (level_ids, level_mix.T)
    rows = (
        level_embed,
        latent_query,
        enc_gain.reshape(1, D),
        attn_gain.reshape(1, D),
        mlp_gain.reshape(1, D),
        dec_gain.reshape(1, D),
    )
    outgoing, token = turn(
        fields.reshape(local_count, width), (devices, piece_cols, width), cut, 1, token=True
    )
    early = load(token, scalars, rows, dec_weight.T, (embed_weight, kv_weight, pool_out))
    late = (qkv_weight, attn_proj, mlp_up, mlp_down)
    got = lax.all_to_all(outgoing, "lon", split_axis=0, concat_axis=0, tiled=True)
    if bands > 1:
        got = got.reshape(ROW_PARTS, lat_count, piece_cols, width)
        got = jnp.roll(got, -(W_LAT // 2), axis=1)
        got = got.reshape(ROW_PARTS, bands, W_LAT, piece_cols, width).transpose(1, 0, 2, 3, 4)
    done = forecast(bands, got.reshape(bands, ROW_PARTS * W_LAT, piece_cols, width), early, late)
    if bands > 1:
        done = done.reshape(bands, ROW_PARTS, W_LAT, piece_cols, width).transpose(1, 0, 2, 3, 4)
        done = done.reshape(ROW_PARTS, lat_count, piece_cols, width)
        done = jnp.roll(done, W_LAT // 2, axis=1)
    done = done.reshape(devices, piece_cols, width)
    home = lax.all_to_all(done, "lon", split_axis=0, concat_axis=0, tiled=True)
    (forecast_here,) = turn(home, (local_count, width), cut, -1)
    return forecast_here.reshape(fields.shape)


def solution(mesh):
    placed = (P(("groups", "lon"), None, None), P("groups")) + (P(),) * 15
    return jax.shard_map(
        shards,
        mesh=mesh,
        in_specs=placed,
        out_specs=P(("groups", "lon"), None, None),
        check_vma=False,
    )
```

```python
import functools
import math

import jax
import jax.numpy as jnp
from jax import lax
from jax.experimental import pallas as pl
from jax.experimental.pallas import tpu as pltpu
from jax.sharding import PartitionSpec as P

D = 512
HEADS = 8
HEAD_DIM = D // HEADS
PIN = 500
LEV = 3
LATL = 2
W_LAT = 4
W_LON = 8
STEPS = 2
ROW_PARTS = 4
MLP = 2048
PATCHES = W_LAT * W_LON
TOKENS = PATCHES * LATL
HALF = D // 2
PAIR = 2 * HEAD_DIM
EARLY, LATE = 11, 4
LANES = 128
LOAD_LIMIT = 56 * 1024 * 1024
MAIN_LIMIT = 56 * 1024 * 1024
EMBED_ROW, MIX_ROW, LATENT_ROW, GAIN_ROW, TABLE_ROWS = 0, 3, 9, 11, 16

GELU_FIRST = math.sqrt(2.0 / math.pi)
GELU_THIRD = 0.044715 * GELU_FIRST
SCORE_SCALE = HEAD_DIM ** (-0.5) * math.log2(math.e)

norm_eps = 1e-05
head_eps = 1e-06

F32 = jnp.float32
BF16 = jnp.bfloat16


def mm(a, b):
    return jnp.dot(a, b, preferred_element_type=F32)


def mm_t(a, b):
    return lax.dot_general(a, b, (((1,), (1,)), ((), ())), preferred_element_type=F32)


def layer_norm(values, gain, centred=False):
    if not centred:
        values = values - jnp.mean(values, axis=-1, keepdims=True)
    spread = jnp.mean(values * values, axis=-1, keepdims=True)
    return (values * gain).astype(BF16), lax.rsqrt(spread + norm_eps)


def centre(rows):
    return rows - jnp.mean(rows, axis=-1, keepdims=True)


def gelu(values):
    curve = values * (GELU_FIRST + GELU_THIRD * (values * values))
    half = 0.5 * values
    return half + half * jnp.tanh(curve)


def iota(shape, dim):
    return lax.broadcasted_iota(jnp.int32, shape, dim)


def load_kernel(*refs):
    (
        ids_from,
        mix_from,
        level_embed_from,
        latent_query_from,
        enc_gain_from,
        attn_gain_from,
        mlp_gain_from,
        dec_gain_from,
        dec_from,
        embed_from,
        kv_from,
        pool_from,
        _,
        table_ref,
        query_ref,
        mean_ref,
        spread_ref,
        ones_ref,
        half_ref,
        allowed_ref,
        dec_ref,
        embed_ref,
        kv_ref,
        pool_ref,
        ids_ref,
        mix_ref,
        level_embed_ref,
        latent_query_ref,
        gain_refs,
        dec_rows_ref,
        embed_rows_ref,
        pool_rows_ref,
        arrivals,
    ) = refs
    pairs = [
        (ids_from, ids_ref),
        (mix_from, mix_ref),
        (level_embed_from, level_embed_ref),
        (latent_query_from, latent_query_ref),
        (enc_gain_from, gain_refs.at[0]),
        (attn_gain_from, gain_refs.at[1]),
        (mlp_gain_from, gain_refs.at[2]),
        (dec_gain_from, gain_refs.at[3]),
        (dec_from, dec_rows_ref),
        (embed_from, embed_rows_ref),
        (pool_from, pool_rows_ref),
        (kv_from, kv_ref),
    ]
    copies = [
        pltpu.make_async_copy(here, there, arrivals.at[i]) for i, (here, there) in enumerate(pairs)
    ]
    for copy in copies:
        copy.start()

    feature_head = iota((D, LANES), 0) // HEAD_DIM
    lane = iota((D, LANES), 1)
    on_head = (feature_head == lane % HEADS) & (lane < LATL * HEADS)
    mean_ref[...] = jnp.where(on_head, 1.0 / HEAD_DIM, 0.0).astype(BF16)
    spread_ref[...] = jnp.where(
        iota((LATL * HEADS, LATL * D), 0) == iota((LATL * HEADS, LATL * D), 1) // HEAD_DIM, 1.0, 0.0
    ).astype(BF16)
    ones_ref[...] = jnp.where(
        iota((HALF, HALF), 0) // HEAD_DIM == iota((HALF, HALF), 1) // HEAD_DIM, 1.0 / HEAD_DIM, 0.0
    ).astype(BF16)
    half_ref[...] = jnp.where(
        (iota((PAIR, PAIR), 0) < HEAD_DIM) == (iota((PAIR, PAIR), 1) < HEAD_DIM), 1.0, 0.0
    ).astype(BF16)
    row_bit = (iota((TOKENS, PAIR), 0) // 4) % 2
    lane_bit = (iota((TOKENS, PAIR), 1) // 4) % 2
    allowed_ref[...] = jnp.where(row_bit == lane_bit, 1.0, 0.0)

    for copy in copies[:8]:
        copy.wait()
    level_embed = centre(level_embed_ref[...].astype(F32))
    for l in range(LEV):
        level = ids_ref[l]
        row = level_embed[LEV - 1 : LEV]
        for i in reversed(range(LEV - 1)):
            row = jnp.where(level == i, level_embed[i : i + 1], row)
        table_ref[EMBED_ROW + l : EMBED_ROW + l + 1, :] = row
        for j in range(LATL):
            at = MIX_ROW + l * LATL + j
            table_ref[at : at + 1, :] = jnp.full((1, D), mix_ref[j, level])
    latent = latent_query_ref[...].astype(F32)
    table_ref[LATENT_ROW : LATENT_ROW + LATL, :] = centre(latent)
    for i in range(4):
        table_ref[GAIN_ROW + i : GAIN_ROW + i + 1, :] = gain_refs[i]
    row_id = iota((LANES, D), 0)
    own_head = (row_id % HEADS) == iota((LANES, D), 1) // HEAD_DIM
    spots = jnp.zeros((LANES, D), F32)
    for j in range(LATL):
        mine = own_head & (row_id // HEADS == j)
        spots = jnp.where(mine, jnp.broadcast_to(latent[j : j + 1], (LANES, D)), spots)
    mean_square = jnp.sum(spots * spots, axis=-1, keepdims=True) / HEAD_DIM
    query_ref[...] = (spots * lax.rsqrt(mean_square + head_eps)).T.astype(BF16)

    copies[8].wait()
    dec_ref[...] = dec_rows_ref[...].astype(F32).T.astype(BF16)
    copies[9].wait()
    embed_ref[...] = centre(embed_rows_ref[...].astype(F32)).astype(BF16)
    copies[10].wait()
    pool_ref[...] = centre(pool_rows_ref[...].astype(F32)).astype(BF16)
    copies[11].wait()


def load(after, scalars, rows, dec, early):
    far = pl.BlockSpec(memory_space=pl.ANY)
    made = [
        pltpu.VMEM((TABLE_ROWS, D), F32),
        pltpu.VMEM((D, LANES), BF16),
        pltpu.VMEM((D, LANES), BF16),
        pltpu.VMEM((LATL * HEADS, LATL * D), BF16),
        pltpu.VMEM((HALF, HALF), BF16),
        pltpu.VMEM((PAIR, PAIR), BF16),
        pltpu.VMEM((TOKENS, PAIR), F32),
        pltpu.VMEM(dec.shape[::-1], BF16),
    ] + [pltpu.VMEM(a.shape, a.dtype) for a in early]
    inputs = (*scalars, *rows, dec, *early)
    return pl.pallas_call(
        load_kernel,
        in_specs=[far] * (len(inputs) + 1),
        out_specs=[pl.BlockSpec(memory_space=pltpu.VMEM)] * len(made),
        out_shape=made,
        scratch_shapes=[pltpu.SMEM(a.shape, a.dtype) for a in scalars]
        + [
            pltpu.VMEM((LEV, D), BF16),
            pltpu.VMEM((LATL, D), BF16),
            pltpu.VMEM((4, 1, D), F32),
            pltpu.VMEM(dec.shape, BF16),
            pltpu.VMEM(early[0].shape, BF16),
            pltpu.VMEM(early[2].shape, BF16),
            pltpu.SemaphoreType.DMA((len(inputs),)),
        ],
        compiler_params=pltpu.CompilerParams(vmem_limit_bytes=LOAD_LIMIT),
        cost_estimate=pl.CostEstimate(flops=0, bytes_accessed=8_000_000, transcendentals=0),
    )(*inputs, after)


def forecast_kernel(windows, *refs):
    (
        table_ref,
        query_ref,
        mean_ref,
        spread_ref,
        ones_ref,
        half_ref,
        allowed_ref,
        dec_ref,
        embed_ref,
        kv_ref,
        pool_ref,
    ) = refs[:EARLY]
    far, (x_ref, out_ref), refs = refs[EARLY:][:LATE], refs[EARLY + LATE :][:2], refs[EARLY + LATE + 2 :]
    near, (wide, arrivals) = refs[:LATE], refs[LATE:]
    qkv_ref, proj_ref, up_ref, down_ref = near
    copies = [
        pltpu.make_async_copy(far[i], near[i], arrivals.at[i]) for i in range(LATE)
    ]

    def in_first_window(action):
        if windows == 1:
            action()
        else:
            pl.when(pl.program_id(0) == 0)(action)

    def start(*wanted):
        def action():
            for i in wanted:
                copies[i].start()

        in_first_window(action)

    def wait(turn_index, *wanted):
        def action():
            for i in wanted:
                copies[i].wait()

        if turn_index == 0:
            in_first_window(action)

    start(0, 1, 2, 3)

    def entry(at):
        return table_ref[at : at + 1, :]

    def embed(l):
        return entry(EMBED_ROW + l)

    def mixing(l, j):
        return entry(MIX_ROW + l * LATL + j)

    low = iota((1, PAIR), 1) < HEAD_DIM
    each = jnp.full((16, PAIR), 1.0 / HEAD_DIM, BF16)

    arrived = x_ref[0].reshape(PATCHES, LEV * PIN).astype(F32)
    current = jnp.concatenate(
        [arrived[:, l * PIN : (l + 1) * PIN] for l in range(LEV)], axis=0
    )

    def by_level(values):
        return [values[l * PATCHES : (l + 1) * PATCHES] for l in range(LEV)]

    for turn_index in range(STEPS):
        tokens = by_level(mm(current.astype(BF16), embed_ref[...]))
        tokens = jnp.concatenate([tokens[l] + embed(l) for l in range(LEV)], axis=0)
        tokens, factor = layer_norm(tokens, entry(GAIN_ROW), centred=True)
        keyval = mm(tokens, kv_ref[...])
        keys = keyval[:, :D]
        values = by_level(keyval[:, D:])
        mean_square = mm((keys * keys).astype(BF16), mean_ref[...])[:, : LATL * HEADS]
        scores = mm(keys.astype(BF16), query_ref[...])[:, : LATL * HEADS]
        scale = factor * lax.rsqrt(factor * factor * mean_square + head_eps)
        parts = by_level(jnp.exp2(scores * (scale * SCORE_SCALE)))
        inverse = 1.0 / (parts[0] + parts[1] + parts[2])
        factors = by_level(factor)
        weights = jnp.concatenate(
            [parts[l] * (inverse * factors[l]) for l in range(LEV)], axis=0
        ).astype(BF16)
        wide_weights = by_level(mm(weights, spread_ref[...]))
        pooled = []
        for j in range(LATL):
            terms = [wide_weights[l][:, j * D : (j + 1) * D] * values[l] for l in range(LEV)]
            pooled.append(terms[0] + terms[1] + terms[2])
        latents = mm(jnp.concatenate(pooled, axis=0).astype(BF16), pool_ref[...])
        latents = jnp.concatenate(
            [
                latents[j * PATCHES : (j + 1) * PATCHES] + entry(LATENT_ROW + j)
                for j in range(LATL)
            ],
            axis=0,
        )
        normed, factor = layer_norm(latents, entry(GAIN_ROW + 1), centred=True)
        wait(turn_index, 0, 1)
        projected = mm(normed, qkv_ref[...])
        allowed = allowed_ref[...]
        if windows > 1:
            cut = jnp.where(pl.program_id(0) == windows - 1, 1.0, 0.0)
            allowed = 1.0 - cut * (1.0 - allowed)
        queries = jnp.concatenate([projected[:, :HALF], projected[:, HALF:D]], axis=0)
        mean_square = mm((queries * queries).astype(BF16), ones_ref[...])
        twice = jnp.concatenate([factor, factor], axis=0)
        query_scale = lax.rsqrt(twice * twice * mean_square + head_eps)
        query_scale = query_scale * (twice * SCORE_SCALE)
        win_keys = projected[:, D : 2 * D] * factor
        win_values = projected[:, 2 * D :] * factor
        mixed = []
        for pair in range(HEADS // 2):
            half, at = pair // 2, (pair % 2) * PAIR
            rows = slice(half * TOKENS, (half + 1) * TOKENS)
            query = queries[rows, at : at + PAIR].astype(BF16)
            key = win_keys[:, pair * PAIR : (pair + 1) * PAIR]
            value = win_values[:, pair * PAIR : (pair + 1) * PAIR]
            key = jnp.concatenate([jnp.where(low, key, 0.0), jnp.where(low, 0.0, key)], axis=0)
            value = jnp.concatenate(
                [jnp.where(low, value, 0.0), jnp.where(low, 0.0, value)], axis=0
            ).astype(BF16)
            key_square = mm_t(each, (key * key).astype(BF16))[:1]
            scale = query_scale[rows, at : at + PAIR] * lax.rsqrt(key_square + head_eps)
            weights = jnp.exp2(mm_t(query, key.astype(BF16)) * scale) * allowed
            both = mm(weights.astype(BF16), jnp.concatenate([value, half_ref[...]], axis=1))
            mixed.append((both[:, :PAIR] / both[:, PAIR:]).astype(BF16))
        attended = latents + mm(jnp.concatenate(mixed, axis=1), proj_ref[...])
        normed, factor = layer_norm(attended, entry(GAIN_ROW + 2))
        wait(turn_index, 2, 3)
        hidden = gelu(mm(normed, up_ref[...]) * factor).astype(BF16)
        backbone = attended + mm(hidden, down_ref[...])
        first, second = backbone[:PATCHES], backbone[PATCHES:]
        blended = jnp.concatenate(
            [mixing(l, 0) * first + mixing(l, 1) * second + embed(l) for l in range(LEV)], axis=0
        )
        normed, factor = layer_norm(blended, entry(GAIN_ROW + 3))
        current = (current + mm(normed, dec_ref[...]) * factor).astype(BF16).astype(F32)

    for l in range(LEV):
        wide[:, l * PIN : (l + 1) * PIN] = current[l * PATCHES : (l + 1) * PATCHES]
    out_ref[0] = wide[...].astype(BF16).reshape(out_ref.shape[1:])


def forecast(windows, arranged, early, late):
    vmem = pl.BlockSpec(memory_space=pltpu.VMEM)
    if windows == 1:
        block, grid = vmem, ()
        result = pltpu.VMEM(arranged.shape, BF16)
        arranged = pltpu.with_memory_space_constraint(arranged, pltpu.VMEM)
    else:
        result = jax.ShapeDtypeStruct(arranged.shape, BF16)
        block = pl.BlockSpec((1,) + arranged.shape[1:], lambda i: (i, 0, 0, 0))
        grid = (windows,)
    early = [pltpu.with_memory_space_constraint(a, pltpu.VMEM) for a in early]
    return pl.pallas_call(
        functools.partial(forecast_kernel, windows),
        grid=grid,
        in_specs=[vmem] * EARLY + [pl.BlockSpec(memory_space=pl.ANY)] * LATE + [block],
        out_specs=block,
        out_shape=result,
        scratch_shapes=[pltpu.VMEM(a.shape, a.dtype) for a in late]
        + [
            pltpu.VMEM((PATCHES, LEV * PIN), F32),
            pltpu.SemaphoreType.DMA((LATE,)),
        ],
        compiler_params=pltpu.CompilerParams(vmem_limit_bytes=MAIN_LIMIT),
    )(*early, *late, arranged)


def turn_kernel(step, direction, x_ref, out_ref, *token_ref):
    for ref in token_ref:
        ref[...] = jnp.zeros_like(ref)
    shift = jnp.where(lax.axis_index("lon") < step, 1, 0)
    if direction > 0:
        count = out_ref.shape[0]
        blocks = x_ref[...].reshape(out_ref.shape)
        for i in range(count):
            out_ref[lax.rem(i + count - shift, count)] = blocks[i]
    else:
        count = x_ref.shape[0]
        blocks = [x_ref[lax.rem(i + count - shift, count)] for i in range(count)]
        out_ref[...] = jnp.stack(blocks).reshape(out_ref.shape)


def turn(array, shape, step, direction, token=False):
    shapes = [jax.ShapeDtypeStruct(shape, BF16)]
    if token:
        shapes.append(jax.ShapeDtypeStruct((8, LANES), F32))
    return pl.pallas_call(
        functools.partial(turn_kernel, step, direction), out_shape=shapes
    )(array)


def shards(
    fields,
    level_ids,
    embed_weight,
    level_embed,
    enc_gain,
    latent_query,
    kv_weight,
    pool_out,
    attn_gain,
    qkv_weight,
    attn_proj,
    mlp_gain,
    mlp_up,
    mlp_down,
    level_mix,
    dec_gain,
    dec_weight,
):
    devices = lax.axis_size("lon")
    width = fields.shape[2]
    local_count = fields.shape[1]
    piece_cols = local_count // devices
    lat_count = devices // ROW_PARTS
    bands = lat_count // W_LAT
    cut = (W_LON // 2 // piece_cols) * lat_count
    scalars = (level_ids, level_mix.T)
    rows = (
        level_embed,
        latent_query,
        enc_gain.reshape(1, D),
        attn_gain.reshape(1, D),
        mlp_gain.reshape(1, D),
        dec_gain.reshape(1, D),
    )
    outgoing, token = turn(
        fields.reshape(local_count, width), (devices, piece_cols, width), cut, 1, token=True
    )
    early = load(token, scalars, rows, dec_weight.T, (embed_weight, kv_weight, pool_out))
    late = (qkv_weight, attn_proj, mlp_up, mlp_down)
    got = lax.all_to_all(outgoing, "lon", split_axis=0, concat_axis=0, tiled=True)
    if bands > 1:
        got = got.reshape(ROW_PARTS, lat_count, piece_cols, width)
        got = jnp.roll(got, -(W_LAT // 2), axis=1)
        got = got.reshape(ROW_PARTS, bands, W_LAT, piece_cols, width).transpose(1, 0, 2, 3, 4)
    done = forecast(bands, got.reshape(bands, ROW_PARTS * W_LAT, piece_cols, width), early, late)
    if bands > 1:
        done = done.reshape(bands, ROW_PARTS, W_LAT, piece_cols, width).transpose(1, 0, 2, 3, 4)
        done = done.reshape(ROW_PARTS, lat_count, piece_cols, width)
        done = jnp.roll(done, W_LAT // 2, axis=1)
    done = done.reshape(devices, piece_cols, width)
    home = lax.all_to_all(done, "lon", split_axis=0, concat_axis=0, tiled=True)
    (forecast_here,) = turn(home, (local_count, width), cut, -1)
    return forecast_here.reshape(fields.shape)


def solution(mesh):
    placed = (P(("groups", "lon"), None, None), P("groups")) + (P(),) * 15
    return jax.shard_map(
        shards,
        mesh=mesh,
        in_specs=placed,
        out_specs=P(("groups", "lon"), None, None),
        check_vma=False,
    )
```

```python
import functools
import math

import jax
import jax.numpy as jnp
from jax import lax
from jax.experimental import pallas as pl
from jax.experimental.pallas import tpu as pltpu
from jax.sharding import PartitionSpec as P

D = 512
HEADS = 8
HEAD_DIM = D // HEADS
PIN = 500
LEV = 3
LATL = 2
W_LAT = 4
W_LON = 8
STEPS = 2
ROW_PARTS = 4
MLP = 2048
PATCHES = W_LAT * W_LON
TOKENS = PATCHES * LATL
HALF = D // 2
PAIR = 2 * HEAD_DIM
EARLY, LATE = 10, 4
LANES = 128
LOAD_LIMIT = 56 * 1024 * 1024
MAIN_LIMIT = 56 * 1024 * 1024
EMBED_ROW, MIX_ROW, LATENT_ROW, GAIN_ROW, TABLE_ROWS = 0, 3, 9, 11, 16

GELU_FIRST = math.sqrt(2.0 / math.pi)
GELU_THIRD = 0.044715 * GELU_FIRST
SCORE_SCALE = HEAD_DIM ** (-0.5) * math.log2(math.e)

norm_eps = 1e-05
head_eps = 1e-06

F32 = jnp.float32
BF16 = jnp.bfloat16


def mm(a, b):
    return jnp.dot(a, b, preferred_element_type=F32)


def mm_t(a, b):
    return lax.dot_general(a, b, (((1,), (1,)), ((), ())), preferred_element_type=F32)


def row_factor(centred):
    return lax.rsqrt(jnp.mean(centred * centred, axis=-1, keepdims=True) + norm_eps)


def centre(rows):
    return rows - jnp.mean(rows, axis=-1, keepdims=True)


def gelu(values):
    curve = values * (GELU_FIRST + GELU_THIRD * (values * values))
    half = 0.5 * values
    return half + half * jnp.tanh(curve)


def iota(shape, dim):
    return lax.broadcasted_iota(jnp.int32, shape, dim)


def load_kernel(*refs):
    (
        ids_from,
        mix_from,
        level_embed_from,
        latent_query_from,
        enc_gain_from,
        attn_gain_from,
        mlp_gain_from,
        dec_gain_from,
        dec_from,
        embed_from,
        kv_from,
        pool_from,
        _,
        table_ref,
        query_ref,
        mean_ref,
        spread_ref,
        ones_ref,
        allowed_ref,
        dec_ref,
        embed_ref,
        kv_ref,
        pool_ref,
        ids_ref,
        mix_ref,
        level_embed_ref,
        latent_query_ref,
        gain_refs,
        dec_rows_ref,
        embed_rows_ref,
        pool_rows_ref,
        arrivals,
    ) = refs
    pairs = [
        (ids_from, ids_ref),
        (mix_from, mix_ref),
        (level_embed_from, level_embed_ref),
        (latent_query_from, latent_query_ref),
        (enc_gain_from, gain_refs.at[0]),
        (attn_gain_from, gain_refs.at[1]),
        (mlp_gain_from, gain_refs.at[2]),
        (dec_gain_from, gain_refs.at[3]),
        (dec_from, dec_rows_ref),
        (embed_from, embed_rows_ref),
        (pool_from, pool_rows_ref),
        (kv_from, kv_ref),
    ]
    copies = [
        pltpu.make_async_copy(here, there, arrivals.at[i]) for i, (here, there) in enumerate(pairs)
    ]
    for copy in copies:
        copy.start()

    feature_head = iota((D, LANES), 0) // HEAD_DIM
    lane = iota((D, LANES), 1)
    on_head = (feature_head == lane % HEADS) & (lane < LATL * HEADS)
    mean_ref[...] = jnp.where(on_head, 1.0 / HEAD_DIM, 0.0).astype(BF16)
    spread_ref[...] = jnp.where(
        iota((LATL * HEADS, LATL * D), 0) == iota((LATL * HEADS, LATL * D), 1) // HEAD_DIM, 1.0, 0.0
    ).astype(BF16)
    ones_ref[...] = jnp.where(
        iota((HALF, HALF), 0) // HEAD_DIM == iota((HALF, HALF), 1) // HEAD_DIM, 1.0 / HEAD_DIM, 0.0
    ).astype(BF16)
    row_bit = (iota((TOKENS, PAIR), 0) // 4) % 2
    lane_bit = (iota((TOKENS, PAIR), 1) // 4) % 2
    allowed_ref[...] = jnp.where(row_bit == lane_bit, 1.0, 0.0)

    for copy in copies[:8]:
        copy.wait()
    level_embed = centre(level_embed_ref[...].astype(F32))
    for l in range(LEV):
        level = ids_ref[l]
        row = level_embed[LEV - 1 : LEV]
        for i in reversed(range(LEV - 1)):
            row = jnp.where(level == i, level_embed[i : i + 1], row)
        table_ref[EMBED_ROW + l : EMBED_ROW + l + 1, :] = row
        for j in range(LATL):
            at = MIX_ROW + l * LATL + j
            table_ref[at : at + 1, :] = jnp.full((1, D), mix_ref[j, level])
    latent = latent_query_ref[...].astype(F32)
    table_ref[LATENT_ROW : LATENT_ROW + LATL, :] = centre(latent)
    for i in range(4):
        table_ref[GAIN_ROW + i : GAIN_ROW + i + 1, :] = gain_refs[i]
    row_id = iota((LANES, D), 0)
    own_head = (row_id % HEADS) == iota((LANES, D), 1) // HEAD_DIM
    spots = jnp.zeros((LANES, D), F32)
    for j in range(LATL):
        mine = own_head & (row_id // HEADS == j)
        spots = jnp.where(mine, jnp.broadcast_to(latent[j : j + 1], (LANES, D)), spots)
    mean_square = jnp.sum(spots * spots, axis=-1, keepdims=True) / HEAD_DIM
    query_ref[...] = (spots * lax.rsqrt(mean_square + head_eps)).T.astype(BF16)

    copies[8].wait()
    dec_ref[...] = dec_rows_ref[...].astype(F32).T.astype(BF16)
    copies[9].wait()
    embed_ref[...] = centre(embed_rows_ref[...].astype(F32)).astype(BF16)
    copies[10].wait()
    pool_ref[...] = centre(pool_rows_ref[...].astype(F32)).astype(BF16)
    copies[11].wait()


def load(after, scalars, rows, dec, early):
    far = pl.BlockSpec(memory_space=pl.ANY)
    made = [
        pltpu.VMEM((TABLE_ROWS, D), F32),
        pltpu.VMEM((D, LANES), BF16),
        pltpu.VMEM((D, LANES), BF16),
        pltpu.VMEM((LATL * HEADS, LATL * D), BF16),
        pltpu.VMEM((HALF, HALF), BF16),
        pltpu.VMEM((TOKENS, PAIR), F32),
        pltpu.VMEM(dec.shape[::-1], BF16),
    ] + [pltpu.VMEM(a.shape, a.dtype) for a in early]
    inputs = (*scalars, *rows, dec, *early)
    return pl.pallas_call(
        load_kernel,
        in_specs=[far] * (len(inputs) + 1),
        out_specs=[pl.BlockSpec(memory_space=pltpu.VMEM)] * len(made),
        out_shape=made,
        scratch_shapes=[pltpu.SMEM(a.shape, a.dtype) for a in scalars]
        + [
            pltpu.VMEM((LEV, D), BF16),
            pltpu.VMEM((LATL, D), BF16),
            pltpu.VMEM((4, 1, D), F32),
            pltpu.VMEM(dec.shape, BF16),
            pltpu.VMEM(early[0].shape, BF16),
            pltpu.VMEM(early[2].shape, BF16),
            pltpu.SemaphoreType.DMA((len(inputs),)),
        ],
        compiler_params=pltpu.CompilerParams(vmem_limit_bytes=LOAD_LIMIT),
        cost_estimate=pl.CostEstimate(flops=0, bytes_accessed=8_000_000, transcendentals=0),
    )(*inputs, after)


def forecast_kernel(windows, *refs):
    (
        table_ref,
        query_ref,
        mean_ref,
        spread_ref,
        ones_ref,
        allowed_ref,
        dec_ref,
        embed_ref,
        kv_ref,
        pool_ref,
    ) = refs[:EARLY]
    far, (x_ref, out_ref), refs = refs[EARLY:][:LATE], refs[EARLY + LATE :][:2], refs[EARLY + LATE + 2 :]
    near, (wide, arrivals) = refs[:LATE], refs[LATE:]
    qkv_ref, proj_ref, up_ref, down_ref = near
    copies = [
        pltpu.make_async_copy(far[i], near[i], arrivals.at[i]) for i in range(LATE)
    ]

    def in_first_window(action):
        if windows == 1:
            action()
        else:
            pl.when(pl.program_id(0) == 0)(action)

    def start(*wanted):
        def action():
            for i in wanted:
                copies[i].start()

        in_first_window(action)

    def wait(turn_index, *wanted):
        def action():
            for i in wanted:
                copies[i].wait()

        if turn_index == 0:
            in_first_window(action)

    start(0, 1, 2, 3)

    def entry(at):
        return table_ref[at : at + 1, :]

    def embed(l):
        return entry(EMBED_ROW + l)

    def mixing(l, j):
        return entry(MIX_ROW + l * LATL + j)

    half_head = iota((1, HALF), 1) // HEAD_DIM
    each = jnp.full((16, HALF), 1.0 / HEAD_DIM, BF16)

    arrived = x_ref[0].reshape(PATCHES, LEV * PIN).astype(F32)
    current = jnp.concatenate(
        [arrived[:, l * PIN : (l + 1) * PIN] for l in range(LEV)], axis=0
    )

    def by_level(values):
        return [values[l * PATCHES : (l + 1) * PATCHES] for l in range(LEV)]

    for turn_index in range(STEPS):
        tokens = by_level(mm(current.astype(BF16), embed_ref[...]))
        tokens = jnp.concatenate([tokens[l] + embed(l) for l in range(LEV)], axis=0)
        keyval = mm((tokens * entry(GAIN_ROW)).astype(BF16), kv_ref[...])
        factor = row_factor(tokens)
        keys = keyval[:, :D]
        values = by_level(keyval[:, D:])
        scores = mm(keys.astype(BF16), query_ref[...])[:, : LATL * HEADS]
        mean_square = mm((keys * keys).astype(BF16), mean_ref[...])[:, : LATL * HEADS]
        scale = factor * lax.rsqrt(factor * factor * mean_square + head_eps)
        parts = by_level(jnp.exp2(scores * (scale * SCORE_SCALE)))
        inverse = 1.0 / (parts[0] + parts[1] + parts[2])
        factors = by_level(factor)
        weights = jnp.concatenate(
            [parts[l] * (inverse * factors[l]) for l in range(LEV)], axis=0
        ).astype(BF16)
        wide_weights = by_level(mm(weights, spread_ref[...]))
        pooled = []
        for j in range(LATL):
            terms = [wide_weights[l][:, j * D : (j + 1) * D] * values[l] for l in range(LEV)]
            pooled.append(terms[0] + terms[1] + terms[2])
        latents = mm(jnp.concatenate(pooled, axis=0).astype(BF16), pool_ref[...])
        latents = jnp.concatenate(
            [
                latents[j * PATCHES : (j + 1) * PATCHES] + entry(LATENT_ROW + j)
                for j in range(LATL)
            ],
            axis=0,
        )
        wait(turn_index, 0, 1)
        projected = mm((latents * entry(GAIN_ROW + 1)).astype(BF16), qkv_ref[...])
        factor = row_factor(latents)
        allowed = allowed_ref[...]
        if windows > 1:
            cut = jnp.where(pl.program_id(0) == windows - 1, 1.0, 0.0)
            allowed = 1.0 - cut * (1.0 - allowed)
        allowed = jnp.concatenate([allowed, allowed], axis=1)
        win_queries = projected[:, :D]
        win_keys = projected[:, D : 2 * D] * factor
        win_values = projected[:, 2 * D :] * (factor * (1.0 / HEAD_DIM))
        halves = [slice(i * HALF, (i + 1) * HALF) for i in range(2)]

        def apart(rows):
            return jnp.concatenate(
                [jnp.where(half_head == h, rows, 0.0) for h in range(HEADS // 2)], axis=0
            )

        keys = [apart(win_keys[:, half]) for half in halves]
        scores = [
            mm_t(win_queries[:, half].astype(BF16), key.astype(BF16))
            for half, key in zip(halves, keys)
        ]
        queries = jnp.concatenate([win_queries[:, half] for half in halves], axis=0)
        query_square = mm((queries * queries).astype(BF16), ones_ref[...])
        key_squares = [mm_t(each, (key * key).astype(BF16))[:1] for key in keys]
        values = [
            jnp.concatenate([apart(win_values[:, half]).astype(BF16), ones_ref[...]], axis=1)
            for half in halves
        ]
        weights = []
        for i in range(2):
            square = query_square[i * TOKENS : (i + 1) * TOKENS]
            scale = lax.rsqrt(factor * factor * square + head_eps) * (factor * SCORE_SCALE)
            scale = scale * lax.rsqrt(key_squares[i] + head_eps)
            weights.append((jnp.exp2(scores[i] * scale) * allowed).astype(BF16))
        both = [mm(weights[i], values[i]) for i in range(2)]
        mixed = [(each_both[:, :HALF] / each_both[:, HALF:]).astype(BF16) for each_both in both]
        attended = latents + mm(jnp.concatenate(mixed, axis=1), proj_ref[...])
        wait(turn_index, 2, 3)
        centred = centre(attended)
        hidden = mm((centred * entry(GAIN_ROW + 2)).astype(BF16), up_ref[...])
        hidden = gelu(hidden * row_factor(centred)).astype(BF16)
        backbone = attended + mm(hidden, down_ref[...])
        first, second = backbone[:PATCHES], backbone[PATCHES:]
        blended = jnp.concatenate(
            [mixing(l, 0) * first + mixing(l, 1) * second + embed(l) for l in range(LEV)], axis=0
        )
        centred = centre(blended)
        added = mm((centred * entry(GAIN_ROW + 3)).astype(BF16), dec_ref[...])
        current = (current + added * row_factor(centred)).astype(BF16).astype(F32)

    for l in range(LEV):
        wide[:, l * PIN : (l + 1) * PIN] = current[l * PATCHES : (l + 1) * PATCHES]
    out_ref[0] = wide[...].astype(BF16).reshape(out_ref.shape[1:])


def forecast(windows, arranged, early, late):
    vmem = pl.BlockSpec(memory_space=pltpu.VMEM)
    if windows == 1:
        block, grid = vmem, ()
        result = pltpu.VMEM(arranged.shape, BF16)
        arranged = pltpu.with_memory_space_constraint(arranged, pltpu.VMEM)
    else:
        result = jax.ShapeDtypeStruct(arranged.shape, BF16)
        block = pl.BlockSpec((1,) + arranged.shape[1:], lambda i: (i, 0, 0, 0))
        grid = (windows,)
    early = [pltpu.with_memory_space_constraint(a, pltpu.VMEM) for a in early]
    return pl.pallas_call(
        functools.partial(forecast_kernel, windows),
        grid=grid,
        in_specs=[vmem] * EARLY + [pl.BlockSpec(memory_space=pl.ANY)] * LATE + [block],
        out_specs=block,
        out_shape=result,
        scratch_shapes=[pltpu.VMEM(a.shape, a.dtype) for a in late]
        + [
            pltpu.VMEM((PATCHES, LEV * PIN), F32),
            pltpu.SemaphoreType.DMA((LATE,)),
        ],
        compiler_params=pltpu.CompilerParams(vmem_limit_bytes=MAIN_LIMIT),
    )(*early, *late, arranged)


def turn_kernel(step, direction, x_ref, out_ref, *token_ref):
    for ref in token_ref:
        ref[...] = jnp.zeros_like(ref)
    shift = jnp.where(lax.axis_index("lon") < step, 1, 0)
    if direction > 0:
        count = out_ref.shape[0]
        blocks = x_ref[...].reshape(out_ref.shape)
        for i in range(count):
            out_ref[lax.rem(i + count - shift, count)] = blocks[i]
    else:
        count = x_ref.shape[0]
        blocks = [x_ref[lax.rem(i + count - shift, count)] for i in range(count)]
        out_ref[...] = jnp.stack(blocks).reshape(out_ref.shape)


def turn(array, shape, step, direction, token=False):
    shapes = [jax.ShapeDtypeStruct(shape, BF16)]
    if token:
        shapes.append(jax.ShapeDtypeStruct((8, LANES), F32))
    return pl.pallas_call(
        functools.partial(turn_kernel, step, direction), out_shape=shapes
    )(array)


def shards(
    fields,
    level_ids,
    embed_weight,
    level_embed,
    enc_gain,
    latent_query,
    kv_weight,
    pool_out,
    attn_gain,
    qkv_weight,
    attn_proj,
    mlp_gain,
    mlp_up,
    mlp_down,
    level_mix,
    dec_gain,
    dec_weight,
):
    devices = lax.axis_size("lon")
    width = fields.shape[2]
    local_count = fields.shape[1]
    piece_cols = local_count // devices
    lat_count = devices // ROW_PARTS
    bands = lat_count // W_LAT
    cut = (W_LON // 2 // piece_cols) * lat_count
    scalars = (level_ids, level_mix.T)
    rows = (
        level_embed,
        latent_query,
        enc_gain.reshape(1, D),
        attn_gain.reshape(1, D),
        mlp_gain.reshape(1, D),
        dec_gain.reshape(1, D),
    )
    outgoing, token = turn(
        fields.reshape(local_count, width), (devices, piece_cols, width), cut, 1, token=True
    )
    early = load(token, scalars, rows, dec_weight.T, (embed_weight, kv_weight, pool_out))
    late = (qkv_weight, attn_proj, mlp_up, mlp_down)
    got = lax.all_to_all(outgoing, "lon", split_axis=0, concat_axis=0, tiled=True)
    if bands > 1:
        got = got.reshape(ROW_PARTS, lat_count, piece_cols, width)
        got = jnp.roll(got, -(W_LAT // 2), axis=1)
        got = got.reshape(ROW_PARTS, bands, W_LAT, piece_cols, width).transpose(1, 0, 2, 3, 4)
    done = forecast(bands, got.reshape(bands, ROW_PARTS * W_LAT, piece_cols, width), early, late)
    if bands > 1:
        done = done.reshape(bands, ROW_PARTS, W_LAT, piece_cols, width).transpose(1, 0, 2, 3, 4)
        done = done.reshape(ROW_PARTS, lat_count, piece_cols, width)
        done = jnp.roll(done, W_LAT // 2, axis=1)
    done = done.reshape(devices, piece_cols, width)
    home = lax.all_to_all(done, "lon", split_axis=0, concat_axis=0, tiled=True)
    (forecast_here,) = turn(home, (local_count, width), cut, -1)
    return forecast_here.reshape(fields.shape)


def solution(mesh):
    placed = (P(("groups", "lon"), None, None), P("groups")) + (P(),) * 15
    return jax.shard_map(
        shards,
        mesh=mesh,
        in_specs=placed,
        out_specs=P(("groups", "lon"), None, None),
        check_vma=False,
    )
```

```python
import functools
import math

import jax
import jax.numpy as jnp
from jax import lax
from jax.experimental import pallas as pl
from jax.experimental.pallas import tpu as pltpu
from jax.sharding import PartitionSpec as P

D = 512
HEADS = 8
HEAD_DIM = D // HEADS
PIN = 500
LEV = 3
LATL = 2
W_LAT = 4
W_LON = 8
STEPS = 2
ROW_PARTS = 4
MLP = 2048
PATCHES = W_LAT * W_LON
TOKENS = PATCHES * LATL
HALF = D // 2
PAIR = 2 * HEAD_DIM
EARLY, LATE = 10, 4
LANES = 128
LOAD_LIMIT = 56 * 1024 * 1024
TURN_LIMIT = 16 * 1024 * 1024
MAIN_LIMIT = 56 * 1024 * 1024
EMBED_ROW, MIX_ROW, LATENT_ROW, GAIN_ROW, TABLE_ROWS = 0, 3, 9, 11, 16

GELU_FIRST = math.sqrt(2.0 / math.pi)
GELU_THIRD = 0.044715 * GELU_FIRST
SCORE_SCALE = HEAD_DIM ** (-0.5) * math.log2(math.e)

norm_eps = 1e-05
head_eps = 1e-06

F32 = jnp.float32
BF16 = jnp.bfloat16


def mm(a, b):
    return jnp.dot(a, b, preferred_element_type=F32)


def mm_t(a, b):
    return lax.dot_general(a, b, (((1,), (1,)), ((), ())), preferred_element_type=F32)


def row_factor(centred):
    return lax.rsqrt(jnp.mean(centred * centred, axis=-1, keepdims=True) + norm_eps)


def centre(rows):
    return rows - jnp.mean(rows, axis=-1, keepdims=True)


def gelu(values):
    curve = values * (GELU_FIRST + GELU_THIRD * (values * values))
    half = 0.5 * values
    return half + half * jnp.tanh(curve)


def iota(shape, dim):
    return lax.broadcasted_iota(jnp.int32, shape, dim)


def load_kernel(*refs):
    (
        ids_from,
        mix_from,
        level_embed_from,
        latent_query_from,
        enc_gain_from,
        attn_gain_from,
        mlp_gain_from,
        dec_gain_from,
        dec_from,
        embed_from,
        kv_from,
        pool_from,
        _,
        table_ref,
        query_ref,
        mean_ref,
        spread_ref,
        ones_ref,
        allowed_ref,
        dec_ref,
        embed_ref,
        kv_ref,
        pool_ref,
        ids_ref,
        mix_ref,
        level_embed_ref,
        latent_query_ref,
        gain_refs,
        dec_rows_ref,
        embed_rows_ref,
        pool_rows_ref,
        arrivals,
    ) = refs
    pairs = [
        (ids_from, ids_ref),
        (mix_from, mix_ref),
        (level_embed_from, level_embed_ref),
        (latent_query_from, latent_query_ref),
        (enc_gain_from, gain_refs.at[0]),
        (attn_gain_from, gain_refs.at[1]),
        (mlp_gain_from, gain_refs.at[2]),
        (dec_gain_from, gain_refs.at[3]),
        (dec_from, dec_rows_ref),
        (embed_from, embed_rows_ref),
        (pool_from, pool_rows_ref),
        (kv_from, kv_ref),
    ]
    copies = [
        pltpu.make_async_copy(here, there, arrivals.at[i]) for i, (here, there) in enumerate(pairs)
    ]
    for copy in copies:
        copy.start()

    feature_head = iota((D, LANES), 0) // HEAD_DIM
    lane = iota((D, LANES), 1)
    on_head = (feature_head == lane % HEADS) & (lane < LATL * HEADS)
    mean_ref[...] = jnp.where(on_head, 1.0 / HEAD_DIM, 0.0).astype(BF16)
    spread_ref[...] = jnp.where(
        iota((LATL * HEADS, LATL * D), 0) == iota((LATL * HEADS, LATL * D), 1) // HEAD_DIM, 1.0, 0.0
    ).astype(BF16)
    ones_ref[...] = jnp.where(
        iota((HALF, HALF), 0) // HEAD_DIM == iota((HALF, HALF), 1) // HEAD_DIM, 1.0 / HEAD_DIM, 0.0
    ).astype(BF16)
    row_bit = (iota((TOKENS, PAIR), 0) // 4) % 2
    lane_bit = (iota((TOKENS, PAIR), 1) // 4) % 2
    allowed_ref[...] = jnp.where(row_bit == lane_bit, 1.0, 0.0)

    for copy in copies[:8]:
        copy.wait()
    level_embed = centre(level_embed_ref[...].astype(F32))
    for l in range(LEV):
        level = ids_ref[l]
        row = level_embed[LEV - 1 : LEV]
        for i in reversed(range(LEV - 1)):
            row = jnp.where(level == i, level_embed[i : i + 1], row)
        table_ref[EMBED_ROW + l : EMBED_ROW + l + 1, :] = row
        for j in range(LATL):
            at = MIX_ROW + l * LATL + j
            table_ref[at : at + 1, :] = jnp.full((1, D), mix_ref[j, level])
    latent = latent_query_ref[...].astype(F32)
    table_ref[LATENT_ROW : LATENT_ROW + LATL, :] = centre(latent)
    for i in range(4):
        table_ref[GAIN_ROW + i : GAIN_ROW + i + 1, :] = gain_refs[i]
    row_id = iota((LANES, D), 0)
    own_head = (row_id % HEADS) == iota((LANES, D), 1) // HEAD_DIM
    spots = jnp.zeros((LANES, D), F32)
    for j in range(LATL):
        mine = own_head & (row_id // HEADS == j)
        spots = jnp.where(mine, jnp.broadcast_to(latent[j : j + 1], (LANES, D)), spots)
    mean_square = jnp.sum(spots * spots, axis=-1, keepdims=True) / HEAD_DIM
    query_ref[...] = (spots * lax.rsqrt(mean_square + head_eps)).T.astype(BF16)

    copies[8].wait()
    dec_ref[...] = dec_rows_ref[...].astype(F32).T.astype(BF16)
    copies[9].wait()
    embed_ref[...] = centre(embed_rows_ref[...].astype(F32)).astype(BF16)
    copies[10].wait()
    pool_ref[...] = centre(pool_rows_ref[...].astype(F32)).astype(BF16)
    copies[11].wait()


def load(after, scalars, rows, dec, early):
    far = pl.BlockSpec(memory_space=pl.ANY)
    made = [
        pltpu.VMEM((TABLE_ROWS, D), F32),
        pltpu.VMEM((D, LANES), BF16),
        pltpu.VMEM((D, LANES), BF16),
        pltpu.VMEM((LATL * HEADS, LATL * D), BF16),
        pltpu.VMEM((HALF, HALF), BF16),
        pltpu.VMEM((TOKENS, PAIR), F32),
        pltpu.VMEM(dec.shape[::-1], BF16),
    ] + [pltpu.VMEM(a.shape, a.dtype) for a in early]
    inputs = (*scalars, *rows, dec, *early)
    return pl.pallas_call(
        load_kernel,
        in_specs=[far] * len(inputs) + [pl.BlockSpec(memory_space=pltpu.VMEM)],
        out_specs=[pl.BlockSpec(memory_space=pltpu.VMEM)] * len(made),
        out_shape=made,
        scratch_shapes=[pltpu.SMEM(a.shape, a.dtype) for a in scalars]
        + [
            pltpu.VMEM((LEV, D), BF16),
            pltpu.VMEM((LATL, D), BF16),
            pltpu.VMEM((4, 1, D), F32),
            pltpu.VMEM(dec.shape, BF16),
            pltpu.VMEM(early[0].shape, BF16),
            pltpu.VMEM(early[2].shape, BF16),
            pltpu.SemaphoreType.DMA((len(inputs),)),
        ],
        compiler_params=pltpu.CompilerParams(vmem_limit_bytes=LOAD_LIMIT),
        cost_estimate=pl.CostEstimate(flops=0, bytes_accessed=8_000_000, transcendentals=0),
    )(*inputs, pltpu.with_memory_space_constraint(after, pltpu.VMEM))


def forecast_kernel(windows, *refs):
    (
        table_ref,
        query_ref,
        mean_ref,
        spread_ref,
        ones_ref,
        allowed_ref,
        dec_ref,
        embed_ref,
        kv_ref,
        pool_ref,
    ) = refs[:EARLY]
    far, (x_ref, out_ref), refs = refs[EARLY:][:LATE], refs[EARLY + LATE :][:2], refs[EARLY + LATE + 2 :]
    near, (wide, arrivals) = refs[:LATE], refs[LATE:]
    qkv_ref, proj_ref, up_ref, down_ref = near
    copies = [
        pltpu.make_async_copy(far[i], near[i], arrivals.at[i]) for i in range(LATE)
    ]

    def in_first_window(action):
        if windows == 1:
            action()
        else:
            pl.when(pl.program_id(0) == 0)(action)

    def start(*wanted):
        def action():
            for i in wanted:
                copies[i].start()

        in_first_window(action)

    def wait(turn_index, *wanted):
        def action():
            for i in wanted:
                copies[i].wait()

        if turn_index == 0:
            in_first_window(action)

    start(0, 1, 2, 3)

    def entry(at):
        return table_ref[at : at + 1, :]

    def embed(l):
        return entry(EMBED_ROW + l)

    def mixing(l, j):
        return entry(MIX_ROW + l * LATL + j)

    half_head = iota((1, HALF), 1) // HEAD_DIM
    each = jnp.full((16, HALF), 1.0 / HEAD_DIM, BF16)

    arrived = x_ref[0].reshape(PATCHES, LEV * PIN).astype(F32)
    current = jnp.concatenate(
        [arrived[:, l * PIN : (l + 1) * PIN] for l in range(LEV)], axis=0
    )

    def by_level(values):
        return [values[l * PATCHES : (l + 1) * PATCHES] for l in range(LEV)]

    for turn_index in range(STEPS):
        tokens = by_level(mm(current.astype(BF16), embed_ref[...]))
        tokens = jnp.concatenate([tokens[l] + embed(l) for l in range(LEV)], axis=0)
        keyval = mm((tokens * entry(GAIN_ROW)).astype(BF16), kv_ref[...])
        factor = row_factor(tokens)
        keys = keyval[:, :D]
        values = by_level(keyval[:, D:])
        scores = mm(keys.astype(BF16), query_ref[...])[:, : LATL * HEADS]
        mean_square = mm((keys * keys).astype(BF16), mean_ref[...])[:, : LATL * HEADS]
        scale = factor * lax.rsqrt(factor * factor * mean_square + head_eps)
        parts = by_level(jnp.exp2(scores * (scale * SCORE_SCALE)))
        inverse = 1.0 / (parts[0] + parts[1] + parts[2])
        factors = by_level(factor)
        weights = jnp.concatenate(
            [parts[l] * (inverse * factors[l]) for l in range(LEV)], axis=0
        ).astype(BF16)
        wide_weights = by_level(mm(weights, spread_ref[...]))
        pooled = []
        for j in range(LATL):
            terms = [wide_weights[l][:, j * D : (j + 1) * D] * values[l] for l in range(LEV)]
            pooled.append(terms[0] + terms[1] + terms[2])
        latents = mm(jnp.concatenate(pooled, axis=0).astype(BF16), pool_ref[...])
        latents = jnp.concatenate(
            [
                latents[j * PATCHES : (j + 1) * PATCHES] + entry(LATENT_ROW + j)
                for j in range(LATL)
            ],
            axis=0,
        )
        wait(turn_index, 0, 1)
        projected = mm((latents * entry(GAIN_ROW + 1)).astype(BF16), qkv_ref[...])
        factor = row_factor(latents)
        allowed = allowed_ref[...]
        if windows > 1:
            cut = jnp.where(pl.program_id(0) == windows - 1, 1.0, 0.0)
            allowed = 1.0 - cut * (1.0 - allowed)
        allowed = jnp.concatenate([allowed, allowed], axis=1)
        win_queries = projected[:, :D]
        win_keys = projected[:, D : 2 * D] * factor
        win_values = projected[:, 2 * D :] * (factor * (1.0 / HEAD_DIM))
        halves = [slice(i * HALF, (i + 1) * HALF) for i in range(2)]

        def apart(rows):
            return jnp.concatenate(
                [jnp.where(half_head == h, rows, 0.0) for h in range(HEADS // 2)], axis=0
            )

        keys = [apart(win_keys[:, half]) for half in halves]
        scores = [
            mm_t(win_queries[:, half].astype(BF16), key.astype(BF16))
            for half, key in zip(halves, keys)
        ]
        queries = jnp.concatenate([win_queries[:, half] for half in halves], axis=0)
        query_square = mm((queries * queries).astype(BF16), ones_ref[...])
        key_squares = [mm_t(each, (key * key).astype(BF16))[:1] for key in keys]
        values = [
            jnp.concatenate([apart(win_values[:, half]).astype(BF16), ones_ref[...]], axis=1)
            for half in halves
        ]
        weights = []
        for i in range(2):
            square = query_square[i * TOKENS : (i + 1) * TOKENS]
            scale = lax.rsqrt(factor * factor * square + head_eps) * (factor * SCORE_SCALE)
            scale = scale * lax.rsqrt(key_squares[i] + head_eps)
            weights.append((jnp.exp2(scores[i] * scale) * allowed).astype(BF16))
        both = [mm(weights[i], values[i]) for i in range(2)]
        mixed = [(each_both[:, :HALF] / each_both[:, HALF:]).astype(BF16) for each_both in both]
        attended = latents + mm(jnp.concatenate(mixed, axis=1), proj_ref[...])
        wait(turn_index, 2)
        centred = centre(attended)
        hidden = mm((centred * entry(GAIN_ROW + 2)).astype(BF16), up_ref[...])
        hidden = gelu(hidden * row_factor(centred)).astype(BF16)
        wait(turn_index, 3)
        backbone = attended + mm(hidden, down_ref[...])
        first, second = backbone[:PATCHES], backbone[PATCHES:]
        blended = jnp.concatenate(
            [mixing(l, 0) * first + mixing(l, 1) * second + embed(l) for l in range(LEV)], axis=0
        )
        centred = centre(blended)
        added = mm((centred * entry(GAIN_ROW + 3)).astype(BF16), dec_ref[...])
        current = (current + added * row_factor(centred)).astype(BF16).astype(F32)

    for l in range(LEV):
        wide[:, l * PIN : (l + 1) * PIN] = current[l * PATCHES : (l + 1) * PATCHES]
    out_ref[0] = wide[...].astype(BF16).reshape(out_ref.shape[1:])


def forecast(windows, arranged, early, late):
    vmem = pl.BlockSpec(memory_space=pltpu.VMEM)
    if windows == 1:
        block, grid = vmem, ()
        result = pltpu.VMEM(arranged.shape, BF16)
        arranged = pltpu.with_memory_space_constraint(arranged, pltpu.VMEM)
    else:
        result = jax.ShapeDtypeStruct(arranged.shape, BF16)
        block = pl.BlockSpec((1,) + arranged.shape[1:], lambda i: (i, 0, 0, 0))
        grid = (windows,)
    early = [pltpu.with_memory_space_constraint(a, pltpu.VMEM) for a in early]
    return pl.pallas_call(
        functools.partial(forecast_kernel, windows),
        grid=grid,
        in_specs=[vmem] * EARLY + [pl.BlockSpec(memory_space=pl.ANY)] * LATE + [block],
        out_specs=block,
        out_shape=result,
        scratch_shapes=[pltpu.VMEM(a.shape, a.dtype) for a in late]
        + [
            pltpu.VMEM((PATCHES, LEV * PIN), F32),
            pltpu.SemaphoreType.DMA((LATE,)),
        ],
        compiler_params=pltpu.CompilerParams(vmem_limit_bytes=MAIN_LIMIT),
    )(*early, *late, arranged)


def turn_kernel(step, direction, x_ref, out_ref, *token_ref):
    for ref in token_ref:
        ref[...] = jnp.zeros_like(ref)
    shift = jnp.where(lax.axis_index("lon") < step, 1, 0)
    if direction > 0:
        count = out_ref.shape[0]
        blocks = x_ref[...].reshape(out_ref.shape)
        for i in range(count):
            out_ref[lax.rem(i + count - shift, count)] = blocks[i]
    else:
        count = x_ref.shape[0]
        blocks = [x_ref[lax.rem(i + count - shift, count)] for i in range(count)]
        out_ref[...] = jnp.stack(blocks).reshape(out_ref.shape)


def turn(array, shape, step, direction, near=False, token=False):
    if near and not token:
        array = pltpu.with_memory_space_constraint(array, pltpu.VMEM)
    held = near and token
    shapes = [pltpu.VMEM(shape, BF16) if held else jax.ShapeDtypeStruct(shape, BF16)]
    if token:
        shapes.append(pltpu.VMEM((8, LANES), F32))
    return pl.pallas_call(
        functools.partial(turn_kernel, step, direction),
        out_shape=shapes,
        compiler_params=pltpu.CompilerParams(vmem_limit_bytes=TURN_LIMIT),
    )(array)


def shards(
    fields,
    level_ids,
    embed_weight,
    level_embed,
    enc_gain,
    latent_query,
    kv_weight,
    pool_out,
    attn_gain,
    qkv_weight,
    attn_proj,
    mlp_gain,
    mlp_up,
    mlp_down,
    level_mix,
    dec_gain,
    dec_weight,
):
    devices = lax.axis_size("lon")
    width = fields.shape[2]
    local_count = fields.shape[1]
    piece_cols = local_count // devices
    lat_count = devices // ROW_PARTS
    bands = lat_count // W_LAT
    cut = (W_LON // 2 // piece_cols) * lat_count
    scalars = (level_ids, level_mix.T)
    rows = (
        level_embed,
        latent_query,
        enc_gain.reshape(1, D),
        attn_gain.reshape(1, D),
        mlp_gain.reshape(1, D),
        dec_gain.reshape(1, D),
    )
    outgoing, token = turn(
        fields.reshape(local_count, width), (devices, piece_cols, width), cut, 1, bands == 1, token=True
    )
    early = load(token, scalars, rows, dec_weight.T, (embed_weight, kv_weight, pool_out))
    late = (qkv_weight, attn_proj, mlp_up, mlp_down)
    got = lax.all_to_all(outgoing, "lon", split_axis=0, concat_axis=0, tiled=True)
    if bands > 1:
        got = got.reshape(ROW_PARTS, lat_count, piece_cols, width)
        got = jnp.roll(got, -(W_LAT // 2), axis=1)
        got = got.reshape(ROW_PARTS, bands, W_LAT, piece_cols, width).transpose(1, 0, 2, 3, 4)
    done = forecast(bands, got.reshape(bands, ROW_PARTS * W_LAT, piece_cols, width), early, late)
    if bands > 1:
        done = done.reshape(bands, ROW_PARTS, W_LAT, piece_cols, width).transpose(1, 0, 2, 3, 4)
        done = done.reshape(ROW_PARTS, lat_count, piece_cols, width)
        done = jnp.roll(done, W_LAT // 2, axis=1)
    done = done.reshape(devices, piece_cols, width)
    home = lax.all_to_all(done, "lon", split_axis=0, concat_axis=0, tiled=True)
    (forecast_here,) = turn(home, (local_count, width), cut, -1, bands == 1)
    return forecast_here.reshape(fields.shape)


def solution(mesh):
    placed = (P(("groups", "lon"), None, None), P("groups")) + (P(),) * 15
    return jax.shard_map(
        shards,
        mesh=mesh,
        in_specs=placed,
        out_specs=P(("groups", "lon"), None, None),
        check_vma=False,
    )
```

```python
import functools
import math

import jax
import jax.numpy as jnp
from jax import lax
from jax.experimental import pallas as pl
from jax.experimental.pallas import tpu as pltpu
from jax.sharding import PartitionSpec as P

D = 512
HEADS = 8
HEAD_DIM = D // HEADS
PIN = 500
LEV = 3
LATL = 2
W_LAT = 4
W_LON = 8
STEPS = 2
ROW_PARTS = 4
MLP = 2048
PATCHES = W_LAT * W_LON
TOKENS = PATCHES * LATL
HALF = D // 2
PAIR = 2 * HEAD_DIM
EARLY, LATE = 10, 4
LANES = 128
LOAD_LIMIT = 56 * 1024 * 1024
TURN_LIMIT = 16 * 1024 * 1024
MAIN_LIMIT = 56 * 1024 * 1024
EMBED_ROW, MIX_ROW, LATENT_ROW, GAIN_ROW, TABLE_ROWS = 0, 3, 9, 11, 16

GELU_FIRST = math.sqrt(2.0 / math.pi)
GELU_THIRD = 0.044715 * GELU_FIRST
SCORE_SCALE = HEAD_DIM ** (-0.5) * math.log2(math.e)

norm_eps = 1e-05
head_eps = 1e-06

F32 = jnp.float32
BF16 = jnp.bfloat16


def mm(a, b):
    return jnp.dot(a, b, preferred_element_type=F32)


def mm_t(a, b):
    return lax.dot_general(a, b, (((1,), (1,)), ((), ())), preferred_element_type=F32)


def row_factor(centred):
    return lax.rsqrt(jnp.mean(centred * centred, axis=-1, keepdims=True) + norm_eps)


def centre(rows):
    return rows - jnp.mean(rows, axis=-1, keepdims=True)


def gelu(values):
    curve = values * (GELU_FIRST + GELU_THIRD * (values * values))
    half = 0.5 * values
    return half + half * jnp.tanh(curve)


def iota(shape, dim):
    return lax.broadcasted_iota(jnp.int32, shape, dim)


def load_kernel(*refs):
    (
        ids_from,
        mix_from,
        level_embed_from,
        latent_query_from,
        enc_gain_from,
        attn_gain_from,
        mlp_gain_from,
        dec_gain_from,
        dec_from,
        embed_from,
        kv_from,
        pool_from,
        _,
        table_ref,
        query_ref,
        mean_ref,
        spread_ref,
        ones_ref,
        allowed_ref,
        dec_ref,
        embed_ref,
        kv_ref,
        pool_ref,
        ids_ref,
        mix_ref,
        level_embed_ref,
        latent_query_ref,
        gain_refs,
        dec_rows_ref,
        embed_rows_ref,
        pool_rows_ref,
        arrivals,
    ) = refs
    pairs = [
        (ids_from, ids_ref),
        (mix_from, mix_ref),
        (level_embed_from, level_embed_ref),
        (latent_query_from, latent_query_ref),
        (enc_gain_from, gain_refs.at[0]),
        (attn_gain_from, gain_refs.at[1]),
        (mlp_gain_from, gain_refs.at[2]),
        (dec_gain_from, gain_refs.at[3]),
        (dec_from, dec_rows_ref),
        (embed_from, embed_rows_ref),
        (pool_from, pool_rows_ref),
        (kv_from, kv_ref),
    ]
    copies = [
        pltpu.make_async_copy(here, there, arrivals.at[i]) for i, (here, there) in enumerate(pairs)
    ]
    for copy in copies:
        copy.start()

    feature_head = iota((D, LANES), 0) // HEAD_DIM
    lane = iota((D, LANES), 1)
    on_head = (feature_head == lane % HEADS) & (lane < LATL * HEADS)
    mean_ref[...] = jnp.where(on_head, 1.0 / HEAD_DIM, 0.0).astype(BF16)
    spread_ref[...] = jnp.where(
        iota((LATL * HEADS, LATL * D), 0) == iota((LATL * HEADS, LATL * D), 1) // HEAD_DIM, 1.0, 0.0
    ).astype(BF16)
    ones_ref[...] = jnp.where(
        iota((HALF, HALF), 0) // HEAD_DIM == iota((HALF, HALF), 1) // HEAD_DIM, 1.0 / HEAD_DIM, 0.0
    ).astype(BF16)
    row_bit = (iota((TOKENS, PAIR), 0) // 4) % 2
    lane_bit = (iota((TOKENS, PAIR), 1) // 4) % 2
    allowed_ref[...] = jnp.where(row_bit == lane_bit, 1.0, 0.0)

    for copy in copies[:8]:
        copy.wait()
    level_embed = centre(level_embed_ref[...].astype(F32))
    for l in range(LEV):
        level = ids_ref[l]
        row = level_embed[LEV - 1 : LEV]
        for i in reversed(range(LEV - 1)):
            row = jnp.where(level == i, level_embed[i : i + 1], row)
        table_ref[EMBED_ROW + l : EMBED_ROW + l + 1, :] = row
        for j in range(LATL):
            at = MIX_ROW + l * LATL + j
            table_ref[at : at + 1, :] = jnp.full((1, D), mix_ref[j, level])
    latent = latent_query_ref[...].astype(F32)
    table_ref[LATENT_ROW : LATENT_ROW + LATL, :] = centre(latent)
    for i in range(4):
        table_ref[GAIN_ROW + i : GAIN_ROW + i + 1, :] = gain_refs[i]
    row_id = iota((LANES, D), 0)
    own_head = (row_id % HEADS) == iota((LANES, D), 1) // HEAD_DIM
    spots = jnp.zeros((LANES, D), F32)
    for j in range(LATL):
        mine = own_head & (row_id // HEADS == j)
        spots = jnp.where(mine, jnp.broadcast_to(latent[j : j + 1], (LANES, D)), spots)
    mean_square = jnp.sum(spots * spots, axis=-1, keepdims=True) / HEAD_DIM
    query_ref[...] = (spots * lax.rsqrt(mean_square + head_eps)).T.astype(BF16)

    copies[8].wait()
    dec_ref[...] = dec_rows_ref[...].astype(F32).T.astype(BF16)
    copies[9].wait()
    embed_ref[...] = centre(embed_rows_ref[...].astype(F32)).astype(BF16)
    copies[10].wait()
    pool_ref[...] = centre(pool_rows_ref[...].astype(F32)).astype(BF16)
    copies[11].wait()


def load(after, scalars, rows, dec, early):
    far = pl.BlockSpec(memory_space=pl.ANY)
    made = [
        pltpu.VMEM((TABLE_ROWS, D), F32),
        pltpu.VMEM((D, LANES), BF16),
        pltpu.VMEM((D, LANES), BF16),
        pltpu.VMEM((LATL * HEADS, LATL * D), BF16),
        pltpu.VMEM((HALF, HALF), BF16),
        pltpu.VMEM((TOKENS, PAIR), F32),
        pltpu.VMEM(dec.shape[::-1], BF16),
    ] + [pltpu.VMEM(a.shape, a.dtype) for a in early]
    inputs = (*scalars, *rows, dec, *early)
    return pl.pallas_call(
        load_kernel,
        in_specs=[far] * len(inputs) + [pl.BlockSpec(memory_space=pltpu.VMEM)],
        out_specs=[pl.BlockSpec(memory_space=pltpu.VMEM)] * len(made),
        out_shape=made,
        scratch_shapes=[pltpu.SMEM(a.shape, a.dtype) for a in scalars]
        + [
            pltpu.VMEM((LEV, D), BF16),
            pltpu.VMEM((LATL, D), BF16),
            pltpu.VMEM((4, 1, D), F32),
            pltpu.VMEM(dec.shape, BF16),
            pltpu.VMEM(early[0].shape, BF16),
            pltpu.VMEM(early[2].shape, BF16),
            pltpu.SemaphoreType.DMA((len(inputs),)),
        ],
        compiler_params=pltpu.CompilerParams(vmem_limit_bytes=LOAD_LIMIT),
        cost_estimate=pl.CostEstimate(flops=0, bytes_accessed=8_000_000, transcendentals=0),
    )(*inputs, pltpu.with_memory_space_constraint(after, pltpu.VMEM))


def forecast_kernel(windows, *refs):
    (
        table_ref,
        query_ref,
        mean_ref,
        spread_ref,
        ones_ref,
        allowed_ref,
        dec_ref,
        embed_ref,
        kv_ref,
        pool_ref,
    ) = refs[:EARLY]
    far, (x_ref, out_ref), refs = refs[EARLY:][:LATE], refs[EARLY + LATE :][:2], refs[EARLY + LATE + 2 :]
    near, (wide, arrivals) = refs[:LATE], refs[LATE:]
    qkv_ref, proj_ref, up_ref, down_ref = near
    copies = [
        pltpu.make_async_copy(far[i], near[i], arrivals.at[i]) for i in range(LATE)
    ]

    def in_first_window(action):
        if windows == 1:
            action()
        else:
            pl.when(pl.program_id(0) == 0)(action)

    def start(*wanted):
        def action():
            for i in wanted:
                copies[i].start()

        in_first_window(action)

    def wait(turn_index, *wanted):
        def action():
            for i in wanted:
                copies[i].wait()

        if turn_index == 0:
            in_first_window(action)

    start(0, 1, 2, 3)

    def entry(at):
        return table_ref[at : at + 1, :]

    def embed(l):
        return entry(EMBED_ROW + l)

    def mixing(l, j):
        return entry(MIX_ROW + l * LATL + j)

    half_head = iota((1, HALF), 1) // HEAD_DIM
    each = jnp.full((16, HALF), 1.0 / HEAD_DIM, BF16)

    arrived = x_ref[0].reshape(PATCHES, LEV * PIN).astype(F32)
    current = jnp.concatenate(
        [arrived[:, l * PIN : (l + 1) * PIN] for l in range(LEV)], axis=0
    )

    def by_level(values):
        return [values[l * PATCHES : (l + 1) * PATCHES] for l in range(LEV)]

    for turn_index in range(STEPS):
        tokens = by_level(mm(current.astype(BF16), embed_ref[...]))
        tokens = jnp.concatenate([tokens[l] + embed(l) for l in range(LEV)], axis=0)
        keyval = mm((tokens * entry(GAIN_ROW)).astype(BF16), kv_ref[...])
        factor = row_factor(tokens)
        keys = keyval[:, :D]
        values = by_level(keyval[:, D:])
        scores = mm(keys.astype(BF16), query_ref[...])[:, : LATL * HEADS]
        mean_square = mm((keys * keys).astype(BF16), mean_ref[...])[:, : LATL * HEADS]
        scale = factor * lax.rsqrt(factor * factor * mean_square + head_eps)
        parts = by_level(jnp.exp2(scores * (scale * SCORE_SCALE)))
        inverse = 1.0 / (parts[0] + parts[1] + parts[2])
        factors = by_level(factor)
        weights = jnp.concatenate(
            [parts[l] * (inverse * factors[l]) for l in range(LEV)], axis=0
        ).astype(BF16)
        wide_weights = by_level(mm(weights, spread_ref[...]))
        pooled = []
        for j in range(LATL):
            terms = [wide_weights[l][:, j * D : (j + 1) * D] * values[l] for l in range(LEV)]
            pooled.append(terms[0] + terms[1] + terms[2])
        latents = mm(jnp.concatenate(pooled, axis=0).astype(BF16), pool_ref[...])
        latents = jnp.concatenate(
            [
                latents[j * PATCHES : (j + 1) * PATCHES] + entry(LATENT_ROW + j)
                for j in range(LATL)
            ],
            axis=0,
        )
        wait(turn_index, 0)
        projected = mm((latents * entry(GAIN_ROW + 1)).astype(BF16), qkv_ref[...])
        factor = row_factor(latents)
        allowed = allowed_ref[...]
        if windows > 1:
            cut = jnp.where(pl.program_id(0) == windows - 1, 1.0, 0.0)
            allowed = 1.0 - cut * (1.0 - allowed)
        allowed = jnp.concatenate([allowed, allowed], axis=1)
        win_queries = projected[:, :D]
        win_keys = projected[:, D : 2 * D] * factor
        win_values = projected[:, 2 * D :] * (factor * (1.0 / HEAD_DIM))
        halves = [slice(i * HALF, (i + 1) * HALF) for i in range(2)]

        def apart(rows):
            return jnp.concatenate(
                [jnp.where(half_head == h, rows, 0.0) for h in range(HEADS // 2)], axis=0
            )

        keys = [apart(win_keys[:, half]) for half in halves]
        scores = [
            mm_t(win_queries[:, half].astype(BF16), key.astype(BF16))
            for half, key in zip(halves, keys)
        ]
        queries = jnp.concatenate([win_queries[:, half] for half in halves], axis=0)
        query_square = mm((queries * queries).astype(BF16), ones_ref[...])
        key_squares = [mm_t(each, (key * key).astype(BF16))[:1] for key in keys]
        values = [
            jnp.concatenate([apart(win_values[:, half]).astype(BF16), ones_ref[...]], axis=1)
            for half in halves
        ]
        weights = []
        for i in range(2):
            square = query_square[i * TOKENS : (i + 1) * TOKENS]
            scale = lax.rsqrt(factor * factor * square + head_eps) * (factor * SCORE_SCALE)
            scale = scale * lax.rsqrt(key_squares[i] + head_eps)
            weights.append((jnp.exp2(scores[i] * scale) * allowed).astype(BF16))
        both = [mm(weights[i], values[i]) for i in range(2)]
        mixed = [(each_both[:, :HALF] / each_both[:, HALF:]).astype(BF16) for each_both in both]
        wait(turn_index, 1)
        attended = latents + mm(jnp.concatenate(mixed, axis=1), proj_ref[...])
        wait(turn_index, 2)
        centred = centre(attended)
        hidden = mm((centred * entry(GAIN_ROW + 2)).astype(BF16), up_ref[...])
        hidden = gelu(hidden * row_factor(centred)).astype(BF16)
        wait(turn_index, 3)
        backbone = attended + mm(hidden, down_ref[...])
        first, second = backbone[:PATCHES], backbone[PATCHES:]
        blended = jnp.concatenate(
            [mixing(l, 0) * first + mixing(l, 1) * second + embed(l) for l in range(LEV)], axis=0
        )
        centred = centre(blended)
        added = mm((centred * entry(GAIN_ROW + 3)).astype(BF16), dec_ref[...])
        current = (current + added * row_factor(centred)).astype(BF16).astype(F32)

    for l in range(LEV):
        wide[:, l * PIN : (l + 1) * PIN] = current[l * PATCHES : (l + 1) * PATCHES]
    out_ref[0] = wide[...].astype(BF16).reshape(out_ref.shape[1:])


def forecast(windows, arranged, early, late):
    vmem = pl.BlockSpec(memory_space=pltpu.VMEM)
    if windows == 1:
        block, grid = vmem, ()
        result = pltpu.VMEM(arranged.shape, BF16)
        arranged = pltpu.with_memory_space_constraint(arranged, pltpu.VMEM)
    else:
        result = jax.ShapeDtypeStruct(arranged.shape, BF16)
        block = pl.BlockSpec((1,) + arranged.shape[1:], lambda i: (i, 0, 0, 0))
        grid = (windows,)
    early = [pltpu.with_memory_space_constraint(a, pltpu.VMEM) for a in early]
    return pl.pallas_call(
        functools.partial(forecast_kernel, windows),
        grid=grid,
        in_specs=[vmem] * EARLY + [pl.BlockSpec(memory_space=pl.ANY)] * LATE + [block],
        out_specs=block,
        out_shape=result,
        scratch_shapes=[pltpu.VMEM(a.shape, a.dtype) for a in late]
        + [
            pltpu.VMEM((PATCHES, LEV * PIN), F32),
            pltpu.SemaphoreType.DMA((LATE,)),
        ],
        compiler_params=pltpu.CompilerParams(vmem_limit_bytes=MAIN_LIMIT),
    )(*early, *late, arranged)


def turn_kernel(step, direction, x_ref, out_ref, *token_ref):
    for ref in token_ref:
        ref[...] = jnp.zeros_like(ref)
    shift = jnp.where(lax.axis_index("lon") < step, 1, 0)
    if direction > 0:
        count = out_ref.shape[0]
        blocks = x_ref[...].reshape(out_ref.shape)
        for i in range(count):
            out_ref[lax.rem(i + count - shift, count)] = blocks[i]
    else:
        count = x_ref.shape[0]
        blocks = [x_ref[lax.rem(i + count - shift, count)] for i in range(count)]
        out_ref[...] = jnp.stack(blocks).reshape(out_ref.shape)


def turn(array, shape, step, direction, near=False, token=False):
    if near and not token:
        array = pltpu.with_memory_space_constraint(array, pltpu.VMEM)
    held = near and token
    shapes = [pltpu.VMEM(shape, BF16) if held else jax.ShapeDtypeStruct(shape, BF16)]
    if token:
        shapes.append(pltpu.VMEM((8, LANES), F32))
    return pl.pallas_call(
        functools.partial(turn_kernel, step, direction),
        out_shape=shapes,
        compiler_params=pltpu.CompilerParams(vmem_limit_bytes=None if token else TURN_LIMIT),
    )(array)


def shards(
    fields,
    level_ids,
    embed_weight,
    level_embed,
    enc_gain,
    latent_query,
    kv_weight,
    pool_out,
    attn_gain,
    qkv_weight,
    attn_proj,
    mlp_gain,
    mlp_up,
    mlp_down,
    level_mix,
    dec_gain,
    dec_weight,
):
    devices = lax.axis_size("lon")
    width = fields.shape[2]
    local_count = fields.shape[1]
    piece_cols = local_count // devices
    lat_count = devices // ROW_PARTS
    bands = lat_count // W_LAT
    cut = (W_LON // 2 // piece_cols) * lat_count
    scalars = (level_ids, level_mix.T)
    rows = (
        level_embed,
        latent_query,
        enc_gain.reshape(1, D),
        attn_gain.reshape(1, D),
        mlp_gain.reshape(1, D),
        dec_gain.reshape(1, D),
    )
    outgoing, token = turn(
        fields.reshape(local_count, width), (devices, piece_cols, width), cut, 1, bands == 1, token=True
    )
    early = load(token, scalars, rows, dec_weight.T, (embed_weight, kv_weight, pool_out))
    late = (qkv_weight, attn_proj, mlp_up, mlp_down)
    got = lax.all_to_all(outgoing, "lon", split_axis=0, concat_axis=0, tiled=True)
    if bands > 1:
        got = got.reshape(ROW_PARTS, lat_count, piece_cols, width)
        got = jnp.roll(got, -(W_LAT // 2), axis=1)
        got = got.reshape(ROW_PARTS, bands, W_LAT, piece_cols, width).transpose(1, 0, 2, 3, 4)
    done = forecast(bands, got.reshape(bands, ROW_PARTS * W_LAT, piece_cols, width), early, late)
    if bands > 1:
        done = done.reshape(bands, ROW_PARTS, W_LAT, piece_cols, width).transpose(1, 0, 2, 3, 4)
        done = done.reshape(ROW_PARTS, lat_count, piece_cols, width)
        done = jnp.roll(done, W_LAT // 2, axis=1)
    done = done.reshape(devices, piece_cols, width)
    home = lax.all_to_all(done, "lon", split_axis=0, concat_axis=0, tiled=True)
    (forecast_here,) = turn(home, (local_count, width), cut, -1, bands == 1)
    return forecast_here.reshape(fields.shape)


def solution(mesh):
    placed = (P(("groups", "lon"), None, None), P("groups")) + (P(),) * 15
    return jax.shard_map(
        shards,
        mesh=mesh,
        in_specs=placed,
        out_specs=P(("groups", "lon"), None, None),
        check_vma=False,
    )
```

```python
import functools
import math

import jax
import jax.numpy as jnp
from jax import lax
from jax.experimental import pallas as pl
from jax.experimental.pallas import tpu as pltpu
from jax.sharding import PartitionSpec as P

D = 512
HEADS = 8
HEAD_DIM = D // HEADS
PIN = 500
LEV = 3
LATL = 2
W_LAT = 4
W_LON = 8
STEPS = 2
ROW_PARTS = 4
MLP = 2048
PATCHES = W_LAT * W_LON
TOKENS = PATCHES * LATL
HALF = D // 2
PAIR = 2 * HEAD_DIM
EARLY, LATE = 10, 4
LANES = 128
CHUNK = 16
LOAD_LIMIT = 56 * 1024 * 1024
TURN_LIMIT = 16 * 1024 * 1024
MAIN_LIMIT = 56 * 1024 * 1024
EMBED_ROW, MIX_ROW, LATENT_ROW, GAIN_ROW, TABLE_ROWS = 0, 3, 9, 11, 16

GELU_FIRST = math.sqrt(2.0 / math.pi)
GELU_THIRD = 0.044715 * GELU_FIRST
SCORE_SCALE = HEAD_DIM ** (-0.5) * math.log2(math.e)

norm_eps = 1e-05
head_eps = 1e-06

F32 = jnp.float32
BF16 = jnp.bfloat16


def mm(a, b):
    return jnp.dot(a, b, preferred_element_type=F32)


def mm_t(a, b):
    return lax.dot_general(a, b, (((1,), (1,)), ((), ())), preferred_element_type=F32)


def row_factor(centred):
    return lax.rsqrt(jnp.mean(centred * centred, axis=-1, keepdims=True) + norm_eps)


def centre(rows):
    return rows - jnp.mean(rows, axis=-1, keepdims=True)


def gelu(values):
    curve = values * (GELU_FIRST + GELU_THIRD * (values * values))
    half = 0.5 * values
    return half + half * jnp.tanh(curve)


def iota(shape, dim):
    return lax.broadcasted_iota(jnp.int32, shape, dim)


def load_kernel(*refs):
    (
        ids_from,
        mix_from,
        level_embed_from,
        latent_query_from,
        enc_gain_from,
        attn_gain_from,
        mlp_gain_from,
        dec_gain_from,
        dec_from,
        embed_from,
        kv_from,
        pool_from,
        _,
        table_ref,
        query_ref,
        mean_ref,
        spread_ref,
        ones_ref,
        allowed_ref,
        dec_ref,
        embed_ref,
        kv_ref,
        pool_ref,
        ids_ref,
        mix_ref,
        level_embed_ref,
        latent_query_ref,
        gain_refs,
        dec_rows_ref,
        embed_rows_ref,
        pool_rows_ref,
        arrivals,
    ) = refs
    pairs = [
        (ids_from, ids_ref),
        (mix_from, mix_ref),
        (level_embed_from, level_embed_ref),
        (latent_query_from, latent_query_ref),
        (enc_gain_from, gain_refs.at[0]),
        (attn_gain_from, gain_refs.at[1]),
        (mlp_gain_from, gain_refs.at[2]),
        (dec_gain_from, gain_refs.at[3]),
        (dec_from, dec_rows_ref),
        (embed_from, embed_rows_ref),
        (pool_from, pool_rows_ref),
        (kv_from, kv_ref),
    ]
    copies = [
        pltpu.make_async_copy(here, there, arrivals.at[i]) for i, (here, there) in enumerate(pairs)
    ]
    for copy in copies:
        copy.start()

    feature_head = iota((D, LANES), 0) // HEAD_DIM
    lane = iota((D, LANES), 1)
    on_head = (feature_head == lane % HEADS) & (lane < LATL * HEADS)
    mean_ref[...] = jnp.where(on_head, 1.0 / HEAD_DIM, 0.0).astype(BF16)
    spread_ref[...] = jnp.where(
        iota((LATL * HEADS, LATL * D), 0) == iota((LATL * HEADS, LATL * D), 1) // HEAD_DIM, 1.0, 0.0
    ).astype(BF16)
    ones_ref[...] = jnp.where(
        iota((HALF, HALF), 0) // HEAD_DIM == iota((HALF, HALF), 1) // HEAD_DIM, 1.0 / HEAD_DIM, 0.0
    ).astype(BF16)
    row_bit = (iota((TOKENS, PAIR), 0) // 4) % 2
    lane_bit = (iota((TOKENS, PAIR), 1) // 4) % 2
    allowed_ref[...] = jnp.where(row_bit == lane_bit, 1.0, 0.0)

    for copy in copies[:8]:
        copy.wait()
    level_embed = centre(level_embed_ref[...].astype(F32))
    for l in range(LEV):
        level = ids_ref[l]
        row = level_embed[LEV - 1 : LEV]
        for i in reversed(range(LEV - 1)):
            row = jnp.where(level == i, level_embed[i : i + 1], row)
        table_ref[EMBED_ROW + l : EMBED_ROW + l + 1, :] = row
        for j in range(LATL):
            at = MIX_ROW + l * LATL + j
            table_ref[at : at + 1, :] = jnp.full((1, D), mix_ref[j, level])
    latent = latent_query_ref[...].astype(F32)
    table_ref[LATENT_ROW : LATENT_ROW + LATL, :] = centre(latent)
    for i in range(4):
        table_ref[GAIN_ROW + i : GAIN_ROW + i + 1, :] = gain_refs[i]
    row_id = iota((LANES, D), 0)
    own_head = (row_id % HEADS) == iota((LANES, D), 1) // HEAD_DIM
    spots = jnp.zeros((LANES, D), F32)
    for j in range(LATL):
        mine = own_head & (row_id // HEADS == j)
        spots = jnp.where(mine, jnp.broadcast_to(latent[j : j + 1], (LANES, D)), spots)
    mean_square = jnp.sum(spots * spots, axis=-1, keepdims=True) / HEAD_DIM
    query_ref[...] = (spots * lax.rsqrt(mean_square + head_eps)).T.astype(BF16)

    copies[8].wait()
    dec_ref[...] = dec_rows_ref[...].astype(F32).T.astype(BF16)
    copies[9].wait()
    embed_ref[...] = centre(embed_rows_ref[...].astype(F32)).astype(BF16)
    copies[10].wait()
    pool_ref[...] = centre(pool_rows_ref[...].astype(F32)).astype(BF16)
    copies[11].wait()


def load(after, scalars, rows, dec, early):
    far = pl.BlockSpec(memory_space=pl.ANY)
    made = [
        pltpu.VMEM((TABLE_ROWS, D), F32),
        pltpu.VMEM((D, LANES), BF16),
        pltpu.VMEM((D, LANES), BF16),
        pltpu.VMEM((LATL * HEADS, LATL * D), BF16),
        pltpu.VMEM((HALF, HALF), BF16),
        pltpu.VMEM((TOKENS, PAIR), F32),
        pltpu.VMEM(dec.shape[::-1], BF16),
    ] + [pltpu.VMEM(a.shape, a.dtype) for a in early]
    inputs = (*scalars, *rows, dec, *early)
    return pl.pallas_call(
        load_kernel,
        in_specs=[far] * len(inputs) + [pl.BlockSpec(memory_space=pltpu.VMEM)],
        out_specs=[pl.BlockSpec(memory_space=pltpu.VMEM)] * len(made),
        out_shape=made,
        scratch_shapes=[pltpu.SMEM(a.shape, a.dtype) for a in scalars]
        + [
            pltpu.VMEM((LEV, D), BF16),
            pltpu.VMEM((LATL, D), BF16),
            pltpu.VMEM((4, 1, D), F32),
            pltpu.VMEM(dec.shape, BF16),
            pltpu.VMEM(early[0].shape, BF16),
            pltpu.VMEM(early[2].shape, BF16),
            pltpu.SemaphoreType.DMA((len(inputs),)),
        ],
        compiler_params=pltpu.CompilerParams(vmem_limit_bytes=LOAD_LIMIT),
        cost_estimate=pl.CostEstimate(flops=0, bytes_accessed=8_000_000, transcendentals=0),
    )(*inputs, pltpu.with_memory_space_constraint(after, pltpu.VMEM))


def forecast_kernel(windows, *refs):
    (
        table_ref,
        query_ref,
        mean_ref,
        spread_ref,
        ones_ref,
        allowed_ref,
        dec_ref,
        embed_ref,
        kv_ref,
        pool_ref,
    ) = refs[:EARLY]
    far, (x_ref, out_ref), refs = refs[EARLY:][:LATE], refs[EARLY + LATE :][:2], refs[EARLY + LATE + 2 :]
    near, (wide, arrivals) = refs[:LATE], refs[LATE:]
    qkv_ref, proj_ref, up_ref, down_ref = near
    copies = [
        pltpu.make_async_copy(far[i], near[i], arrivals.at[i]) for i in range(LATE)
    ]

    def in_first_window(action):
        if windows == 1:
            action()
        else:
            pl.when(pl.program_id(0) == 0)(action)

    def start(*wanted):
        def action():
            for i in wanted:
                copies[i].start()

        in_first_window(action)

    def wait(turn_index, *wanted):
        def action():
            for i in wanted:
                copies[i].wait()

        if turn_index == 0:
            in_first_window(action)

    start(0, 1)

    def entry(at):
        return table_ref[at : at + 1, :]

    def embed(l):
        return entry(EMBED_ROW + l)

    def mixing(l, j):
        return entry(MIX_ROW + l * LATL + j)

    half_head = iota((1, HALF), 1) // HEAD_DIM
    each = jnp.full((16, HALF), 1.0 / HEAD_DIM, BF16)

    arrived = x_ref[0].reshape(PATCHES, LEV * PIN).astype(F32)
    current = jnp.concatenate(
        [arrived[:, l * PIN : (l + 1) * PIN] for l in range(LEV)], axis=0
    )

    start(2)

    def by_level(values):
        return [values[l * PATCHES : (l + 1) * PATCHES] for l in range(LEV)]

    for turn_index in range(STEPS):
        tokens = by_level(mm(current.astype(BF16), embed_ref[...]))
        tokens = jnp.concatenate([tokens[l] + embed(l) for l in range(LEV)], axis=0)
        keyval = mm((tokens * entry(GAIN_ROW)).astype(BF16), kv_ref[...])
        if turn_index == 0:
            start(3)
        factor = row_factor(tokens)
        keys = keyval[:, :D]
        values = by_level(keyval[:, D:])
        scores = mm(keys.astype(BF16), query_ref[...])[:, : LATL * HEADS]
        mean_square = mm((keys * keys).astype(BF16), mean_ref[...])[:, : LATL * HEADS]
        scale = factor * lax.rsqrt(factor * factor * mean_square + head_eps)
        parts = by_level(jnp.exp2(scores * (scale * SCORE_SCALE)))
        inverse = 1.0 / (parts[0] + parts[1] + parts[2])
        factors = by_level(factor)
        weights = jnp.concatenate(
            [parts[l] * (inverse * factors[l]) for l in range(LEV)], axis=0
        ).astype(BF16)
        wide_weights = by_level(mm(weights, spread_ref[...]))
        pooled = []
        for j in range(LATL):
            terms = [wide_weights[l][:, j * D : (j + 1) * D] * values[l] for l in range(LEV)]
            pooled.append(terms[0] + terms[1] + terms[2])
        latents = mm(jnp.concatenate(pooled, axis=0).astype(BF16), pool_ref[...])
        latents = jnp.concatenate(
            [
                latents[j * PATCHES : (j + 1) * PATCHES] + entry(LATENT_ROW + j)
                for j in range(LATL)
            ],
            axis=0,
        )
        wait(turn_index, 0)
        projected = mm((latents * entry(GAIN_ROW + 1)).astype(BF16), qkv_ref[...])
        factor = row_factor(latents)
        allowed = allowed_ref[...]
        if windows > 1:
            cut = jnp.where(pl.program_id(0) == windows - 1, 1.0, 0.0)
            allowed = 1.0 - cut * (1.0 - allowed)
        allowed = jnp.concatenate([allowed, allowed], axis=1)
        win_queries = projected[:, :D]
        win_keys = projected[:, D : 2 * D] * factor
        win_values = projected[:, 2 * D :] * (factor * (1.0 / HEAD_DIM))
        halves = [slice(i * HALF, (i + 1) * HALF) for i in range(2)]

        def apart(rows):
            return jnp.concatenate(
                [jnp.where(half_head == h, rows, 0.0) for h in range(HEADS // 2)], axis=0
            )

        keys = [apart(win_keys[:, half]) for half in halves]
        scores = [
            mm_t(win_queries[:, half].astype(BF16), key.astype(BF16))
            for half, key in zip(halves, keys)
        ]
        queries = jnp.concatenate([win_queries[:, half] for half in halves], axis=0)
        query_square = mm((queries * queries).astype(BF16), ones_ref[...])
        key_squares = [mm_t(each, (key * key).astype(BF16))[:1] for key in keys]
        values = [
            jnp.concatenate([apart(win_values[:, half]).astype(BF16), ones_ref[...]], axis=1)
            for half in halves
        ]
        weights = []
        for i in range(2):
            square = query_square[i * TOKENS : (i + 1) * TOKENS]
            scale = lax.rsqrt(factor * factor * square + head_eps) * (factor * SCORE_SCALE)
            scale = scale * lax.rsqrt(key_squares[i] + head_eps)
            weights.append((jnp.exp2(scores[i] * scale) * allowed).astype(BF16))
        both = [mm(weights[i], values[i]) for i in range(2)]
        mixed = [(each_both[:, :HALF] / each_both[:, HALF:]).astype(BF16) for each_both in both]
        wait(turn_index, 1)
        attended = latents + mm(jnp.concatenate(mixed, axis=1), proj_ref[...])
        wait(turn_index, 2)
        centred = centre(attended)
        hidden = mm((centred * entry(GAIN_ROW + 2)).astype(BF16), up_ref[...])
        hidden = gelu(hidden * row_factor(centred)).astype(BF16)
        wait(turn_index, 3)
        backbone = attended + mm(hidden, down_ref[...])
        first, second = backbone[:PATCHES], backbone[PATCHES:]
        blended = jnp.concatenate(
            [mixing(l, 0) * first + mixing(l, 1) * second + embed(l) for l in range(LEV)], axis=0
        )
        centred = centre(blended)
        added = mm((centred * entry(GAIN_ROW + 3)).astype(BF16), dec_ref[...])
        current = (current + added * row_factor(centred)).astype(BF16).astype(F32)

    for l in range(LEV):
        wide[:, l * PIN : (l + 1) * PIN] = current[l * PATCHES : (l + 1) * PATCHES]
    out_ref[0] = wide[...].astype(BF16).reshape(out_ref.shape[1:])


def forecast(windows, arranged, early, late):
    vmem = pl.BlockSpec(memory_space=pltpu.VMEM)
    if windows == 1:
        block, grid = vmem, ()
        result = pltpu.VMEM(arranged.shape, BF16)
        arranged = pltpu.with_memory_space_constraint(arranged, pltpu.VMEM)
    else:
        result = jax.ShapeDtypeStruct(arranged.shape, BF16)
        block = pl.BlockSpec((1,) + arranged.shape[1:], lambda i: (i, 0, 0, 0))
        grid = (windows,)
    early = [pltpu.with_memory_space_constraint(a, pltpu.VMEM) for a in early]
    return pl.pallas_call(
        functools.partial(forecast_kernel, windows),
        grid=grid,
        in_specs=[vmem] * EARLY + [pl.BlockSpec(memory_space=pl.ANY)] * LATE + [block],
        out_specs=block,
        out_shape=result,
        scratch_shapes=[pltpu.VMEM(a.shape, a.dtype) for a in late]
        + [
            pltpu.VMEM((PATCHES, LEV * PIN), F32),
            pltpu.SemaphoreType.DMA((LATE,)),
        ],
        compiler_params=pltpu.CompilerParams(vmem_limit_bytes=MAIN_LIMIT),
    )(*early, *late, arranged)


def turn_out_kernel(step, x_ref, out_ref, token_ref, near, arrivals):
    count, size = out_ref.shape[:2]
    copies = [
        pltpu.make_async_copy(
            x_ref.at[pl.ds(i * CHUNK, CHUNK)], near.at[pl.ds(i * CHUNK, CHUNK)], arrivals.at[i]
        )
        for i in range(count * size // CHUNK)
    ]
    for copy in copies:
        copy.start()
    token_ref[...] = jnp.zeros_like(token_ref)
    shift = jnp.where(lax.axis_index("lon") < step, 1, 0)
    blocks = CHUNK // size
    for i, copy in enumerate(copies):
        copy.wait()
        piece = near[i * CHUNK : (i + 1) * CHUNK, :].reshape((blocks,) + out_ref.shape[1:])
        for j in range(blocks):
            out_ref[lax.rem(i * blocks + j + count - shift, count)] = piece[j]


def turn_back_kernel(step, x_ref, out_ref):
    count = x_ref.shape[0]
    shift = jnp.where(lax.axis_index("lon") < step, 1, 0)
    blocks = [x_ref[lax.rem(i + count - shift, count)] for i in range(count)]
    out_ref[...] = jnp.stack(blocks).reshape(out_ref.shape)


def turn_out(array, shape, step, near):
    return pl.pallas_call(
        functools.partial(turn_out_kernel, step),
        in_specs=[pl.BlockSpec(memory_space=pl.ANY)],
        out_shape=[
            pltpu.VMEM(shape, BF16) if near else jax.ShapeDtypeStruct(shape, BF16),
            pltpu.VMEM((8, LANES), F32),
        ],
        out_specs=[pl.BlockSpec(memory_space=pltpu.VMEM)] * 2,
        scratch_shapes=[
            pltpu.VMEM(array.shape, BF16),
            pltpu.SemaphoreType.DMA((array.shape[0] // CHUNK,)),
        ],
    )(array)


def turn_back(array, shape, step, near):
    if near:
        array = pltpu.with_memory_space_constraint(array, pltpu.VMEM)
    return pl.pallas_call(
        functools.partial(turn_back_kernel, step),
        out_shape=jax.ShapeDtypeStruct(shape, BF16),
        compiler_params=pltpu.CompilerParams(vmem_limit_bytes=TURN_LIMIT),
    )(array)


def shards(
    fields,
    level_ids,
    embed_weight,
    level_embed,
    enc_gain,
    latent_query,
    kv_weight,
    pool_out,
    attn_gain,
    qkv_weight,
    attn_proj,
    mlp_gain,
    mlp_up,
    mlp_down,
    level_mix,
    dec_gain,
    dec_weight,
):
    devices = lax.axis_size("lon")
    width = fields.shape[2]
    local_count = fields.shape[1]
    piece_cols = local_count // devices
    lat_count = devices // ROW_PARTS
    bands = lat_count // W_LAT
    cut = (W_LON // 2 // piece_cols) * lat_count
    scalars = (level_ids, level_mix.T)
    rows = (
        level_embed,
        latent_query,
        enc_gain.reshape(1, D),
        attn_gain.reshape(1, D),
        mlp_gain.reshape(1, D),
        dec_gain.reshape(1, D),
    )
    outgoing, token = turn_out(
        fields.reshape(local_count, width), (devices, piece_cols, width), cut, bands == 1
    )
    early = load(token, scalars, rows, dec_weight.T, (embed_weight, kv_weight, pool_out))
    late = (qkv_weight, attn_proj, mlp_up, mlp_down)
    got = lax.all_to_all(outgoing, "lon", split_axis=0, concat_axis=0, tiled=True)
    if bands > 1:
        got = got.reshape(ROW_PARTS, lat_count, piece_cols, width)
        got = jnp.roll(got, -(W_LAT // 2), axis=1)
        got = got.reshape(ROW_PARTS, bands, W_LAT, piece_cols, width).transpose(1, 0, 2, 3, 4)
    done = forecast(bands, got.reshape(bands, ROW_PARTS * W_LAT, piece_cols, width), early, late)
    if bands > 1:
        done = done.reshape(bands, ROW_PARTS, W_LAT, piece_cols, width).transpose(1, 0, 2, 3, 4)
        done = done.reshape(ROW_PARTS, lat_count, piece_cols, width)
        done = jnp.roll(done, W_LAT // 2, axis=1)
    done = done.reshape(devices, piece_cols, width)
    home = lax.all_to_all(done, "lon", split_axis=0, concat_axis=0, tiled=True)
    forecast_here = turn_back(home, (local_count, width), cut, bands == 1)
    return forecast_here.reshape(fields.shape)


def solution(mesh):
    placed = (P(("groups", "lon"), None, None), P("groups")) + (P(),) * 15
    return jax.shard_map(
        shards,
        mesh=mesh,
        in_specs=placed,
        out_specs=P(("groups", "lon"), None, None),
        check_vma=False,
    )
```

```python
import functools
import math

import jax
import jax.numpy as jnp
from jax import lax
from jax.experimental import pallas as pl
from jax.experimental.pallas import tpu as pltpu
from jax.sharding import PartitionSpec as P

D = 512
HEADS = 8
HEAD_DIM = D // HEADS
PIN = 500
LEV = 3
LATL = 2
W_LAT = 4
W_LON = 8
STEPS = 2
ROW_PARTS = 4
MLP = 2048
PATCHES = W_LAT * W_LON
TOKENS = PATCHES * LATL
HALF = D // 2
PAIR = 2 * HEAD_DIM
EARLY, LATE = 10, 4
LANES = 128
CHUNK = 16
LOAD_LIMIT = 56 * 1024 * 1024
TURN_LIMIT = 16 * 1024 * 1024
MAIN_LIMIT = 56 * 1024 * 1024
EMBED_ROW, MIX_ROW, LATENT_ROW, GAIN_ROW, TABLE_ROWS = 0, 3, 9, 11, 16

GELU_FIRST = math.sqrt(2.0 / math.pi)
GELU_THIRD = 0.044715 * GELU_FIRST
SCORE_SCALE = HEAD_DIM ** (-0.5) * math.log2(math.e)

norm_eps = 1e-05
head_eps = 1e-06

F32 = jnp.float32
BF16 = jnp.bfloat16


def mm(a, b):
    return jnp.dot(a, b, preferred_element_type=F32)


def mm_t(a, b):
    return lax.dot_general(a, b, (((1,), (1,)), ((), ())), preferred_element_type=F32)


def row_factor(centred):
    return lax.rsqrt(jnp.mean(centred * centred, axis=-1, keepdims=True) + norm_eps)


def centre(rows):
    return rows - jnp.mean(rows, axis=-1, keepdims=True)


def gelu(values):
    curve = values * (GELU_FIRST + GELU_THIRD * (values * values))
    half = 0.5 * values
    return half + half * jnp.tanh(curve)


def iota(shape, dim):
    return lax.broadcasted_iota(jnp.int32, shape, dim)


def load_kernel(*refs):
    (
        ids_from,
        mix_from,
        level_embed_from,
        latent_query_from,
        enc_gain_from,
        attn_gain_from,
        mlp_gain_from,
        dec_gain_from,
        dec_from,
        embed_from,
        kv_from,
        pool_from,
        _,
        table_ref,
        query_ref,
        mean_ref,
        spread_ref,
        ones_ref,
        allowed_ref,
        dec_ref,
        embed_ref,
        kv_ref,
        pool_ref,
        ids_ref,
        mix_ref,
        level_embed_ref,
        latent_query_ref,
        gain_refs,
        dec_rows_ref,
        embed_rows_ref,
        pool_rows_ref,
        arrivals,
    ) = refs
    pairs = [
        (ids_from, ids_ref),
        (mix_from, mix_ref),
        (level_embed_from, level_embed_ref),
        (latent_query_from, latent_query_ref),
        (enc_gain_from, gain_refs.at[0]),
        (attn_gain_from, gain_refs.at[1]),
        (mlp_gain_from, gain_refs.at[2]),
        (dec_gain_from, gain_refs.at[3]),
        (dec_from, dec_rows_ref),
        (embed_from, embed_rows_ref),
        (pool_from, pool_rows_ref),
        (kv_from, kv_ref),
    ]
    copies = [
        pltpu.make_async_copy(here, there, arrivals.at[i]) for i, (here, there) in enumerate(pairs)
    ]
    for copy in copies:
        copy.start()

    feature_head = iota((D, LANES), 0) // HEAD_DIM
    lane = iota((D, LANES), 1)
    on_head = (feature_head == lane % HEADS) & (lane < LATL * HEADS)
    mean_ref[...] = jnp.where(on_head, 1.0 / HEAD_DIM, 0.0).astype(BF16)
    spread_ref[...] = jnp.where(
        iota((LATL * HEADS, LATL * D), 0) == iota((LATL * HEADS, LATL * D), 1) // HEAD_DIM, 1.0, 0.0
    ).astype(BF16)
    ones_ref[...] = jnp.where(
        iota((HALF, HALF), 0) // HEAD_DIM == iota((HALF, HALF), 1) // HEAD_DIM, 1.0 / HEAD_DIM, 0.0
    ).astype(BF16)
    row_bit = (iota((TOKENS, PAIR), 0) // 4) % 2
    lane_bit = (iota((TOKENS, PAIR), 1) // 4) % 2
    allowed_ref[...] = jnp.where(row_bit == lane_bit, 1.0, 0.0)

    for copy in copies[:8]:
        copy.wait()
    level_embed = centre(level_embed_ref[...].astype(F32))
    for l in range(LEV):
        level = ids_ref[l]
        row = level_embed[LEV - 1 : LEV]
        for i in reversed(range(LEV - 1)):
            row = jnp.where(level == i, level_embed[i : i + 1], row)
        table_ref[EMBED_ROW + l : EMBED_ROW + l + 1, :] = row
        for j in range(LATL):
            at = MIX_ROW + l * LATL + j
            table_ref[at : at + 1, :] = jnp.full((1, D), mix_ref[j, level])
    latent = latent_query_ref[...].astype(F32)
    table_ref[LATENT_ROW : LATENT_ROW + LATL, :] = centre(latent)
    for i in range(4):
        table_ref[GAIN_ROW + i : GAIN_ROW + i + 1, :] = gain_refs[i]
    row_id = iota((LANES, D), 0)
    own_head = (row_id % HEADS) == iota((LANES, D), 1) // HEAD_DIM
    spots = jnp.zeros((LANES, D), F32)
    for j in range(LATL):
        mine = own_head & (row_id // HEADS == j)
        spots = jnp.where(mine, jnp.broadcast_to(latent[j : j + 1], (LANES, D)), spots)
    mean_square = jnp.sum(spots * spots, axis=-1, keepdims=True) / HEAD_DIM
    query_ref[...] = (spots * lax.rsqrt(mean_square + head_eps)).T.astype(BF16)

    copies[8].wait()
    dec_ref[...] = dec_rows_ref[...].astype(F32).T.astype(BF16)
    copies[9].wait()
    embed_ref[...] = centre(embed_rows_ref[...].astype(F32)).astype(BF16)
    copies[10].wait()
    pool_ref[...] = centre(pool_rows_ref[...].astype(F32)).astype(BF16)
    copies[11].wait()


def load(after, scalars, rows, dec, early):
    far = pl.BlockSpec(memory_space=pl.ANY)
    made = [
        pltpu.VMEM((TABLE_ROWS, D), F32),
        pltpu.VMEM((D, LANES), BF16),
        pltpu.VMEM((D, LANES), BF16),
        pltpu.VMEM((LATL * HEADS, LATL * D), BF16),
        pltpu.VMEM((HALF, HALF), BF16),
        pltpu.VMEM((TOKENS, PAIR), F32),
        pltpu.VMEM(dec.shape[::-1], BF16),
    ] + [pltpu.VMEM(a.shape, a.dtype) for a in early]
    inputs = (*scalars, *rows, dec, *early)
    return pl.pallas_call(
        load_kernel,
        in_specs=[far] * len(inputs) + [pl.BlockSpec(memory_space=pltpu.VMEM)],
        out_specs=[pl.BlockSpec(memory_space=pltpu.VMEM)] * len(made),
        out_shape=made,
        scratch_shapes=[pltpu.SMEM(a.shape, a.dtype) for a in scalars]
        + [
            pltpu.VMEM((LEV, D), BF16),
            pltpu.VMEM((LATL, D), BF16),
            pltpu.VMEM((4, 1, D), F32),
            pltpu.VMEM(dec.shape, BF16),
            pltpu.VMEM(early[0].shape, BF16),
            pltpu.VMEM(early[2].shape, BF16),
            pltpu.SemaphoreType.DMA((len(inputs),)),
        ],
        compiler_params=pltpu.CompilerParams(vmem_limit_bytes=LOAD_LIMIT),
        cost_estimate=pl.CostEstimate(flops=0, bytes_accessed=8_000_000, transcendentals=0),
    )(*inputs, pltpu.with_memory_space_constraint(after, pltpu.VMEM))


def forecast_kernel(windows, *refs):
    (
        table_ref,
        query_ref,
        mean_ref,
        spread_ref,
        ones_ref,
        allowed_ref,
        dec_ref,
        embed_ref,
        kv_ref,
        pool_ref,
    ) = refs[:EARLY]
    far, (x_ref, out_ref), refs = refs[EARLY:][:LATE], refs[EARLY + LATE :][:2], refs[EARLY + LATE + 2 :]
    near, (wide, arrivals) = refs[:LATE], refs[LATE:]
    qkv_ref, proj_ref, up_ref, down_ref = near
    copies = [
        pltpu.make_async_copy(far[i], near[i], arrivals.at[i]) for i in range(LATE)
    ]

    def in_first_window(action):
        if windows == 1:
            action()
        else:
            pl.when(pl.program_id(0) == 0)(action)

    def start(*wanted):
        def action():
            for i in wanted:
                copies[i].start()

        in_first_window(action)

    def wait(turn_index, *wanted):
        def action():
            for i in wanted:
                copies[i].wait()

        if turn_index == 0:
            in_first_window(action)

    start(0, 1)

    def entry(at):
        return table_ref[at : at + 1, :]

    def embed(l):
        return entry(EMBED_ROW + l)

    def mixing(l, j):
        return entry(MIX_ROW + l * LATL + j)

    half_head = iota((1, HALF), 1) // HEAD_DIM
    each = jnp.full((16, HALF), 1.0 / HEAD_DIM, BF16)

    arrived = x_ref[0].reshape(PATCHES, LEV * PIN).astype(F32)
    current = jnp.concatenate(
        [arrived[:, l * PIN : (l + 1) * PIN] for l in range(LEV)], axis=0
    )

    start(2)

    def by_level(values):
        return [values[l * PATCHES : (l + 1) * PATCHES] for l in range(LEV)]

    for turn_index in range(STEPS):
        tokens = by_level(mm(current.astype(BF16), embed_ref[...]))
        tokens = jnp.concatenate([tokens[l] + embed(l) for l in range(LEV)], axis=0)
        keyval = mm((tokens * entry(GAIN_ROW)).astype(BF16), kv_ref[...])
        if turn_index == 0:
            start(3)
        factor = row_factor(tokens)
        keys = keyval[:, :D]
        values = by_level(keyval[:, D:])
        scores = mm(keys.astype(BF16), query_ref[...])[:, : LATL * HEADS]
        mean_square = mm((keys * keys).astype(BF16), mean_ref[...])[:, : LATL * HEADS]
        scale = factor * lax.rsqrt(factor * factor * mean_square + head_eps)
        parts = by_level(jnp.exp2(scores * (scale * SCORE_SCALE)))
        inverse = 1.0 / (parts[0] + parts[1] + parts[2])
        factors = by_level(factor)
        weights = jnp.concatenate(
            [parts[l] * (inverse * factors[l]) for l in range(LEV)], axis=0
        ).astype(BF16)
        wide_weights = by_level(mm(weights, spread_ref[...]))
        pooled = []
        for j in range(LATL):
            terms = [wide_weights[l][:, j * D : (j + 1) * D] * values[l] for l in range(LEV)]
            pooled.append(terms[0] + terms[1] + terms[2])
        latents = mm(jnp.concatenate(pooled, axis=0).astype(BF16), pool_ref[...])
        latents = jnp.concatenate(
            [
                latents[j * PATCHES : (j + 1) * PATCHES] + entry(LATENT_ROW + j)
                for j in range(LATL)
            ],
            axis=0,
        )
        wait(turn_index, 0)
        projected = mm((latents * entry(GAIN_ROW + 1)).astype(BF16), qkv_ref[...])
        factor = row_factor(latents)
        allowed = allowed_ref[...]
        if windows > 1:
            cut = jnp.where(pl.program_id(0) == windows - 1, 1.0, 0.0)
            allowed = 1.0 - cut * (1.0 - allowed)
        allowed = jnp.concatenate([allowed, allowed], axis=1)
        win_queries = projected[:, :D]
        win_keys = projected[:, D : 2 * D] * factor
        win_values = projected[:, 2 * D :] * (factor * (1.0 / HEAD_DIM))
        halves = [slice(i * HALF, (i + 1) * HALF) for i in range(2)]

        def apart(rows):
            return jnp.concatenate(
                [jnp.where(half_head == h, rows, 0.0) for h in range(HEADS // 2)], axis=0
            )

        keys = [apart(win_keys[:, half]) for half in halves]
        scores = [
            mm_t(win_queries[:, half].astype(BF16), key.astype(BF16))
            for half, key in zip(halves, keys)
        ]
        queries = jnp.concatenate([win_queries[:, half] for half in halves], axis=0)
        query_square = mm((queries * queries).astype(BF16), ones_ref[...])
        key_squares = [mm_t(each, (key * key).astype(BF16))[:1] for key in keys]
        values = [
            jnp.concatenate([apart(win_values[:, half]).astype(BF16), ones_ref[...]], axis=1)
            for half in halves
        ]
        weights = []
        for i in range(2):
            square = query_square[i * TOKENS : (i + 1) * TOKENS]
            scale = lax.rsqrt(factor * factor * square + head_eps) * (factor * SCORE_SCALE)
            scale = scale * lax.rsqrt(key_squares[i] + head_eps)
            weights.append((jnp.exp2(scores[i] * scale) * allowed).astype(BF16))
        both = [mm(weights[i], values[i]) for i in range(2)]
        mixed = [(each_both[:, :HALF] / each_both[:, HALF:]).astype(BF16) for each_both in both]
        wait(turn_index, 1)
        attended = latents + mm(jnp.concatenate(mixed, axis=1), proj_ref[...])
        wait(turn_index, 2)
        centred = centre(attended)
        normed = (centred * entry(GAIN_ROW + 2)).astype(BF16)
        units = [slice(i * MLP // 2, (i + 1) * MLP // 2) for i in range(2)]
        hidden = [mm(normed, up_ref[:, unit]) for unit in units]
        factor = row_factor(centred)
        first = gelu(hidden[0] * factor).astype(BF16)
        wait(turn_index, 3)
        first = mm(first, down_ref[units[0], :])
        second = gelu(hidden[1] * factor).astype(BF16)
        backbone = attended + first + mm(second, down_ref[units[1], :])
        first, second = backbone[:PATCHES], backbone[PATCHES:]
        blended = jnp.concatenate(
            [mixing(l, 0) * first + mixing(l, 1) * second + embed(l) for l in range(LEV)], axis=0
        )
        centred = centre(blended)
        added = mm((centred * entry(GAIN_ROW + 3)).astype(BF16), dec_ref[...])
        current = (current + added * row_factor(centred)).astype(BF16).astype(F32)

    for l in range(LEV):
        wide[:, l * PIN : (l + 1) * PIN] = current[l * PATCHES : (l + 1) * PATCHES]
    out_ref[0] = wide[...].astype(BF16).reshape(out_ref.shape[1:])


def forecast(windows, arranged, early, late):
    vmem = pl.BlockSpec(memory_space=pltpu.VMEM)
    if windows == 1:
        block, grid = vmem, ()
        result = pltpu.VMEM(arranged.shape, BF16)
        arranged = pltpu.with_memory_space_constraint(arranged, pltpu.VMEM)
    else:
        result = jax.ShapeDtypeStruct(arranged.shape, BF16)
        block = pl.BlockSpec((1,) + arranged.shape[1:], lambda i: (i, 0, 0, 0))
        grid = (windows,)
    early = [pltpu.with_memory_space_constraint(a, pltpu.VMEM) for a in early]
    return pl.pallas_call(
        functools.partial(forecast_kernel, windows),
        grid=grid,
        in_specs=[vmem] * EARLY + [pl.BlockSpec(memory_space=pl.ANY)] * LATE + [block],
        out_specs=block,
        out_shape=result,
        scratch_shapes=[pltpu.VMEM(a.shape, a.dtype) for a in late]
        + [
            pltpu.VMEM((PATCHES, LEV * PIN), F32),
            pltpu.SemaphoreType.DMA((LATE,)),
        ],
        compiler_params=pltpu.CompilerParams(vmem_limit_bytes=MAIN_LIMIT),
    )(*early, *late, arranged)


def turn_out_kernel(step, x_ref, out_ref, token_ref, near, arrivals):
    count, size = out_ref.shape[:2]
    copies = [
        pltpu.make_async_copy(
            x_ref.at[pl.ds(i * CHUNK, CHUNK)], near.at[pl.ds(i * CHUNK, CHUNK)], arrivals.at[i]
        )
        for i in range(count * size // CHUNK)
    ]
    for copy in copies:
        copy.start()
    token_ref[...] = jnp.zeros_like(token_ref)
    shift = jnp.where(lax.axis_index("lon") < step, 1, 0)
    blocks = CHUNK // size
    for i, copy in enumerate(copies):
        copy.wait()
        piece = near[i * CHUNK : (i + 1) * CHUNK, :].reshape((blocks,) + out_ref.shape[1:])
        for j in range(blocks):
            out_ref[lax.rem(i * blocks + j + count - shift, count)] = piece[j]


def turn_back_kernel(step, x_ref, out_ref):
    count = x_ref.shape[0]
    shift = jnp.where(lax.axis_index("lon") < step, 1, 0)
    blocks = [x_ref[lax.rem(i + count - shift, count)] for i in range(count)]
    out_ref[...] = jnp.stack(blocks).reshape(out_ref.shape)


def turn_out(array, shape, step, near):
    return pl.pallas_call(
        functools.partial(turn_out_kernel, step),
        in_specs=[pl.BlockSpec(memory_space=pl.ANY)],
        out_shape=[
            pltpu.VMEM(shape, BF16) if near else jax.ShapeDtypeStruct(shape, BF16),
            pltpu.VMEM((8, LANES), F32),
        ],
        out_specs=[pl.BlockSpec(memory_space=pltpu.VMEM)] * 2,
        scratch_shapes=[
            pltpu.VMEM(array.shape, BF16),
            pltpu.SemaphoreType.DMA((array.shape[0] // CHUNK,)),
        ],
    )(array)


def turn_back(array, shape, step, near):
    if near:
        array = pltpu.with_memory_space_constraint(array, pltpu.VMEM)
    return pl.pallas_call(
        functools.partial(turn_back_kernel, step),
        out_shape=jax.ShapeDtypeStruct(shape, BF16),
        compiler_params=pltpu.CompilerParams(vmem_limit_bytes=TURN_LIMIT),
    )(array)


def shards(
    fields,
    level_ids,
    embed_weight,
    level_embed,
    enc_gain,
    latent_query,
    kv_weight,
    pool_out,
    attn_gain,
    qkv_weight,
    attn_proj,
    mlp_gain,
    mlp_up,
    mlp_down,
    level_mix,
    dec_gain,
    dec_weight,
):
    devices = lax.axis_size("lon")
    width = fields.shape[2]
    local_count = fields.shape[1]
    piece_cols = local_count // devices
    lat_count = devices // ROW_PARTS
    bands = lat_count // W_LAT
    cut = (W_LON // 2 // piece_cols) * lat_count
    scalars = (level_ids, level_mix.T)
    rows = (
        level_embed,
        latent_query,
        enc_gain.reshape(1, D),
        attn_gain.reshape(1, D),
        mlp_gain.reshape(1, D),
        dec_gain.reshape(1, D),
    )
    outgoing, token = turn_out(
        fields.reshape(local_count, width), (devices, piece_cols, width), cut, bands == 1
    )
    early = load(token, scalars, rows, dec_weight.T, (embed_weight, kv_weight, pool_out))
    late = (qkv_weight, attn_proj, mlp_up, mlp_down)
    got = lax.all_to_all(outgoing, "lon", split_axis=0, concat_axis=0, tiled=True)
    if bands > 1:
        got = got.reshape(ROW_PARTS, lat_count, piece_cols, width)
        got = jnp.roll(got, -(W_LAT // 2), axis=1)
        got = got.reshape(ROW_PARTS, bands, W_LAT, piece_cols, width).transpose(1, 0, 2, 3, 4)
    done = forecast(bands, got.reshape(bands, ROW_PARTS * W_LAT, piece_cols, width), early, late)
    if bands > 1:
        done = done.reshape(bands, ROW_PARTS, W_LAT, piece_cols, width).transpose(1, 0, 2, 3, 4)
        done = done.reshape(ROW_PARTS, lat_count, piece_cols, width)
        done = jnp.roll(done, W_LAT // 2, axis=1)
    done = done.reshape(devices, piece_cols, width)
    home = lax.all_to_all(done, "lon", split_axis=0, concat_axis=0, tiled=True)
    forecast_here = turn_back(home, (local_count, width), cut, bands == 1)
    return forecast_here.reshape(fields.shape)


def solution(mesh):
    placed = (P(("groups", "lon"), None, None), P("groups")) + (P(),) * 15
    return jax.shard_map(
        shards,
        mesh=mesh,
        in_specs=placed,
        out_specs=P(("groups", "lon"), None, None),
        check_vma=False,
    )
```

```python
import functools
import math

import jax
import jax.numpy as jnp
from jax import lax
from jax.experimental import pallas as pl
from jax.experimental.pallas import tpu as pltpu
from jax.sharding import PartitionSpec as P

D = 512
HEADS = 8
HEAD_DIM = D // HEADS
PIN = 500
LEV = 3
LATL = 2
W_LAT = 4
W_LON = 8
STEPS = 2
ROW_PARTS = 4
MLP = 2048
PATCHES = W_LAT * W_LON
TOKENS = PATCHES * LATL
HALF = D // 2
PAIR = 2 * HEAD_DIM
EARLY, LATE = 10, 4
LANES = 128
CHUNK = 16
LOAD_LIMIT = 56 * 1024 * 1024
TURN_LIMIT = 16 * 1024 * 1024
MAIN_LIMIT = 56 * 1024 * 1024
EMBED_ROW, MIX_ROW, LATENT_ROW, GAIN_ROW, TABLE_ROWS = 0, 3, 9, 11, 16

GELU_FIRST = math.sqrt(2.0 / math.pi)
GELU_THIRD = 0.044715 * GELU_FIRST
SCORE_SCALE = HEAD_DIM ** (-0.5) * math.log2(math.e)

norm_eps = 1e-05
head_eps = 1e-06

F32 = jnp.float32
BF16 = jnp.bfloat16


def mm(a, b):
    return jnp.dot(a, b, preferred_element_type=F32)


def mm_t(a, b):
    return lax.dot_general(a, b, (((1,), (1,)), ((), ())), preferred_element_type=F32)


def row_factor(centred):
    return lax.rsqrt(jnp.mean(centred * centred, axis=-1, keepdims=True) + norm_eps)


def centre(rows):
    return rows - jnp.mean(rows, axis=-1, keepdims=True)


def gelu(values):
    curve = values * (GELU_FIRST + GELU_THIRD * (values * values))
    half = 0.5 * values
    return half + half * jnp.tanh(curve)


def iota(shape, dim):
    return lax.broadcasted_iota(jnp.int32, shape, dim)


def load_kernel(*refs):
    (
        ids_from,
        mix_from,
        level_embed_from,
        latent_query_from,
        enc_gain_from,
        attn_gain_from,
        mlp_gain_from,
        dec_gain_from,
        dec_from,
        embed_from,
        kv_from,
        pool_from,
        _,
        table_ref,
        query_ref,
        mean_ref,
        spread_ref,
        ones_ref,
        allowed_ref,
        dec_ref,
        embed_ref,
        kv_ref,
        pool_ref,
        ids_ref,
        mix_ref,
        level_embed_ref,
        latent_query_ref,
        gain_refs,
        dec_rows_ref,
        embed_rows_ref,
        pool_rows_ref,
        arrivals,
    ) = refs
    pairs = [
        (ids_from, ids_ref),
        (mix_from, mix_ref),
        (level_embed_from, level_embed_ref),
        (latent_query_from, latent_query_ref),
        (enc_gain_from, gain_refs.at[0]),
        (attn_gain_from, gain_refs.at[1]),
        (mlp_gain_from, gain_refs.at[2]),
        (dec_gain_from, gain_refs.at[3]),
        (dec_from, dec_rows_ref),
        (embed_from, embed_rows_ref),
        (pool_from, pool_rows_ref),
        (kv_from, kv_ref),
    ]
    copies = [
        pltpu.make_async_copy(here, there, arrivals.at[i]) for i, (here, there) in enumerate(pairs)
    ]
    for copy in copies:
        copy.start()

    feature_head = iota((D, LANES), 0) // HEAD_DIM
    lane = iota((D, LANES), 1)
    on_head = (feature_head == lane % HEADS) & (lane < LATL * HEADS)
    mean_ref[...] = jnp.where(on_head, 1.0 / HEAD_DIM, 0.0).astype(BF16)
    spread_ref[...] = jnp.where(
        iota((LATL * HEADS, LATL * D), 0) == iota((LATL * HEADS, LATL * D), 1) // HEAD_DIM, 1.0, 0.0
    ).astype(BF16)
    ones_ref[...] = jnp.where(
        iota((HALF, HALF), 0) // HEAD_DIM == iota((HALF, HALF), 1) // HEAD_DIM, 1.0 / HEAD_DIM, 0.0
    ).astype(BF16)
    row_bit = (iota((TOKENS, PAIR), 0) // 4) % 2
    lane_bit = (iota((TOKENS, PAIR), 1) // 4) % 2
    allowed_ref[...] = jnp.where(row_bit == lane_bit, 1.0, 0.0)

    for copy in copies[:8]:
        copy.wait()
    level_embed = centre(level_embed_ref[...].astype(F32))
    for l in range(LEV):
        level = ids_ref[l]
        row = level_embed[LEV - 1 : LEV]
        for i in reversed(range(LEV - 1)):
            row = jnp.where(level == i, level_embed[i : i + 1], row)
        table_ref[EMBED_ROW + l : EMBED_ROW + l + 1, :] = row
        for j in range(LATL):
            at = MIX_ROW + l * LATL + j
            table_ref[at : at + 1, :] = jnp.full((1, D), mix_ref[j, level])
    latent = latent_query_ref[...].astype(F32)
    table_ref[LATENT_ROW : LATENT_ROW + LATL, :] = centre(latent)
    for i in range(4):
        table_ref[GAIN_ROW + i : GAIN_ROW + i + 1, :] = gain_refs[i]
    row_id = iota((LANES, D), 0)
    own_head = (row_id % HEADS) == iota((LANES, D), 1) // HEAD_DIM
    spots = jnp.zeros((LANES, D), F32)
    for j in range(LATL):
        mine = own_head & (row_id // HEADS == j)
        spots = jnp.where(mine, jnp.broadcast_to(latent[j : j + 1], (LANES, D)), spots)
    mean_square = jnp.sum(spots * spots, axis=-1, keepdims=True) / HEAD_DIM
    query_ref[...] = (spots * lax.rsqrt(mean_square + head_eps)).T.astype(BF16)

    copies[8].wait()
    dec_ref[...] = dec_rows_ref[...].astype(F32).T.astype(BF16)
    copies[9].wait()
    embed_ref[...] = centre(embed_rows_ref[...].astype(F32)).astype(BF16)
    copies[10].wait()
    pool_ref[...] = centre(pool_rows_ref[...].astype(F32)).astype(BF16)
    copies[11].wait()


def load(after, scalars, rows, dec, early):
    far = pl.BlockSpec(memory_space=pl.ANY)
    made = [
        pltpu.VMEM((TABLE_ROWS, D), F32),
        pltpu.VMEM((D, LANES), BF16),
        pltpu.VMEM((D, LANES), BF16),
        pltpu.VMEM((LATL * HEADS, LATL * D), BF16),
        pltpu.VMEM((HALF, HALF), BF16),
        pltpu.VMEM((TOKENS, PAIR), F32),
        pltpu.VMEM(dec.shape[::-1], BF16),
    ] + [pltpu.VMEM(a.shape, a.dtype) for a in early]
    inputs = (*scalars, *rows, dec, *early)
    return pl.pallas_call(
        load_kernel,
        in_specs=[far] * len(inputs) + [pl.BlockSpec(memory_space=pltpu.VMEM)],
        out_specs=[pl.BlockSpec(memory_space=pltpu.VMEM)] * len(made),
        out_shape=made,
        scratch_shapes=[pltpu.SMEM(a.shape, a.dtype) for a in scalars]
        + [
            pltpu.VMEM((LEV, D), BF16),
            pltpu.VMEM((LATL, D), BF16),
            pltpu.VMEM((4, 1, D), F32),
            pltpu.VMEM(dec.shape, BF16),
            pltpu.VMEM(early[0].shape, BF16),
            pltpu.VMEM(early[2].shape, BF16),
            pltpu.SemaphoreType.DMA((len(inputs),)),
        ],
        compiler_params=pltpu.CompilerParams(vmem_limit_bytes=LOAD_LIMIT),
        cost_estimate=pl.CostEstimate(flops=0, bytes_accessed=8_000_000, transcendentals=0),
    )(*inputs, pltpu.with_memory_space_constraint(after, pltpu.VMEM))


def forecast_kernel(windows, *refs):
    (
        table_ref,
        query_ref,
        mean_ref,
        spread_ref,
        ones_ref,
        allowed_ref,
        dec_ref,
        embed_ref,
        kv_ref,
        pool_ref,
    ) = refs[:EARLY]
    far, (x_ref, out_ref), refs = refs[EARLY:][:LATE], refs[EARLY + LATE :][:2], refs[EARLY + LATE + 2 :]
    near, (wide, arrivals) = refs[:LATE], refs[LATE:]
    qkv_ref, proj_ref, up_ref, down_ref = near
    copies = [
        pltpu.make_async_copy(far[i], near[i], arrivals.at[i]) for i in range(LATE)
    ]

    def in_first_window(action):
        if windows == 1:
            action()
        else:
            pl.when(pl.program_id(0) == 0)(action)

    def start(*wanted):
        def action():
            for i in wanted:
                copies[i].start()

        in_first_window(action)

    def wait(turn_index, *wanted):
        def action():
            for i in wanted:
                copies[i].wait()

        if turn_index == 0:
            in_first_window(action)

    start(0, 1)

    def entry(at):
        return table_ref[at : at + 1, :]

    def embed(l):
        return entry(EMBED_ROW + l)

    def mixing(l, j):
        return entry(MIX_ROW + l * LATL + j)

    half_head = iota((1, HALF), 1) // HEAD_DIM
    each = jnp.full((16, HALF), 1.0 / HEAD_DIM, BF16)

    arrived = x_ref[0].reshape(PATCHES, LEV * PIN).astype(F32)
    current = jnp.concatenate(
        [arrived[:, l * PIN : (l + 1) * PIN] for l in range(LEV)], axis=0
    )

    start(2)

    def by_level(values):
        return [values[l * PATCHES : (l + 1) * PATCHES] for l in range(LEV)]

    for turn_index in range(STEPS):
        tokens = by_level(mm(current.astype(BF16), embed_ref[...]))
        tokens = jnp.concatenate([tokens[l] + embed(l) for l in range(LEV)], axis=0)
        keyval = mm((tokens * entry(GAIN_ROW)).astype(BF16), kv_ref[...])
        if turn_index == 0:
            start(3)
        factor = row_factor(tokens)
        keys = keyval[:, :D]
        values = by_level(keyval[:, D:])
        stacked = jnp.concatenate([keys.astype(BF16), (keys * keys).astype(BF16)], axis=0)
        tables = jnp.concatenate([query_ref[...], mean_ref[...]], axis=1)
        found = mm(stacked, tables)
        rows = LEV * PATCHES
        scores = found[:rows, : LATL * HEADS]
        mean_square = found[rows:, LANES : LANES + LATL * HEADS]
        scale = factor * lax.rsqrt(factor * factor * mean_square + head_eps)
        parts = by_level(jnp.exp2(scores * (scale * SCORE_SCALE)))
        inverse = 1.0 / (parts[0] + parts[1] + parts[2])
        factors = by_level(factor)
        weights = jnp.concatenate(
            [parts[l] * (inverse * factors[l]) for l in range(LEV)], axis=0
        ).astype(BF16)
        wide_weights = by_level(mm(weights, spread_ref[...]))
        pooled = []
        for j in range(LATL):
            terms = [wide_weights[l][:, j * D : (j + 1) * D] * values[l] for l in range(LEV)]
            pooled.append(terms[0] + terms[1] + terms[2])
        latents = mm(jnp.concatenate(pooled, axis=0).astype(BF16), pool_ref[...])
        latents = jnp.concatenate(
            [
                latents[j * PATCHES : (j + 1) * PATCHES] + entry(LATENT_ROW + j)
                for j in range(LATL)
            ],
            axis=0,
        )
        wait(turn_index, 0)
        projected = mm((latents * entry(GAIN_ROW + 1)).astype(BF16), qkv_ref[...])
        factor = row_factor(latents)
        allowed = allowed_ref[...]
        if windows > 1:
            cut = jnp.where(pl.program_id(0) == windows - 1, 1.0, 0.0)
            allowed = 1.0 - cut * (1.0 - allowed)
        allowed = jnp.concatenate([allowed, allowed], axis=1)
        win_queries = projected[:, :D]
        win_keys = projected[:, D : 2 * D] * factor
        win_values = projected[:, 2 * D :] * (factor * (1.0 / HEAD_DIM))
        halves = [slice(i * HALF, (i + 1) * HALF) for i in range(2)]

        def apart(rows):
            return jnp.concatenate(
                [jnp.where(half_head == h, rows, 0.0) for h in range(HEADS // 2)], axis=0
            )

        keys = [apart(win_keys[:, half]) for half in halves]
        scores = [
            mm_t(win_queries[:, half].astype(BF16), key.astype(BF16))
            for half, key in zip(halves, keys)
        ]
        queries = jnp.concatenate([win_queries[:, half] for half in halves], axis=0)
        query_square = mm((queries * queries).astype(BF16), ones_ref[...])
        key_squares = [mm_t(each, (key * key).astype(BF16))[:1] for key in keys]
        values = [
            jnp.concatenate([apart(win_values[:, half]).astype(BF16), ones_ref[...]], axis=1)
            for half in halves
        ]
        weights = []
        for i in range(2):
            square = query_square[i * TOKENS : (i + 1) * TOKENS]
            scale = lax.rsqrt(factor * factor * square + head_eps) * (factor * SCORE_SCALE)
            scale = scale * lax.rsqrt(key_squares[i] + head_eps)
            weights.append((jnp.exp2(scores[i] * scale) * allowed).astype(BF16))
        both = [mm(weights[i], values[i]) for i in range(2)]
        mixed = [(each_both[:, :HALF] / each_both[:, HALF:]).astype(BF16) for each_both in both]
        wait(turn_index, 1)
        attended = latents + mm(jnp.concatenate(mixed, axis=1), proj_ref[...])
        wait(turn_index, 2)
        centred = centre(attended)
        normed = (centred * entry(GAIN_ROW + 2)).astype(BF16)
        units = [slice(i * MLP // 2, (i + 1) * MLP // 2) for i in range(2)]
        hidden = [mm(normed, up_ref[:, unit]) for unit in units]
        factor = row_factor(centred)
        first = gelu(hidden[0] * factor).astype(BF16)
        wait(turn_index, 3)
        first = mm(first, down_ref[units[0], :])
        second = gelu(hidden[1] * factor).astype(BF16)
        backbone = attended + first + mm(second, down_ref[units[1], :])
        first, second = backbone[:PATCHES], backbone[PATCHES:]
        blended = jnp.concatenate(
            [mixing(l, 0) * first + mixing(l, 1) * second + embed(l) for l in range(LEV)], axis=0
        )
        centred = centre(blended)
        added = mm((centred * entry(GAIN_ROW + 3)).astype(BF16), dec_ref[...])
        current = (current + added * row_factor(centred)).astype(BF16).astype(F32)

    for l in range(LEV):
        wide[:, l * PIN : (l + 1) * PIN] = current[l * PATCHES : (l + 1) * PATCHES]
    out_ref[0] = wide[...].astype(BF16).reshape(out_ref.shape[1:])


def forecast(windows, arranged, early, late):
    vmem = pl.BlockSpec(memory_space=pltpu.VMEM)
    if windows == 1:
        block, grid = vmem, ()
        result = pltpu.VMEM(arranged.shape, BF16)
        arranged = pltpu.with_memory_space_constraint(arranged, pltpu.VMEM)
    else:
        result = jax.ShapeDtypeStruct(arranged.shape, BF16)
        block = pl.BlockSpec((1,) + arranged.shape[1:], lambda i: (i, 0, 0, 0))
        grid = (windows,)
    early = [pltpu.with_memory_space_constraint(a, pltpu.VMEM) for a in early]
    return pl.pallas_call(
        functools.partial(forecast_kernel, windows),
        grid=grid,
        in_specs=[vmem] * EARLY + [pl.BlockSpec(memory_space=pl.ANY)] * LATE + [block],
        out_specs=block,
        out_shape=result,
        scratch_shapes=[pltpu.VMEM(a.shape, a.dtype) for a in late]
        + [
            pltpu.VMEM((PATCHES, LEV * PIN), F32),
            pltpu.SemaphoreType.DMA((LATE,)),
        ],
        compiler_params=pltpu.CompilerParams(vmem_limit_bytes=MAIN_LIMIT),
    )(*early, *late, arranged)


def turn_out_kernel(step, x_ref, out_ref, token_ref, near, arrivals):
    count, size = out_ref.shape[:2]
    copies = [
        pltpu.make_async_copy(
            x_ref.at[pl.ds(i * CHUNK, CHUNK)], near.at[pl.ds(i * CHUNK, CHUNK)], arrivals.at[i]
        )
        for i in range(count * size // CHUNK)
    ]
    for copy in copies:
        copy.start()
    token_ref[...] = jnp.zeros_like(token_ref)
    shift = jnp.where(lax.axis_index("lon") < step, 1, 0)
    blocks = CHUNK // size
    for i, copy in enumerate(copies):
        copy.wait()
        piece = near[i * CHUNK : (i + 1) * CHUNK, :].reshape((blocks,) + out_ref.shape[1:])
        for j in range(blocks):
            out_ref[lax.rem(i * blocks + j + count - shift, count)] = piece[j]


def turn_back_kernel(step, x_ref, out_ref):
    count = x_ref.shape[0]
    shift = jnp.where(lax.axis_index("lon") < step, 1, 0)
    blocks = [x_ref[lax.rem(i + count - shift, count)] for i in range(count)]
    out_ref[...] = jnp.stack(blocks).reshape(out_ref.shape)


def turn_out(array, shape, step, near):
    return pl.pallas_call(
        functools.partial(turn_out_kernel, step),
        in_specs=[pl.BlockSpec(memory_space=pl.ANY)],
        out_shape=[
            pltpu.VMEM(shape, BF16) if near else jax.ShapeDtypeStruct(shape, BF16),
            pltpu.VMEM((8, LANES), F32),
        ],
        out_specs=[pl.BlockSpec(memory_space=pltpu.VMEM)] * 2,
        scratch_shapes=[
            pltpu.VMEM(array.shape, BF16),
            pltpu.SemaphoreType.DMA((array.shape[0] // CHUNK,)),
        ],
    )(array)


def turn_back(array, shape, step, near):
    if near:
        array = pltpu.with_memory_space_constraint(array, pltpu.VMEM)
    return pl.pallas_call(
        functools.partial(turn_back_kernel, step),
        out_shape=jax.ShapeDtypeStruct(shape, BF16),
        compiler_params=pltpu.CompilerParams(vmem_limit_bytes=TURN_LIMIT),
    )(array)


def shards(
    fields,
    level_ids,
    embed_weight,
    level_embed,
    enc_gain,
    latent_query,
    kv_weight,
    pool_out,
    attn_gain,
    qkv_weight,
    attn_proj,
    mlp_gain,
    mlp_up,
    mlp_down,
    level_mix,
    dec_gain,
    dec_weight,
):
    devices = lax.axis_size("lon")
    width = fields.shape[2]
    local_count = fields.shape[1]
    piece_cols = local_count // devices
    lat_count = devices // ROW_PARTS
    bands = lat_count // W_LAT
    cut = (W_LON // 2 // piece_cols) * lat_count
    scalars = (level_ids, level_mix.T)
    rows = (
        level_embed,
        latent_query,
        enc_gain.reshape(1, D),
        attn_gain.reshape(1, D),
        mlp_gain.reshape(1, D),
        dec_gain.reshape(1, D),
    )
    outgoing, token = turn_out(
        fields.reshape(local_count, width), (devices, piece_cols, width), cut, bands == 1
    )
    early = load(token, scalars, rows, dec_weight.T, (embed_weight, kv_weight, pool_out))
    late = (qkv_weight, attn_proj, mlp_up, mlp_down)
    got = lax.all_to_all(outgoing, "lon", split_axis=0, concat_axis=0, tiled=True)
    if bands > 1:
        got = got.reshape(ROW_PARTS, lat_count, piece_cols, width)
        got = jnp.roll(got, -(W_LAT // 2), axis=1)
        got = got.reshape(ROW_PARTS, bands, W_LAT, piece_cols, width).transpose(1, 0, 2, 3, 4)
    done = forecast(bands, got.reshape(bands, ROW_PARTS * W_LAT, piece_cols, width), early, late)
    if bands > 1:
        done = done.reshape(bands, ROW_PARTS, W_LAT, piece_cols, width).transpose(1, 0, 2, 3, 4)
        done = done.reshape(ROW_PARTS, lat_count, piece_cols, width)
        done = jnp.roll(done, W_LAT // 2, axis=1)
    done = done.reshape(devices, piece_cols, width)
    home = lax.all_to_all(done, "lon", split_axis=0, concat_axis=0, tiled=True)
    forecast_here = turn_back(home, (local_count, width), cut, bands == 1)
    return forecast_here.reshape(fields.shape)


def solution(mesh):
    placed = (P(("groups", "lon"), None, None), P("groups")) + (P(),) * 15
    return jax.shard_map(
        shards,
        mesh=mesh,
        in_specs=placed,
        out_specs=P(("groups", "lon"), None, None),
        check_vma=False,
    )
```

```python
import functools
import math

import jax
import jax.numpy as jnp
from jax import lax
from jax.experimental import pallas as pl
from jax.experimental.pallas import tpu as pltpu
from jax.sharding import PartitionSpec as P

D = 512
HEADS = 8
HEAD_DIM = D // HEADS
PIN = 500
LEV = 3
LATL = 2
W_LAT = 4
W_LON = 8
STEPS = 2
ROW_PARTS = 4
MLP = 2048
PATCHES = W_LAT * W_LON
TOKENS = PATCHES * LATL
HALF = D // 2
PAIR = 2 * HEAD_DIM
EARLY, LATE = 10, 4
LANES = 128
CHUNK = 16
LOAD_LIMIT = 56 * 1024 * 1024
TURN_LIMIT = 16 * 1024 * 1024
MAIN_LIMIT = 56 * 1024 * 1024
EMBED_ROW, MIX_ROW, LATENT_ROW, GAIN_ROW, TABLE_ROWS = 0, 3, 9, 11, 16

GELU_FIRST = math.sqrt(2.0 / math.pi)
GELU_THIRD = 0.044715 * GELU_FIRST
SCORE_SCALE = HEAD_DIM ** (-0.5) * math.log2(math.e)

norm_eps = 1e-05
head_eps = 1e-06

F32 = jnp.float32
BF16 = jnp.bfloat16


def mm(a, b):
    return jnp.dot(a, b, preferred_element_type=F32)


def mm_t(a, b):
    return lax.dot_general(a, b, (((1,), (1,)), ((), ())), preferred_element_type=F32)


def row_factor(centred):
    return lax.rsqrt(jnp.mean(centred * centred, axis=-1, keepdims=True) + norm_eps)


def centre(rows):
    return rows - jnp.mean(rows, axis=-1, keepdims=True)


def gelu(values):
    curve = values * (GELU_FIRST + GELU_THIRD * (values * values))
    half = 0.5 * values
    return half + half * jnp.tanh(curve)


def iota(shape, dim):
    return lax.broadcasted_iota(jnp.int32, shape, dim)


def load_kernel(*refs):
    (
        ids_from,
        mix_from,
        level_embed_from,
        latent_query_from,
        enc_gain_from,
        attn_gain_from,
        mlp_gain_from,
        dec_gain_from,
        dec_from,
        embed_from,
        kv_from,
        pool_from,
        _,
        table_ref,
        query_ref,
        mean_ref,
        spread_ref,
        ones_ref,
        allowed_ref,
        dec_ref,
        embed_ref,
        kv_ref,
        pool_ref,
        ids_ref,
        mix_ref,
        level_embed_ref,
        latent_query_ref,
        gain_refs,
        dec_rows_ref,
        embed_rows_ref,
        pool_rows_ref,
        arrivals,
    ) = refs
    pairs = [
        (ids_from, ids_ref),
        (mix_from, mix_ref),
        (level_embed_from, level_embed_ref),
        (latent_query_from, latent_query_ref),
        (enc_gain_from, gain_refs.at[0]),
        (attn_gain_from, gain_refs.at[1]),
        (mlp_gain_from, gain_refs.at[2]),
        (dec_gain_from, gain_refs.at[3]),
        (dec_from, dec_rows_ref),
        (embed_from, embed_rows_ref),
        (pool_from, pool_rows_ref),
        (kv_from, kv_ref),
    ]
    copies = [
        pltpu.make_async_copy(here, there, arrivals.at[i]) for i, (here, there) in enumerate(pairs)
    ]
    for copy in copies:
        copy.start()

    feature_head = iota((D, LANES), 0) // HEAD_DIM
    lane = iota((D, LANES), 1)
    on_head = (feature_head == lane % HEADS) & (lane < LATL * HEADS)
    mean_ref[...] = jnp.where(on_head, 1.0 / HEAD_DIM, 0.0).astype(BF16)
    spread_ref[...] = jnp.where(
        iota((LATL * HEADS, LATL * D), 0) == iota((LATL * HEADS, LATL * D), 1) // HEAD_DIM, 1.0, 0.0
    ).astype(BF16)
    ones_ref[...] = jnp.where(
        iota((HALF, HALF), 0) // HEAD_DIM == iota((HALF, HALF), 1) // HEAD_DIM, 1.0 / HEAD_DIM, 0.0
    ).astype(BF16)
    row_bit = (iota((TOKENS, PAIR), 0) // 4) % 2
    lane_bit = (iota((TOKENS, PAIR), 1) // 4) % 2
    allowed_ref[...] = jnp.where(row_bit == lane_bit, 1.0, 0.0)

    for copy in copies[:8]:
        copy.wait()
    level_embed = centre(level_embed_ref[...].astype(F32))
    for l in range(LEV):
        level = ids_ref[l]
        row = level_embed[LEV - 1 : LEV]
        for i in reversed(range(LEV - 1)):
            row = jnp.where(level == i, level_embed[i : i + 1], row)
        table_ref[EMBED_ROW + l : EMBED_ROW + l + 1, :] = row
        for j in range(LATL):
            at = MIX_ROW + l * LATL + j
            table_ref[at : at + 1, :] = jnp.full((1, D), mix_ref[j, level])
    latent = latent_query_ref[...].astype(F32)
    table_ref[LATENT_ROW : LATENT_ROW + LATL, :] = centre(latent)
    for i in range(4):
        table_ref[GAIN_ROW + i : GAIN_ROW + i + 1, :] = gain_refs[i]
    row_id = iota((LANES, D), 0)
    own_head = (row_id % HEADS) == iota((LANES, D), 1) // HEAD_DIM
    spots = jnp.zeros((LANES, D), F32)
    for j in range(LATL):
        mine = own_head & (row_id // HEADS == j)
        spots = jnp.where(mine, jnp.broadcast_to(latent[j : j + 1], (LANES, D)), spots)
    mean_square = jnp.sum(spots * spots, axis=-1, keepdims=True) / HEAD_DIM
    query_ref[...] = (spots * lax.rsqrt(mean_square + head_eps)).T.astype(BF16)

    copies[8].wait()
    dec_ref[...] = dec_rows_ref[...].astype(F32).T.astype(BF16)
    copies[9].wait()
    embed_ref[...] = centre(embed_rows_ref[...].astype(F32)).astype(BF16)
    copies[10].wait()
    pool_ref[...] = centre(pool_rows_ref[...].astype(F32)).astype(BF16)
    copies[11].wait()


def load(after, scalars, rows, dec, early):
    far = pl.BlockSpec(memory_space=pl.ANY)
    made = [
        pltpu.VMEM((TABLE_ROWS, D), F32),
        pltpu.VMEM((D, LANES), BF16),
        pltpu.VMEM((D, LANES), BF16),
        pltpu.VMEM((LATL * HEADS, LATL * D), BF16),
        pltpu.VMEM((HALF, HALF), BF16),
        pltpu.VMEM((TOKENS, PAIR), F32),
        pltpu.VMEM(dec.shape[::-1], BF16),
    ] + [pltpu.VMEM(a.shape, a.dtype) for a in early]
    inputs = (*scalars, *rows, dec, *early)
    return pl.pallas_call(
        load_kernel,
        in_specs=[far] * len(inputs) + [pl.BlockSpec(memory_space=pltpu.VMEM)],
        out_specs=[pl.BlockSpec(memory_space=pltpu.VMEM)] * len(made),
        out_shape=made,
        scratch_shapes=[pltpu.SMEM(a.shape, a.dtype) for a in scalars]
        + [
            pltpu.VMEM((LEV, D), BF16),
            pltpu.VMEM((LATL, D), BF16),
            pltpu.VMEM((4, 1, D), F32),
            pltpu.VMEM(dec.shape, BF16),
            pltpu.VMEM(early[0].shape, BF16),
            pltpu.VMEM(early[2].shape, BF16),
            pltpu.SemaphoreType.DMA((len(inputs),)),
        ],
        compiler_params=pltpu.CompilerParams(vmem_limit_bytes=LOAD_LIMIT),
        cost_estimate=pl.CostEstimate(flops=0, bytes_accessed=8_000_000, transcendentals=0),
    )(*inputs, pltpu.with_memory_space_constraint(after, pltpu.VMEM))


def forecast_kernel(windows, *refs):
    (
        table_ref,
        query_ref,
        mean_ref,
        spread_ref,
        ones_ref,
        allowed_ref,
        dec_ref,
        embed_ref,
        kv_ref,
        pool_ref,
    ) = refs[:EARLY]
    far, (x_ref, out_ref), refs = refs[EARLY:][:LATE], refs[EARLY + LATE :][:2], refs[EARLY + LATE + 2 :]
    near, (arrivals,) = refs[:LATE], refs[LATE:]
    qkv_ref, proj_ref, up_ref, down_ref = near
    copies = [
        pltpu.make_async_copy(far[i], near[i], arrivals.at[i]) for i in range(LATE)
    ]

    def in_first_window(action):
        if windows == 1:
            action()
        else:
            pl.when(pl.program_id(0) == 0)(action)

    def start(*wanted):
        def action():
            for i in wanted:
                copies[i].start()

        in_first_window(action)

    def wait(turn_index, *wanted):
        def action():
            for i in wanted:
                copies[i].wait()

        if turn_index == 0:
            in_first_window(action)

    start(0, 1)

    def entry(at):
        return table_ref[at : at + 1, :]

    def embed(l):
        return entry(EMBED_ROW + l)

    def mixing(l, j):
        return entry(MIX_ROW + l * LATL + j)

    half_head = iota((1, HALF), 1) // HEAD_DIM
    each = jnp.full((16, HALF), 1.0 / HEAD_DIM, BF16)

    arrived = x_ref[0].reshape(PATCHES, LEV * PIN).astype(F32)
    current = jnp.concatenate(
        [arrived[:, l * PIN : (l + 1) * PIN] for l in range(LEV)], axis=0
    )

    start(2)

    def by_level(values):
        return [values[l * PATCHES : (l + 1) * PATCHES] for l in range(LEV)]

    for turn_index in range(STEPS):
        tokens = by_level(mm(current.astype(BF16), embed_ref[...]))
        tokens = jnp.concatenate([tokens[l] + embed(l) for l in range(LEV)], axis=0)
        keyval = mm((tokens * entry(GAIN_ROW)).astype(BF16), kv_ref[...])
        if turn_index == 0:
            start(3)
        factor = row_factor(tokens)
        keys = keyval[:, :D]
        values = by_level(keyval[:, D:])
        stacked = jnp.concatenate([keys.astype(BF16), (keys * keys).astype(BF16)], axis=0)
        tables = jnp.concatenate([query_ref[...], mean_ref[...]], axis=1)
        found = mm(stacked, tables)
        rows = LEV * PATCHES
        scores = found[:rows, : LATL * HEADS]
        mean_square = found[rows:, LANES : LANES + LATL * HEADS]
        scale = factor * lax.rsqrt(factor * factor * mean_square + head_eps)
        parts = by_level(jnp.exp2(scores * (scale * SCORE_SCALE)))
        inverse = 1.0 / (parts[0] + parts[1] + parts[2])
        factors = by_level(factor)
        weights = jnp.concatenate(
            [parts[l] * (inverse * factors[l]) for l in range(LEV)], axis=0
        ).astype(BF16)
        wide_weights = by_level(mm(weights, spread_ref[...]))
        pooled = []
        for j in range(LATL):
            terms = [wide_weights[l][:, j * D : (j + 1) * D] * values[l] for l in range(LEV)]
            pooled.append(terms[0] + terms[1] + terms[2])
        latents = mm(jnp.concatenate(pooled, axis=0).astype(BF16), pool_ref[...])
        latents = jnp.concatenate(
            [
                latents[j * PATCHES : (j + 1) * PATCHES] + entry(LATENT_ROW + j)
                for j in range(LATL)
            ],
            axis=0,
        )
        wait(turn_index, 0)
        projected = mm((latents * entry(GAIN_ROW + 1)).astype(BF16), qkv_ref[...])
        factor = row_factor(latents)
        allowed = allowed_ref[...]
        if windows > 1:
            cut = jnp.where(pl.program_id(0) == windows - 1, 1.0, 0.0)
            allowed = 1.0 - cut * (1.0 - allowed)
        allowed = jnp.concatenate([allowed, allowed], axis=1)
        win_queries = projected[:, :D]
        win_keys = projected[:, D : 2 * D] * factor
        win_values = projected[:, 2 * D :] * (factor * (1.0 / HEAD_DIM))
        halves = [slice(i * HALF, (i + 1) * HALF) for i in range(2)]

        def apart(rows):
            return jnp.concatenate(
                [jnp.where(half_head == h, rows, 0.0) for h in range(HEADS // 2)], axis=0
            )

        keys = [apart(win_keys[:, half]) for half in halves]
        scores = [
            mm_t(win_queries[:, half].astype(BF16), key.astype(BF16))
            for half, key in zip(halves, keys)
        ]
        queries = jnp.concatenate([win_queries[:, half] for half in halves], axis=0)
        query_square = mm((queries * queries).astype(BF16), ones_ref[...])
        key_squares = [mm_t(each, (key * key).astype(BF16))[:1] for key in keys]
        values = [
            jnp.concatenate([apart(win_values[:, half]).astype(BF16), ones_ref[...]], axis=1)
            for half in halves
        ]
        weights = []
        for i in range(2):
            square = query_square[i * TOKENS : (i + 1) * TOKENS]
            scale = lax.rsqrt(factor * factor * square + head_eps) * (factor * SCORE_SCALE)
            scale = scale * lax.rsqrt(key_squares[i] + head_eps)
            weights.append((jnp.exp2(scores[i] * scale) * allowed).astype(BF16))
        both = [mm(weights[i], values[i]) for i in range(2)]
        mixed = [(each_both[:, :HALF] / each_both[:, HALF:]).astype(BF16) for each_both in both]
        wait(turn_index, 1)
        attended = latents + mm(jnp.concatenate(mixed, axis=1), proj_ref[...])
        wait(turn_index, 2)
        centred = centre(attended)
        normed = (centred * entry(GAIN_ROW + 2)).astype(BF16)
        units = [slice(i * MLP // 2, (i + 1) * MLP // 2) for i in range(2)]
        hidden = [mm(normed, up_ref[:, unit]) for unit in units]
        factor = row_factor(centred)
        first = gelu(hidden[0] * factor).astype(BF16)
        wait(turn_index, 3)
        first = mm(first, down_ref[units[0], :])
        second = gelu(hidden[1] * factor).astype(BF16)
        backbone = attended + first + mm(second, down_ref[units[1], :])
        first, second = backbone[:PATCHES], backbone[PATCHES:]
        blended = jnp.concatenate(
            [mixing(l, 0) * first + mixing(l, 1) * second + embed(l) for l in range(LEV)], axis=0
        )
        centred = centre(blended)
        added = mm((centred * entry(GAIN_ROW + 3)).astype(BF16), dec_ref[...])
        current = (current + added * row_factor(centred)).astype(BF16).astype(F32)

    wide = jnp.concatenate(by_level(current), axis=1)
    out_ref[0] = wide.astype(BF16).reshape(out_ref.shape[1:])


def forecast(windows, arranged, early, late):
    vmem = pl.BlockSpec(memory_space=pltpu.VMEM)
    if windows == 1:
        block, grid = vmem, ()
        result = pltpu.VMEM(arranged.shape, BF16)
        arranged = pltpu.with_memory_space_constraint(arranged, pltpu.VMEM)
    else:
        result = jax.ShapeDtypeStruct(arranged.shape, BF16)
        block = pl.BlockSpec((1,) + arranged.shape[1:], lambda i: (i, 0, 0, 0))
        grid = (windows,)
    early = [pltpu.with_memory_space_constraint(a, pltpu.VMEM) for a in early]
    return pl.pallas_call(
        functools.partial(forecast_kernel, windows),
        grid=grid,
        in_specs=[vmem] * EARLY + [pl.BlockSpec(memory_space=pl.ANY)] * LATE + [block],
        out_specs=block,
        out_shape=result,
        scratch_shapes=[pltpu.VMEM(a.shape, a.dtype) for a in late]
        + [pltpu.SemaphoreType.DMA((LATE,))],
        compiler_params=pltpu.CompilerParams(vmem_limit_bytes=MAIN_LIMIT),
    )(*early, *late, arranged)


def turn_out_kernel(step, x_ref, out_ref, token_ref, near, arrivals):
    count, size = out_ref.shape[:2]
    copies = [
        pltpu.make_async_copy(
            x_ref.at[pl.ds(i * CHUNK, CHUNK)], near.at[pl.ds(i * CHUNK, CHUNK)], arrivals.at[i]
        )
        for i in range(count * size // CHUNK)
    ]
    for copy in copies:
        copy.start()
    token_ref[...] = jnp.zeros_like(token_ref)
    shift = jnp.where(lax.axis_index("lon") < step, 1, 0)
    blocks = CHUNK // size
    for i, copy in enumerate(copies):
        copy.wait()
        piece = near[i * CHUNK : (i + 1) * CHUNK, :].reshape((blocks,) + out_ref.shape[1:])
        for j in range(blocks):
            out_ref[lax.rem(i * blocks + j + count - shift, count)] = piece[j]


def turn_back_kernel(step, x_ref, out_ref):
    count = x_ref.shape[0]
    shift = jnp.where(lax.axis_index("lon") < step, 1, 0)
    blocks = [x_ref[lax.rem(i + count - shift, count)] for i in range(count)]
    out_ref[...] = jnp.stack(blocks).reshape(out_ref.shape)


def turn_out(array, shape, step, near):
    return pl.pallas_call(
        functools.partial(turn_out_kernel, step),
        in_specs=[pl.BlockSpec(memory_space=pl.ANY)],
        out_shape=[
            pltpu.VMEM(shape, BF16) if near else jax.ShapeDtypeStruct(shape, BF16),
            pltpu.VMEM((8, LANES), F32),
        ],
        out_specs=[pl.BlockSpec(memory_space=pltpu.VMEM)] * 2,
        scratch_shapes=[
            pltpu.VMEM(array.shape, BF16),
            pltpu.SemaphoreType.DMA((array.shape[0] // CHUNK,)),
        ],
    )(array)


def turn_back(array, shape, step, near):
    if near:
        array = pltpu.with_memory_space_constraint(array, pltpu.VMEM)
    return pl.pallas_call(
        functools.partial(turn_back_kernel, step),
        out_shape=jax.ShapeDtypeStruct(shape, BF16),
        compiler_params=pltpu.CompilerParams(vmem_limit_bytes=TURN_LIMIT),
    )(array)


def shards(
    fields,
    level_ids,
    embed_weight,
    level_embed,
    enc_gain,
    latent_query,
    kv_weight,
    pool_out,
    attn_gain,
    qkv_weight,
    attn_proj,
    mlp_gain,
    mlp_up,
    mlp_down,
    level_mix,
    dec_gain,
    dec_weight,
):
    devices = lax.axis_size("lon")
    width = fields.shape[2]
    local_count = fields.shape[1]
    piece_cols = local_count // devices
    lat_count = devices // ROW_PARTS
    bands = lat_count // W_LAT
    cut = (W_LON // 2 // piece_cols) * lat_count
    scalars = (level_ids, level_mix.T)
    rows = (
        level_embed,
        latent_query,
        enc_gain.reshape(1, D),
        attn_gain.reshape(1, D),
        mlp_gain.reshape(1, D),
        dec_gain.reshape(1, D),
    )
    outgoing, token = turn_out(
        fields.reshape(local_count, width), (devices, piece_cols, width), cut, bands == 1
    )
    early = load(token, scalars, rows, dec_weight.T, (embed_weight, kv_weight, pool_out))
    late = (qkv_weight, attn_proj, mlp_up, mlp_down)
    got = lax.all_to_all(outgoing, "lon", split_axis=0, concat_axis=0, tiled=True)
    if bands > 1:
        got = got.reshape(ROW_PARTS, lat_count, piece_cols, width)
        got = jnp.roll(got, -(W_LAT // 2), axis=1)
        got = got.reshape(ROW_PARTS, bands, W_LAT, piece_cols, width).transpose(1, 0, 2, 3, 4)
    done = forecast(bands, got.reshape(bands, ROW_PARTS * W_LAT, piece_cols, width), early, late)
    if bands > 1:
        done = done.reshape(bands, ROW_PARTS, W_LAT, piece_cols, width).transpose(1, 0, 2, 3, 4)
        done = done.reshape(ROW_PARTS, lat_count, piece_cols, width)
        done = jnp.roll(done, W_LAT // 2, axis=1)
    done = done.reshape(devices, piece_cols, width)
    home = lax.all_to_all(done, "lon", split_axis=0, concat_axis=0, tiled=True)
    forecast_here = turn_back(home, (local_count, width), cut, bands == 1)
    return forecast_here.reshape(fields.shape)


def solution(mesh):
    placed = (P(("groups", "lon"), None, None), P("groups")) + (P(),) * 15
    return jax.shard_map(
        shards,
        mesh=mesh,
        in_specs=placed,
        out_specs=P(("groups", "lon"), None, None),
        check_vma=False,
    )
```

```python
import functools
import math

import jax
import jax.numpy as jnp
from jax import lax
from jax.experimental import pallas as pl
from jax.experimental.pallas import tpu as pltpu
from jax.sharding import PartitionSpec as P

D = 512
HEADS = 8
HEAD_DIM = D // HEADS
PIN = 500
LEV = 3
LATL = 2
W_LAT = 4
W_LON = 8
STEPS = 2
ROW_PARTS = 4
MLP = 2048
PATCHES = W_LAT * W_LON
TOKENS = PATCHES * LATL
HALF = D // 2
PAIR = 2 * HEAD_DIM
EARLY, LATE = 10, 4
LANES = 128
CHUNK = 16
LOAD_LIMIT = 56 * 1024 * 1024
TURN_LIMIT = 16 * 1024 * 1024
MAIN_LIMIT = 56 * 1024 * 1024
EMBED_ROW, MIX_ROW, LATENT_ROW, GAIN_ROW, TABLE_ROWS = 0, 3, 9, 11, 16

GELU_FIRST = math.sqrt(2.0 / math.pi)
GELU_THIRD = 0.044715 * GELU_FIRST
SCORE_SCALE = HEAD_DIM ** (-0.5) * math.log2(math.e)

norm_eps = 1e-05
head_eps = 1e-06

F32 = jnp.float32
BF16 = jnp.bfloat16


def mm(a, b):
    return jnp.dot(a, b, preferred_element_type=F32)


def mm_t(a, b):
    return lax.dot_general(a, b, (((1,), (1,)), ((), ())), preferred_element_type=F32)


def row_factor(centred):
    return lax.rsqrt(jnp.mean(centred * centred, axis=-1, keepdims=True) + norm_eps)


def centre(rows):
    return rows - jnp.mean(rows, axis=-1, keepdims=True)


def gelu(values):
    curve = values * (GELU_FIRST + GELU_THIRD * (values * values))
    half = 0.5 * values
    return half + half * jnp.tanh(curve)


def iota(shape, dim):
    return lax.broadcasted_iota(jnp.int32, shape, dim)


def load_kernel(*refs):
    (
        ids_from,
        mix_from,
        level_embed_from,
        latent_query_from,
        enc_gain_from,
        attn_gain_from,
        mlp_gain_from,
        dec_gain_from,
        dec_from,
        embed_from,
        kv_from,
        pool_from,
        _,
        table_ref,
        query_ref,
        mean_ref,
        spread_ref,
        ones_ref,
        allowed_ref,
        dec_ref,
        embed_ref,
        kv_ref,
        pool_ref,
        ids_ref,
        mix_ref,
        level_embed_ref,
        latent_query_ref,
        gain_refs,
        dec_rows_ref,
        embed_rows_ref,
        pool_rows_ref,
        arrivals,
    ) = refs
    pairs = [
        (ids_from, ids_ref),
        (mix_from, mix_ref),
        (level_embed_from, level_embed_ref),
        (latent_query_from, latent_query_ref),
        (enc_gain_from, gain_refs.at[0]),
        (attn_gain_from, gain_refs.at[1]),
        (mlp_gain_from, gain_refs.at[2]),
        (dec_gain_from, gain_refs.at[3]),
        (dec_from, dec_rows_ref),
        (embed_from, embed_rows_ref),
        (pool_from, pool_rows_ref),
        (kv_from, kv_ref),
    ]
    copies = [
        pltpu.make_async_copy(here, there, arrivals.at[i]) for i, (here, there) in enumerate(pairs)
    ]
    for copy in copies:
        copy.start()

    feature_head = iota((D, LANES), 0) // HEAD_DIM
    lane = iota((D, LANES), 1)
    on_head = (feature_head == lane % HEADS) & (lane < LATL * HEADS)
    mean_ref[...] = jnp.where(on_head, 1.0 / HEAD_DIM, 0.0).astype(BF16)
    spread_ref[...] = jnp.where(
        iota((LATL * HEADS, LATL * D), 0) == iota((LATL * HEADS, LATL * D), 1) // HEAD_DIM, 1.0, 0.0
    ).astype(BF16)
    ones_ref[...] = jnp.where(
        iota((HALF, HALF), 0) // HEAD_DIM == iota((HALF, HALF), 1) // HEAD_DIM, 1.0 / HEAD_DIM, 0.0
    ).astype(BF16)
    row_bit = (iota((TOKENS, PAIR), 0) // 4) % 2
    lane_bit = (iota((TOKENS, PAIR), 1) // 4) % 2
    allowed_ref[...] = jnp.where(row_bit == lane_bit, 1.0, 0.0)

    for copy in copies[:8]:
        copy.wait()
    level_embed = centre(level_embed_ref[...].astype(F32))
    for l in range(LEV):
        level = ids_ref[l]
        row = level_embed[LEV - 1 : LEV]
        for i in reversed(range(LEV - 1)):
            row = jnp.where(level == i, level_embed[i : i + 1], row)
        table_ref[EMBED_ROW + l : EMBED_ROW + l + 1, :] = row
        for j in range(LATL):
            at = MIX_ROW + l * LATL + j
            table_ref[at : at + 1, :] = jnp.full((1, D), mix_ref[j, level])
    latent = latent_query_ref[...].astype(F32)
    table_ref[LATENT_ROW : LATENT_ROW + LATL, :] = centre(latent)
    for i in range(4):
        table_ref[GAIN_ROW + i : GAIN_ROW + i + 1, :] = gain_refs[i]
    row_id = iota((LANES, D), 0)
    own_head = (row_id % HEADS) == iota((LANES, D), 1) // HEAD_DIM
    spots = jnp.zeros((LANES, D), F32)
    for j in range(LATL):
        mine = own_head & (row_id // HEADS == j)
        spots = jnp.where(mine, jnp.broadcast_to(latent[j : j + 1], (LANES, D)), spots)
    mean_square = jnp.sum(spots * spots, axis=-1, keepdims=True) / HEAD_DIM
    query_ref[...] = (spots * lax.rsqrt(mean_square + head_eps)).T.astype(BF16)

    copies[8].wait()
    dec_ref[...] = dec_rows_ref[...].astype(F32).T.astype(BF16)
    copies[9].wait()
    embed_ref[...] = centre(embed_rows_ref[...].astype(F32)).astype(BF16)
    copies[10].wait()
    pool_ref[...] = centre(pool_rows_ref[...].astype(F32)).astype(BF16)
    copies[11].wait()


def load(after, scalars, rows, dec, early):
    far = pl.BlockSpec(memory_space=pl.ANY)
    made = [
        pltpu.VMEM((TABLE_ROWS, D), F32),
        pltpu.VMEM((D, LANES), BF16),
        pltpu.VMEM((D, LANES), BF16),
        pltpu.VMEM((LATL * HEADS, LATL * D), BF16),
        pltpu.VMEM((HALF, HALF), BF16),
        pltpu.VMEM((TOKENS, PAIR), F32),
        pltpu.VMEM(dec.shape[::-1], BF16),
    ] + [pltpu.VMEM(a.shape, a.dtype) for a in early]
    inputs = (*scalars, *rows, dec, *early)
    return pl.pallas_call(
        load_kernel,
        in_specs=[far] * len(inputs) + [pl.BlockSpec(memory_space=pltpu.VMEM)],
        out_specs=[pl.BlockSpec(memory_space=pltpu.VMEM)] * len(made),
        out_shape=made,
        scratch_shapes=[pltpu.SMEM(a.shape, a.dtype) for a in scalars]
        + [
            pltpu.VMEM((LEV, D), BF16),
            pltpu.VMEM((LATL, D), BF16),
            pltpu.VMEM((4, 1, D), F32),
            pltpu.VMEM(dec.shape, BF16),
            pltpu.VMEM(early[0].shape, BF16),
            pltpu.VMEM(early[2].shape, BF16),
            pltpu.SemaphoreType.DMA((len(inputs),)),
        ],
        compiler_params=pltpu.CompilerParams(vmem_limit_bytes=LOAD_LIMIT),
        cost_estimate=pl.CostEstimate(flops=0, bytes_accessed=8_000_000, transcendentals=0),
    )(*inputs, pltpu.with_memory_space_constraint(after, pltpu.VMEM))


def forecast_kernel(windows, *refs):
    (
        table_ref,
        query_ref,
        mean_ref,
        spread_ref,
        ones_ref,
        allowed_ref,
        dec_ref,
        embed_ref,
        kv_ref,
        pool_ref,
    ) = refs[:EARLY]
    far, (x_ref, out_ref), refs = refs[EARLY:][:LATE], refs[EARLY + LATE :][:2], refs[EARLY + LATE + 2 :]
    near, (arrivals,) = refs[:LATE], refs[LATE:]
    qkv_ref, proj_ref, up_ref, down_ref = near
    copies = [
        pltpu.make_async_copy(far[i], near[i], arrivals.at[i]) for i in range(LATE)
    ]

    def in_first_window(action):
        if windows == 1:
            action()
        else:
            pl.when(pl.program_id(0) == 0)(action)

    def start(*wanted):
        def action():
            for i in wanted:
                copies[i].start()

        in_first_window(action)

    def wait(turn_index, *wanted):
        def action():
            for i in wanted:
                copies[i].wait()

        if turn_index == 0:
            in_first_window(action)

    start(0, 1)

    def entry(at):
        return table_ref[at : at + 1, :]

    def embed(l):
        return entry(EMBED_ROW + l)

    def mixing(l, j):
        return entry(MIX_ROW + l * LATL + j)

    half_head = iota((1, HALF), 1) // HEAD_DIM
    each = jnp.full((16, HALF), 1.0 / HEAD_DIM, BF16)

    arrived = x_ref[0].reshape(PATCHES, LEV * PIN).astype(F32)
    current = jnp.concatenate(
        [arrived[:, l * PIN : (l + 1) * PIN] for l in range(LEV)], axis=0
    )

    start(2)

    def by_level(values):
        return [values[l * PATCHES : (l + 1) * PATCHES] for l in range(LEV)]

    for turn_index in range(STEPS):
        tokens = by_level(mm(current.astype(BF16), embed_ref[...]))
        tokens = jnp.concatenate([tokens[l] + embed(l) for l in range(LEV)], axis=0)
        keyval = mm((tokens * entry(GAIN_ROW)).astype(BF16), kv_ref[...])
        if turn_index == 0:
            start(3)
        factor = row_factor(tokens)
        keys = keyval[:, :D]
        values = by_level(keyval[:, D:])
        stacked = jnp.concatenate([keys.astype(BF16), (keys * keys).astype(BF16)], axis=0)
        tables = jnp.concatenate([query_ref[...], mean_ref[...]], axis=1)
        found = mm(stacked, tables)
        rows = LEV * PATCHES
        scores = found[:rows, : LATL * HEADS]
        mean_square = found[rows:, LANES : LANES + LATL * HEADS]
        scale = factor * lax.rsqrt(factor * factor * mean_square + head_eps)
        parts = by_level(jnp.exp2(scores * (scale * SCORE_SCALE)))
        inverse = 1.0 / (parts[0] + parts[1] + parts[2])
        factors = by_level(factor)
        weights = jnp.concatenate(
            [parts[l] * (inverse * factors[l]) for l in range(LEV)], axis=0
        ).astype(BF16)
        wide_weights = by_level(mm(weights, spread_ref[...]))
        pooled = []
        for j in range(LATL):
            terms = [wide_weights[l][:, j * D : (j + 1) * D] * values[l] for l in range(LEV)]
            pooled.append(terms[0] + terms[1] + terms[2])
        latents = mm(jnp.concatenate(pooled, axis=0).astype(BF16), pool_ref[...])
        latents = jnp.concatenate(
            [
                latents[j * PATCHES : (j + 1) * PATCHES] + entry(LATENT_ROW + j)
                for j in range(LATL)
            ],
            axis=0,
        )
        wait(turn_index, 0)
        projected = mm((latents * entry(GAIN_ROW + 1)).astype(BF16), qkv_ref[...])
        factor = row_factor(latents)
        allowed = allowed_ref[...]
        if windows > 1:
            cut = jnp.where(pl.program_id(0) == windows - 1, 1.0, 0.0)
            allowed = 1.0 - cut * (1.0 - allowed)
        allowed = jnp.concatenate([allowed, allowed], axis=1)
        win_queries = projected[:, :D]
        win_keys = projected[:, D : 2 * D] * factor
        win_values = projected[:, 2 * D :] * (factor * (1.0 / HEAD_DIM))
        halves = [slice(i * HALF, (i + 1) * HALF) for i in range(2)]

        def apart(rows):
            return jnp.concatenate(
                [jnp.where(half_head == h, rows, 0.0) for h in range(HEADS // 2)], axis=0
            )

        keys = [apart(win_keys[:, half]) for half in halves]
        scores = [
            mm_t(win_queries[:, half].astype(BF16), key.astype(BF16))
            for half, key in zip(halves, keys)
        ]
        queries = jnp.concatenate([win_queries[:, half] for half in halves], axis=0)
        query_square = mm((queries * queries).astype(BF16), ones_ref[...])
        key_squares = [mm_t(each, (key * key).astype(BF16))[:1] for key in keys]
        values = [
            jnp.concatenate([apart(win_values[:, half]).astype(BF16), ones_ref[...]], axis=1)
            for half in halves
        ]
        weights = []
        for i in range(2):
            square = query_square[i * TOKENS : (i + 1) * TOKENS]
            scale = lax.rsqrt(factor * factor * square + head_eps) * (factor * SCORE_SCALE)
            scale = scale * lax.rsqrt(key_squares[i] + head_eps)
            weights.append((jnp.exp2(scores[i] * scale) * allowed).astype(BF16))
        both = [mm(weights[i], values[i]) for i in range(2)]
        mixed = [(each_both[:, :HALF] / each_both[:, HALF:]).astype(BF16) for each_both in both]
        wait(turn_index, 1)
        attended = latents + mm(jnp.concatenate(mixed, axis=1), proj_ref[...])
        wait(turn_index, 2)
        centred = centre(attended)
        hidden = mm((centred * entry(GAIN_ROW + 2)).astype(BF16), up_ref[...])
        hidden = gelu(hidden * row_factor(centred)).astype(BF16)
        wait(turn_index, 3)
        backbone = attended + mm(hidden, down_ref[...])
        first, second = backbone[:PATCHES], backbone[PATCHES:]
        blended = jnp.concatenate(
            [mixing(l, 0) * first + mixing(l, 1) * second + embed(l) for l in range(LEV)], axis=0
        )
        centred = centre(blended)
        added = mm((centred * entry(GAIN_ROW + 3)).astype(BF16), dec_ref[...])
        current = (current + added * row_factor(centred)).astype(BF16).astype(F32)

    wide = jnp.concatenate(by_level(current), axis=1)
    out_ref[0] = wide.astype(BF16).reshape(out_ref.shape[1:])


def forecast(windows, arranged, early, late):
    vmem = pl.BlockSpec(memory_space=pltpu.VMEM)
    if windows == 1:
        block, grid = vmem, ()
        result = pltpu.VMEM(arranged.shape, BF16)
        arranged = pltpu.with_memory_space_constraint(arranged, pltpu.VMEM)
    else:
        result = jax.ShapeDtypeStruct(arranged.shape, BF16)
        block = pl.BlockSpec((1,) + arranged.shape[1:], lambda i: (i, 0, 0, 0))
        grid = (windows,)
    early = [pltpu.with_memory_space_constraint(a, pltpu.VMEM) for a in early]
    return pl.pallas_call(
        functools.partial(forecast_kernel, windows),
        grid=grid,
        in_specs=[vmem] * EARLY + [pl.BlockSpec(memory_space=pl.ANY)] * LATE + [block],
        out_specs=block,
        out_shape=result,
        scratch_shapes=[pltpu.VMEM(a.shape, a.dtype) for a in late]
        + [pltpu.SemaphoreType.DMA((LATE,))],
        compiler_params=pltpu.CompilerParams(vmem_limit_bytes=MAIN_LIMIT),
    )(*early, *late, arranged)


def turn_out_kernel(step, x_ref, out_ref, token_ref, near, arrivals):
    count, size = out_ref.shape[:2]
    copies = [
        pltpu.make_async_copy(
            x_ref.at[pl.ds(i * CHUNK, CHUNK)], near.at[pl.ds(i * CHUNK, CHUNK)], arrivals.at[i]
        )
        for i in range(count * size // CHUNK)
    ]
    for copy in copies:
        copy.start()
    token_ref[...] = jnp.zeros_like(token_ref)
    shift = jnp.where(lax.axis_index("lon") < step, 1, 0)
    blocks = CHUNK // size
    for i, copy in enumerate(copies):
        copy.wait()
        piece = near[i * CHUNK : (i + 1) * CHUNK, :].reshape((blocks,) + out_ref.shape[1:])
        for j in range(blocks):
            out_ref[lax.rem(i * blocks + j + count - shift, count)] = piece[j]


def turn_back_kernel(step, x_ref, out_ref):
    count = x_ref.shape[0]
    shift = jnp.where(lax.axis_index("lon") < step, 1, 0)
    blocks = [x_ref[lax.rem(i + count - shift, count)] for i in range(count)]
    out_ref[...] = jnp.stack(blocks).reshape(out_ref.shape)


def turn_out(array, shape, step, near):
    return pl.pallas_call(
        functools.partial(turn_out_kernel, step),
        in_specs=[pl.BlockSpec(memory_space=pl.ANY)],
        out_shape=[
            pltpu.VMEM(shape, BF16) if near else jax.ShapeDtypeStruct(shape, BF16),
            pltpu.VMEM((8, LANES), F32),
        ],
        out_specs=[pl.BlockSpec(memory_space=pltpu.VMEM)] * 2,
        scratch_shapes=[
            pltpu.VMEM(array.shape, BF16),
            pltpu.SemaphoreType.DMA((array.shape[0] // CHUNK,)),
        ],
    )(array)


def turn_back(array, shape, step, near):
    if near:
        array = pltpu.with_memory_space_constraint(array, pltpu.VMEM)
    return pl.pallas_call(
        functools.partial(turn_back_kernel, step),
        out_shape=jax.ShapeDtypeStruct(shape, BF16),
        compiler_params=pltpu.CompilerParams(vmem_limit_bytes=TURN_LIMIT),
    )(array)


def shards(
    fields,
    level_ids,
    embed_weight,
    level_embed,
    enc_gain,
    latent_query,
    kv_weight,
    pool_out,
    attn_gain,
    qkv_weight,
    attn_proj,
    mlp_gain,
    mlp_up,
    mlp_down,
    level_mix,
    dec_gain,
    dec_weight,
):
    devices = lax.axis_size("lon")
    width = fields.shape[2]
    local_count = fields.shape[1]
    piece_cols = local_count // devices
    lat_count = devices // ROW_PARTS
    bands = lat_count // W_LAT
    cut = (W_LON // 2 // piece_cols) * lat_count
    scalars = (level_ids, level_mix.T)
    rows = (
        level_embed,
        latent_query,
        enc_gain.reshape(1, D),
        attn_gain.reshape(1, D),
        mlp_gain.reshape(1, D),
        dec_gain.reshape(1, D),
    )
    outgoing, token = turn_out(
        fields.reshape(local_count, width), (devices, piece_cols, width), cut, bands == 1
    )
    early = load(token, scalars, rows, dec_weight.T, (embed_weight, kv_weight, pool_out))
    late = (qkv_weight, attn_proj, mlp_up, mlp_down)
    got = lax.all_to_all(outgoing, "lon", split_axis=0, concat_axis=0, tiled=True)
    if bands > 1:
        got = got.reshape(ROW_PARTS, lat_count, piece_cols, width)
        got = jnp.roll(got, -(W_LAT // 2), axis=1)
        got = got.reshape(ROW_PARTS, bands, W_LAT, piece_cols, width).transpose(1, 0, 2, 3, 4)
    done = forecast(bands, got.reshape(bands, ROW_PARTS * W_LAT, piece_cols, width), early, late)
    if bands > 1:
        done = done.reshape(bands, ROW_PARTS, W_LAT, piece_cols, width).transpose(1, 0, 2, 3, 4)
        done = done.reshape(ROW_PARTS, lat_count, piece_cols, width)
        done = jnp.roll(done, W_LAT // 2, axis=1)
    done = done.reshape(devices, piece_cols, width)
    home = lax.all_to_all(done, "lon", split_axis=0, concat_axis=0, tiled=True)
    forecast_here = turn_back(home, (local_count, width), cut, bands == 1)
    return forecast_here.reshape(fields.shape)


def solution(mesh):
    placed = (P(("groups", "lon"), None, None), P("groups")) + (P(),) * 15
    return jax.shard_map(
        shards,
        mesh=mesh,
        in_specs=placed,
        out_specs=P(("groups", "lon"), None, None),
        check_vma=False,
    )
```
